32 devices in a mesh: rep: 2 (over y), fsdp: 16 (over z, x, core).
Axes of the slice: x: 2, y: 2, z: 4, core: 2. Of those that a mesh axis runs over, the one named last changes fastest.
Arguments:
- pixels_a: bfloat16 [32, 3, 160, 160], P(('rep', 'fsdp')), may hold values from -6 to 6
- pixels_b: bfloat16 [32, 3, 240, 240], P(('rep', 'fsdp')), may hold values from -6 to 6
- pixels_c: bfloat16 [32, 3, 384, 384], P(('rep', 'fsdp')), may hold values from -6 to 6
- resize_a: float32 [100, 1024], replicated, may hold values from -0.1875 to 0.1875
- resize_b: float32 [144, 1024], replicated, may hold values from -0.1875 to 0.1875
- resize_c: float32 [256, 1024], replicated, may hold values from -0.1875 to 0.1875
- posmap_a: float32 [256, 49], replicated, may hold values from 0 to 0.08
- posmap_b: float32 [400, 49], replicated, may hold values from 0 to 0.08
- posmap_c: float32 [576, 49], replicated, may hold values from 0 to 0.08
- base_kernel: bfloat16 [3, 1024, 768], P(None, None, 'fsdp'), may hold values from -0.21875 to 0.21875
- patch_bias: bfloat16 [768], P('fsdp'), may hold values from -3 to 3
- posemb: bfloat16 [49, 768], P(None, 'fsdp'), may hold values from -12 to 12
- ln1_gain: bfloat16 [768], P('fsdp'), may hold values from 0.099609375 to 1.8984375
- ln1_bias: bfloat16 [768], P('fsdp'), may hold values from -2 to 2
- qkv_weight: bfloat16 [768, 2304], P('fsdp'), may hold values from -0.21875 to 0.21875
- qv_bias: bfloat16 [2, 768], P(None, 'fsdp'), may hold values from -3 to 3
- out_weight: bfloat16 [768, 768], P('fsdp'), may hold values from -0.875 to 0.875
- out_bias: bfloat16 [768], P('fsdp'), may hold values from -2 to 2
- ln2_gain: bfloat16 [768], P('fsdp'), may hold values from 0.099609375 to 1.8984375
- ln2_bias: bfloat16 [768], P('fsdp'), may hold values from -2 to 2
- up_weight: bfloat16 [768, 3072], P('fsdp'), may hold values from -0.21875 to 0.21875
- up_bias: bfloat16 [3072], P('fsdp'), may hold values from -3 to 3
- down_weight: bfloat16 [3072, 768], P('fsdp'), may hold values from -0.109375 to 0.109375
- down_bias: bfloat16 [768], P('fsdp'), may hold values from -2 to 2
- cotangent_a: bfloat16 [32, 256, 768], P(('rep', 'fsdp')), may hold values from -6 to 6
- cotangent_b: bfloat16 [32, 400, 768], P(('rep', 'fsdp')), may hold values from -6 to 6
- cotangent_c: bfloat16 [32, 576, 768], P(('rep', 'fsdp')), may hold values from -6 to 6
Outputs:
- out_a: bfloat16 [32, 256, 768], P(('rep', 'fsdp'))
- out_b: bfloat16 [32, 400, 768], P(('rep', 'fsdp'))
- out_c: bfloat16 [32, 576, 768], P(('rep', 'fsdp'))
- pixel_grad_a: bfloat16 [32, 3, 160, 160], P(('rep', 'fsdp'))
- pixel_grad_b: bfloat16 [32, 3, 240, 240], P(('rep', 'fsdp'))
- pixel_grad_c: bfloat16 [32, 3, 384, 384], P(('rep', 'fsdp'))
- base_kernel_grad: float32 [3, 1024, 768], P(None, None, 'fsdp')
- patch_bias_grad: float32 [768], P('fsdp')
- posemb_grad: float32 [49, 768], P(None, 'fsdp')
- ln1_gain_grad: float32 [768], P('fsdp')
- ln1_bias_grad: float32 [768], P('fsdp')
- qkv_weight_grad: float32 [768, 2304], P('fsdp')
- qv_bias_grad: float32 [2, 768], P(None, 'fsdp')
- out_weight_grad: float32 [768, 768], P('fsdp')
- out_bias_grad: float32 [768], P('fsdp')
- ln2_gain_grad: float32 [768], P('fsdp')
- ln2_bias_grad: float32 [768], P('fsdp')
- up_weight_grad: float32 [768, 3072], P('fsdp')
- up_bias_grad: float32 [3072], P('fsdp')
- down_weight_grad: float32 [3072, 768], P('fsdp')
- down_bias_grad: float32 [768], P('fsdp')
The draws below stay inside these ranges and needn't reach their ends.
All inputs are finite; a program needn't handle non-finite values.
Results may differ from the reference program's by a relative error of at most 0.013.
Values may be sent and summed in bfloat16 or wider, within the bound.
No kernel may reach another device: no remote copies, remote signals or barrier semaphores. Data moves between devices by JAX's collectives and lax.ppermute only.
A program may use at most 256 MiB of HBM per device.

```python
import math
import jax
import jax.numpy as jnp
from jax import lax

D = 768
HEADS = 12
HEAD = 64
FF = 3072
BASE = 32
POS = 7
RA = 160
PA = 10
RB = 240
PB = 12
RC = 384
PC = 16
LA = 256
LB = 400
LC = 576
IMAGES = 32


def block_scale(rng, extent, pieces, low, top_value):
    factor_of, own = 1.0, jax.random.fold_in(rng, 6)
    for dim, shards_of in pieces:
        heights = jnp.exp(jax.random.uniform(jax.random.fold_in(own, dim), (shards_of,), jnp.float32, low / len(pieces), top_value / len(pieces)))
        factor_of = factor_of * jnp.repeat(heights, extent[dim] // shards_of).reshape([-1 if axis == dim else 1 for axis in range(len(extent))])
    return factor_of


def bell_draw(own_key, extent, deviation, reach, split=(), kind=jnp.bfloat16):
    array = jax.random.normal(own_key, extent, jnp.float32) * deviation
    if len(split) > 0:
        array = block_scale(own_key, extent, split, -0.22, 0.18) * array
    return jnp.clip(array, min=-reach, max=reach).astype(kind)


def setup_inputs(seed: int = 0) -> dict:
    key_list = jax.random.split(jax.random.key(seed), 28)
    pixels_a = bell_draw(key_list[0], (IMAGES, 3, RA, RA), 1.0, 6.0, ((0, 32),))
    pixels_b = bell_draw(key_list[1], (IMAGES, 3, RB, RB), 1.0, 6.0, ((0, 32),))
    pixels_c = bell_draw(key_list[2], (IMAGES, 3, RC, RC), 1.0, 6.0, ((0, 32),))
    resize_a = bell_draw(key_list[3], (PA * PA, BASE * BASE), (BASE * BASE) ** -0.5, 0.1875, (), jnp.float32)
    resize_b = bell_draw(key_list[4], (PB * PB, BASE * BASE), (BASE * BASE) ** -0.5, 0.1875, (), jnp.float32)
    resize_c = bell_draw(key_list[5], (PC * PC, BASE * BASE), (BASE * BASE) ** -0.5, 0.1875, (), jnp.float32)
    posmap_a = jnp.clip(jax.random.uniform(key_list[6], (LA, POS * POS), jnp.float32, 0.0, 0.08), 0.0, 0.08)
    posmap_b = jnp.clip(jax.random.uniform(key_list[7], (LB, POS * POS), jnp.float32, 0.0, 0.08), 0.0, 0.08)
    posmap_c = jnp.clip(jax.random.uniform(key_list[8], (LC, POS * POS), jnp.float32, 0.0, 0.08), 0.0, 0.08)
    base_kernel = bell_draw(key_list[9], (3, BASE * BASE, D), 768 ** -0.5, 0.21875, ((2, 16),))
    patch_bias = bell_draw(key_list[10], (D,), 0.5, 3.0, ((0, 16),))
    posemb = bell_draw(key_list[11], (POS * POS, D), 2.0, 12.0, ((1, 16),))
    ln1_gain = jnp.clip(1.0 + 0.18 * jax.random.normal(key_list[12], (D,), jnp.float32), 0.099609375, 1.8984375).astype(jnp.bfloat16)
    ln1_bias = bell_draw(key_list[13], (D,), 0.3, 2.0, ((0, 16),))
    qkv_weight = bell_draw(key_list[14], (D, 3 * D), D ** -0.5, 0.21875, ((0, 16),))
    qv_bias = bell_draw(key_list[15], (2, D), 0.5, 3.0, ((1, 16),))
    out_weight = bell_draw(key_list[16], (D, D), 48 ** -0.5, 0.875, ((0, 16),))
    out_bias = bell_draw(key_list[17], (D,), 0.3, 2.0, ((0, 16),))
    ln2_gain = jnp.clip(1.0 + 0.18 * jax.random.normal(key_list[18], (D,), jnp.float32), 0.099609375, 1.8984375).astype(jnp.bfloat16)
    ln2_bias = bell_draw(key_list[19], (D,), 0.3, 2.0, ((0, 16),))
    up_weight = bell_draw(key_list[20], (D, FF), D ** -0.5, 0.21875, ((0, 16),))
    up_bias = bell_draw(key_list[21], (FF,), 0.5, 3.0, ((0, 16),))
    down_weight = bell_draw(key_list[22], (FF, D), FF ** -0.5, 0.109375, ((0, 16),))
    down_bias = bell_draw(key_list[23], (D,), 0.3, 2.0, ((0, 16),))
    cotangent_a = bell_draw(key_list[24], (IMAGES, LA, D), 1.0, 6.0, ((0, 32),))
    cotangent_b = bell_draw(key_list[25], (IMAGES, LB, D), 1.0, 6.0, ((0, 32),))
    cotangent_c = bell_draw(key_list[26], (IMAGES, LC, D), 1.0, 6.0, ((0, 32),))
    return {"pixels_a": pixels_a, "pixels_b": pixels_b, "pixels_c": pixels_c, "resize_a": resize_a, "resize_b": resize_b, "resize_c": resize_c, "posmap_a": posmap_a, "posmap_b": posmap_b, "posmap_c": posmap_c, "base_kernel": base_kernel, "patch_bias": patch_bias, "posemb": posemb, "ln1_gain": ln1_gain, "ln1_bias": ln1_bias, "qkv_weight": qkv_weight, "qv_bias": qv_bias, "out_weight": out_weight, "out_bias": out_bias, "ln2_gain": ln2_gain, "ln2_bias": ln2_bias, "up_weight": up_weight, "up_bias": up_bias, "down_weight": down_weight, "down_bias": down_bias, "cotangent_a": cotangent_a, "cotangent_b": cotangent_b, "cotangent_c": cotangent_c}


precise = lax.Precision.HIGHEST

@jax.custom_vjp
def low(v):
    return lax.optimization_barrier(v.astype(jnp.bfloat16)).astype(jnp.float32)

@jax.custom_vjp
def low_back(v):
    return v

def low_keep(v):
    return (low(v), None)

def low_pass(kept, grad):
    return (grad,)

def back_keep(v):
    return (v, None)

def back_low(kept, grad):
    return (low(grad),)
low.defvjp(low_keep, low_pass)
low_back.defvjp(back_keep, back_low)

def layer_norm(values, gain, shift):
    mean_row = lax.optimization_barrier(jnp.mean(values, axis=-1, keepdims=True))
    centred = values - mean_row
    spread = lax.optimization_barrier(jnp.mean(centred * centred, axis=-1, keepdims=True))
    return centred * lax.rsqrt(spread + 1e-06) * gain + shift

def patchify(picture, patch_side):
    grid_side = picture.shape[1] // patch_side
    blocks = picture.reshape(3, grid_side, patch_side, grid_side, patch_side)
    blocks = blocks.transpose(1, 3, 0, 2, 4)
    return blocks.reshape(grid_side * grid_side, 3 * patch_side * patch_side)

def block_rest(weights, embedded):
    base_kernel, patch_bias, posemb, ln1_gain, ln1_bias, qkv_weight, qv_bias, out_weight, out_bias, ln2_gain, ln2_bias, up_weight, up_bias, down_weight, down_bias = weights
    token_count, model_width = embedded.shape
    zero_row = jnp.zeros((model_width,), jnp.float32)
    bias_three = jnp.concatenate([qv_bias[0], zero_row, qv_bias[1]])
    normed_in = low(layer_norm(embedded, ln1_gain, ln1_bias))
    qkv = low(low_back(jnp.dot(normed_in, qkv_weight, precision=precise) + bias_three))
    queries = qkv[:, :model_width].reshape(token_count, HEADS, HEAD)
    key_rows = qkv[:, model_width:2 * model_width].reshape(token_count, HEADS, HEAD)
    value_rows = qkv[:, 2 * model_width:].reshape(token_count, HEADS, HEAD)
    scores = low_back(jnp.einsum('qhd,khd->hqk', queries, key_rows, precision=precise) * (1.0 / math.sqrt(HEAD)))
    attention = jax.nn.softmax(scores, axis=-1)
    mixed = jnp.einsum('hqk,khd->qhd', low(attention), value_rows, precision=precise)
    mixed = low(low_back(mixed.reshape(token_count, model_width)))
    branch = low_back(jnp.dot(mixed, out_weight, precision=precise) + out_bias)
    middle = embedded + branch
    normed_mid = low(layer_norm(middle, ln2_gain, ln2_bias))
    up_pre = low_back(jnp.dot(normed_mid, up_weight, precision=precise) + up_bias)
    act = low(jax.nn.gelu(up_pre))
    down_pre = low_back(jnp.dot(act, down_weight, precision=precise) + down_bias)
    return middle + down_pre

def batch_forward(weights, pixels, resize, posmap, patch_side):
    base_kernel, patch_bias, posemb = (weights[0], weights[1], weights[2])
    model_width = base_kernel.shape[2]
    kernel = jnp.einsum('pb,cbd->cpd', resize, base_kernel, precision=precise)
    kernel = low(kernel.reshape(-1, model_width))
    positions = jnp.dot(posmap, posemb, precision=precise)

    def image_step(picture):
        patches = patchify(picture, patch_side)
        embedded = low_back(jnp.dot(patches, kernel, precision=precise)) + patch_bias + positions
        return block_rest(weights, embedded)
    return lax.map(jax.checkpoint(image_step), pixels)

def reference(pixels_a, pixels_b, pixels_c, resize_a, resize_b, resize_c, posmap_a, posmap_b, posmap_c, base_kernel, patch_bias, posemb, ln1_gain, ln1_bias, qkv_weight, qv_bias, out_weight, out_bias, ln2_gain, ln2_bias, up_weight, up_bias, down_weight, down_bias, cotangent_a, cotangent_b, cotangent_c):
    weights = tuple((item.astype(jnp.float32) for item in (base_kernel, patch_bias, posemb, ln1_gain, ln1_bias, qkv_weight, qv_bias, out_weight, out_bias, ln2_gain, ln2_bias, up_weight, up_bias, down_weight, down_bias)))
    pictures = (pixels_a.astype(jnp.float32), pixels_b.astype(jnp.float32), pixels_c.astype(jnp.float32))

    def whole_layer(weight_set, picture_set):
        return (batch_forward(weight_set, picture_set[0], resize_a, posmap_a, PA), batch_forward(weight_set, picture_set[1], resize_b, posmap_b, PB), batch_forward(weight_set, picture_set[2], resize_c, posmap_c, PC))
    results, pullback = jax.vjp(whole_layer, weights, pictures)
    weight_grads, picture_grads = pullback((cotangent_a.astype(jnp.float32), cotangent_b.astype(jnp.float32), cotangent_c.astype(jnp.float32)))
    return (results[0].astype(jnp.bfloat16), results[1].astype(jnp.bfloat16), results[2].astype(jnp.bfloat16), picture_grads[0].astype(jnp.bfloat16), picture_grads[1].astype(jnp.bfloat16), picture_grads[2].astype(jnp.bfloat16), weight_grads[0], weight_grads[1], weight_grads[2], weight_grads[3], weight_grads[4], weight_grads[5], weight_grads[6], weight_grads[7], weight_grads[8], weight_grads[9], weight_grads[10], weight_grads[11], weight_grads[12], weight_grads[13], weight_grads[14])
```

```python
import functools
import math

import jax
import jax.numpy as jnp
from jax import lax
from jax.experimental import pallas as pl
from jax.experimental.pallas import tpu as pltpu
from jax.sharding import PartitionSpec as P

HEADS = 12
HEAD = 64
SIDES = (10, 12, 16)
SLOT = 16
F32 = jnp.float32
BF16 = jnp.bfloat16


def swap(value, axis, size, bit):
    return lax.ppermute(value, axis, [(i, i ^ bit) for i in range(size)])


def place_kernel(count, pieces, halves, me_ref, *refs):
    parts, whole, sems = refs[:pieces], refs[pieces], refs[pieces + 1]
    me, other = me_ref[0], me_ref[1]
    copies = []
    for h in range(halves):
        for d in range(count):
            part = parts[(d % 2) * halves + h]
            row = lax.bitwise_xor(me, d)
            if halves == 1:
                target = whole.at[row]
            else:
                width = whole.shape[2] // 2
                start = pl.multiple_of(lax.bitwise_xor(other, h) * width, 128)
                target = whole.at[row, :, pl.ds(start, width)]
            copies.append(pltpu.make_async_copy(part.at[d // 2], target, sems.at[h, d]))
    for copy in copies:
        copy.start()
    for copy in copies:
        copy.wait()


def take_kernel(count, me_ref, whole, keep, give, sems):
    me = me_ref[0]
    copies = []
    for d in range(count):
        target = (keep, give)[d % 2].at[d // 2]
        copies.append(
            pltpu.make_async_copy(whole.at[lax.bitwise_xor(me, d)], target, sems.at[d])
        )
    for copy in copies:
        copy.start()
    for copy in copies:
        copy.wait()


def take(whole, where, count):
    _, rows, columns = whole.shape
    shape = jax.ShapeDtypeStruct((count // 2, rows, columns), whole.dtype)
    return pl.pallas_call(
        functools.partial(take_kernel, count),
        out_shape=(shape, shape),
        in_specs=[pl.BlockSpec(memory_space=pltpu.SMEM), pl.BlockSpec(memory_space=pltpu.VMEM)],
        out_specs=[pl.BlockSpec(memory_space=pl.ANY)] * 2,
        scratch_shapes=[pltpu.SemaphoreType.DMA((count,))],
        compiler_params=pltpu.CompilerParams(vmem_limit_bytes=16 * 2**20),
        cost_estimate=pl.CostEstimate(
            flops=0, bytes_accessed=4 * count * rows * columns, transcendentals=0
        ),
    )(where, whole)


def gather(shard, where, count, split):
    rows, columns = shard.shape
    halves = 2 if split else 1
    if split:
        width = columns // 2
        shard = lax.dynamic_slice_in_dim(shard, where[1] * width, width, 1)
    held = shard[None]
    bit = 2
    steps = []
    while bit < count:
        steps.append(bit)
        bit *= 2
    order = [0]
    for bit in reversed(steps):
        held = jnp.concatenate([held, swap(held, "fsdp", count, bit)])
        order = order + [k ^ (bit // 2) for k in order]
    assert len(order) == count // 2
    near = [held]
    if split:
        near.append(swap(held, "rep", 2, 1))
    far = [swap(part, "fsdp", count, 1) for part in near]
    whole = place(near + far, halves, where, count, order)
    return whole.reshape(count * rows, columns)


def place(parts, halves, where, count, order):
    back = [order.index(k) for k in range(count // 2)]
    _, rows, columns = parts[0].shape

    def kernel(me_ref, *refs):
        named = [Ordered(ref, back) for ref in refs[: len(parts)]]
        place_kernel(count, len(parts), halves, me_ref, *named, *refs[len(parts) :])

    return pl.pallas_call(
        kernel,
        out_shape=jax.ShapeDtypeStruct((count, rows, columns * halves), parts[0].dtype),
        in_specs=[pl.BlockSpec(memory_space=pltpu.SMEM)]
        + [pl.BlockSpec(memory_space=pl.ANY)] * len(parts),
        out_specs=pl.BlockSpec(memory_space=pltpu.VMEM),
        scratch_shapes=[pltpu.SemaphoreType.DMA((halves, count))],
        compiler_params=pltpu.CompilerParams(vmem_limit_bytes=16 * 2**20),
        cost_estimate=pl.CostEstimate(
            flops=0, bytes_accessed=4 * count * rows * columns * halves, transcendentals=0
        ),
    )(where, *parts)


class Ordered:
    def __init__(self, ref, order):
        self.ref, self.order = ref, order
        self.at = self

    def __getitem__(self, k):
        return self.ref.at[self.order[k]]


def add(first, second):
    return (first.astype(F32) + second.astype(F32)).astype(BF16)


def scatter(whole, where, count, split):
    rows, columns = whole.shape[0] // count, whole.shape[1]
    keep, give = take(whole.reshape(count, rows, columns), where, count)
    got = swap(give, "fsdp", count, 1)
    half = columns // 2
    if split:
        mine, theirs = where[1] * half, (1 - where[1]) * half
        cut = lambda part, start: lax.dynamic_slice_in_dim(part, start, half, 2)
        arrived = swap(add(cut(keep, theirs), cut(got, theirs)), "rep", 2, 1)
        held = add3(cut(keep, mine), cut(got, mine), arrived)
    else:
        held = None
    size, bit = count // 4, 2
    while size:
        if held is None:
            pairs_k = keep.reshape(size, 2, rows, columns)
            pairs_g = got.reshape(size, 2, rows, columns)
            there = add(pairs_k[:, 1], pairs_g[:, 1])
            here = add(pairs_k[:, 0], pairs_g[:, 0])
        else:
            pairs = held.reshape(size, 2, rows, held.shape[2])
            there, here = pairs[:, 1], pairs[:, 0]
        held = add(here, swap(there, "fsdp", count, bit))
        size, bit = size // 2, bit * 2
    held = held[0]
    if split:
        other = swap(held, "rep", 2, 1)
        low = where[1] == 0
        return jnp.concatenate(
            [jnp.where(low, held, other), jnp.where(low, other, held)], axis=1
        ).astype(F32)
    return add(held, swap(held, "rep", 2, 1)).astype(F32)


def add3(first, second, third):
    return (first.astype(F32) + second.astype(F32) + third.astype(F32)).astype(BF16)


def up_to(value, unit):
    return -(-value // unit) * unit

def swap_chunks(lines):
    chunk = lax.broadcasted_iota(jnp.int32, lines[0].shape, 1) // SLOT
    for step in (1, 2, 4):
        stays = (chunk & step) == 0
        for i in range(8):
            if i & step == 0:
                low, high = lines[i], lines[i + step]
                lines[i] = jnp.where(stays, low, pltpu.roll(high, step * SLOT, 1))
                lines[i + step] = jnp.where(stays, pltpu.roll(low, 128 - step * SLOT, 1), high)
    return lines

def spread(side, grid, columns):
    pixel = lax.broadcasted_iota(jnp.int32, (grid * side, columns), 0)
    column = lax.broadcasted_iota(jnp.int32, (grid * side, columns), 1)
    place = column % SLOT
    return ((pixel == column // SLOT * side + place) & (place < side)).astype(BF16)

def patch_kernel(*refs):
    pixels, outs, rows_ref, flat_ref = refs[:3], refs[3:6], refs[6], refs[7]
    for side, pixel_ref, out in zip(SIDES, pixels, outs):
        high = pixel_ref.shape[2]
        grid = high // side
        columns = up_to(grid * SLOT, 128)
        table = None if side == SLOT else spread(side, grid, columns)
        for c in range(3):
            picture = pixel_ref[0, c]
            if table is None:
                wide = picture.astype(F32)
            else:
                wide = jnp.dot(picture, table, preferred_element_type=F32)
            for block in range(columns // 128):
                rows_ref[3 * c + block, :high, :] = wide[:, 128 * block:128 * block + 128]
        slots = 3 * side
        for group in range(out.shape[1] // 128):
            for block in range(columns // 128):
                lines = []
                for q in range(8 * group, 8 * group + 8):
                    if q < slots:
                        lines.append(rows_ref[q // side * 3 + block, pl.ds(q % side, grid, stride=side), :])
                    else:
                        lines.append(jnp.zeros((grid, 128), F32))
                lines = swap_chunks(lines)
                for g in range(8):
                    if 8 * block + g < grid:
                        flat_ref[group, pl.ds(8 * block + g, grid, stride=grid), :] = lines[g]
        for group in range(out.shape[1] // 128):
            out[:, 128 * group:128 * group + 128] = flat_ref[group, :grid * grid, :].astype(BF16)

def patch_all(pixels):
    shapes = []
    for picture, side in zip(pixels, SIDES):
        grid = picture.shape[2] // side
        shapes.append(jax.ShapeDtypeStruct((grid * grid, up_to(3 * side * SLOT, 128)), BF16))
    high = max(p.shape[2] for p in pixels)
    return pl.pallas_call(
        patch_kernel,
        out_shape=shapes,
        in_specs=[pl.BlockSpec(memory_space=pltpu.VMEM)] * 3,
        out_specs=[pl.BlockSpec(memory_space=pltpu.VMEM)] * 3,
        scratch_shapes=[pltpu.VMEM((9, high, 128), F32), pltpu.VMEM((max(s.shape[1] for s in shapes) // 128, max(s.shape[0] for s in shapes), 128), F32)],
        compiler_params=pltpu.CompilerParams(vmem_limit_bytes=24 * 2**20),
        cost_estimate=pl.CostEstimate(flops=5 * 10**9, bytes_accessed=4 * 10**6, transcendentals=0),
    )(*pixels)

def unpatch_kernel(starts, bounds, grad_ref, kernel_ref, *refs):
    outs, flat_ref, rows_ref = refs[:3], refs[3], refs[4]
    for i, side in enumerate(SIDES):
        out = outs[i]
        high = out.shape[2]
        grid = high // side
        columns = up_to(grid * SLOT, 128)
        width = bounds[i + 1] - bounds[i]
        grads = grad_ref[starts[i]:starts[i + 1], :]
        flat = jnp.dot(grads, kernel_ref[:, bounds[i]:bounds[i + 1]], preferred_element_type=F32)
        for group in range(width // 128):
            flat_ref[group, :grid * grid, :] = flat[:, 128 * group:128 * group + 128]
        slots = 3 * side
        for group in range(width // 128):
            for block in range(columns // 128):
                lines = []
                for g in range(8):
                    if 8 * block + g < grid:
                        lines.append(flat_ref[group, pl.ds(8 * block + g, grid, stride=grid), :])
                    else:
                        lines.append(jnp.zeros((grid, 128), F32))
                lines = swap_chunks(lines)
                for q in range(8 * group, min(8 * group + 8, slots)):
                    rows_ref[q // side * 3 + block, pl.ds(q % side, grid, stride=side), :] = lines[q % 8]
        table = None if side == SLOT else spread(side, grid, columns)
        for c in range(3):
            picture = jnp.concatenate([rows_ref[3 * c + block, :high, :] for block in range(columns // 128)], axis=1).astype(BF16)
            if table is not None:
                picture = lax.dot_general(picture, table, (((1,), (1,)), ((), ())), preferred_element_type=F32).astype(BF16)
            out[0, c] = picture

def unpatch_all(grads, kernels, starts, bounds, sides):
    high = max(sides)
    whole = pl.BlockSpec(memory_space=pltpu.VMEM)
    return pl.pallas_call(
        functools.partial(unpatch_kernel, starts, bounds),
        out_shape=[jax.ShapeDtypeStruct((1, 3, s, s), BF16) for s in sides],
        in_specs=[whole] * 2,
        out_specs=[whole] * 3,
        scratch_shapes=[pltpu.VMEM((max(e - s for s, e in zip(bounds, bounds[1:])) // 128, max(e - s for s, e in zip(starts, starts[1:])), 128), F32),
            pltpu.VMEM((9, high, 128), F32)],
        compiler_params=pltpu.CompilerParams(vmem_limit_bytes=32 * 2**20),
        cost_estimate=pl.CostEstimate(flops=5 * 10**9, bytes_accessed=10 * 10**6, transcendentals=0),
    )(grads, kernels)


def three_terms(value):
    first = lax.reduce_precision(value, 8, 7)
    rest = value - first
    second = lax.reduce_precision(rest, 8, 7)
    return first.astype(BF16), second.astype(BF16), (rest - second).astype(BF16)


def exact_dot(value, low, dims):
    return sum(
        lax.dot_general(term, low, dims, preferred_element_type=F32)
        for term in reversed(three_terms(value))
    )


def unit(values):
    mean_row = jnp.mean(values, axis=-1, keepdims=True)
    centred = values - mean_row
    inverse = lax.rsqrt(jnp.mean(centred * centred, axis=-1, keepdims=True) + 1e-06)
    return centred * inverse, inverse


def norm_backward(grad_out, unit_rows, inverse, gain):
    grad_unit = grad_out * gain
    inner = jnp.mean(grad_unit * unit_rows, axis=-1, keepdims=True)
    grad_in = inverse * (
        grad_unit - jnp.mean(grad_unit, axis=-1, keepdims=True) - unit_rows * inner
    )
    return grad_in, jnp.sum(grad_out * unit_rows, axis=0), jnp.sum(grad_out, axis=0)


def chunks(total, most):
    pieces = -(-total // most)
    size = -(-total // pieces)
    size = -(-size // 16) * 16
    return [(s, min(size, total - s)) for s in range(0, total, size)]

def outer_t(first, second):
    return lax.dot_general(first, second, (((1,), (1,)), ((), ())), preferred_element_type=F32)

def attend_kernel(starts, chunk, q_ref, k_ref, v_ref, mixed_ref, total_ref):
    pair = pl.program_id(0)
    @pl.when(pair == 0)
    def _():
        total_ref[...] = jnp.zeros_like(total_ref)
    for begin, end in zip(starts, starts[1:]):
        keys, values = k_ref[begin:end, :], v_ref[begin:end, :]
        for offset, size in chunks(end - begin, chunk):
            rows = slice(begin + offset, begin + offset + size)
            queries = q_ref[rows, :] * (HEAD ** -0.5)
            lane = lax.broadcasted_iota(jnp.int32, (size, 128), 1)
            mixed, totals = [], []
            for head in range(2):
                own = (lane < HEAD) if head == 0 else (lane >= HEAD)
                scores = outer_t(jnp.where(own, queries, jnp.zeros_like(queries)), keys)
                top = jnp.max(scores, axis=1, keepdims=True)
                expo = jnp.exp(scores - top)
                total = jnp.sum(expo, axis=1, keepdims=True)
                out = jnp.dot(expo.astype(BF16), values, preferred_element_type=F32)
                mixed.append(out / total)
                totals.append(top + jnp.log(total))
            mixed_ref[rows, :] = jnp.where(lane < HEAD, mixed[0], mixed[1]).astype(BF16)
            held = total_ref[rows, :]
            held = jnp.where(lane == 2 * pair, totals[0], held)
            total_ref[rows, :] = jnp.where(lane == 2 * pair + 1, totals[1], held)

def attend_forward(qkv, starts, chunk=576):
    rows, width = qkv.shape[0], qkv.shape[1] // 3
    pairs = width // 128
    block = lambda first: pl.BlockSpec((rows, 128), lambda j: (0, first * pairs + j))
    return pl.pallas_call(
        functools.partial(attend_kernel, starts, chunk),
        grid=(pairs,),
        out_shape=(jax.ShapeDtypeStruct((rows, width), BF16), jax.ShapeDtypeStruct((rows, 128), F32)),
        in_specs=[block(0), block(1), block(2)],
        out_specs=[pl.BlockSpec((rows, 128), lambda j: (0, j)), pl.BlockSpec((rows, 128), lambda j: (0, 0))],
        compiler_params=pltpu.CompilerParams(vmem_limit_bytes=32 * 2**20),
        cost_estimate=pl.CostEstimate(flops=20 * 10**9, bytes_accessed=8 * rows * width, transcendentals=0),
    )(qkv, qkv, qkv)

def terms(value):
    first = value.astype(BF16)
    rest = value - first.astype(F32)
    second = rest.astype(BF16)
    return first, second, (rest - second.astype(F32)).astype(BF16)

def attend_back_kernel(starts, chunk, q_ref, k_ref, v_ref, mixed_ref, grad_ref, total_ref, out_ref, left, right, acc):
    pair = pl.program_id(0)
    scale = HEAD ** -0.5
    zero = jnp.zeros((), BF16)
    for begin, end in zip(starts, starts[1:]):
        size = end - begin
        for offset, part in chunks(size, chunk):
            rows = slice(begin + offset, begin + offset + part)
            lane = lax.broadcasted_iota(jnp.int32, (part, 128), 1)
            queries, grads = q_ref[rows, :] * scale, grad_ref[rows, :]
            product = grads.astype(F32) * mixed_ref[rows, :].astype(F32)
            total_all = total_ref[rows, :]
            for head in range(2):
                own = (lane < HEAD) if head == 0 else (lane >= HEAD)
                free = HEAD * (1 - head)
                inner = jnp.sum(jnp.where(own, product, 0.0), axis=1, keepdims=True)
                total = jnp.sum(jnp.where(lane == 2 * pair + head, total_all, 0.0), axis=1, keepdims=True)
                for target, value, line in ((left, queries, total), (right, grads, inner)):
                    wide = jnp.where(own, value, zero)
                    for i, term in enumerate(terms(line)):
                        wide = jnp.where(lane == free + i, term, wide)
                    target[head, offset:offset + part, :] = wide
        queries, grads = q_ref[begin:end, :], grad_ref[begin:end, :]
        acc[...] = jnp.zeros_like(acc)
        for offset, part in chunks(size, chunk):
            rows = slice(begin + offset, begin + offset + part)
            lane = lax.broadcasted_iota(jnp.int32, (part, 128), 1)
            keys, values = k_ref[rows, :], v_ref[rows, :]
            grad_key, grad_value = [], []
            for head in range(2):
                own = (lane < HEAD) if head == 0 else (lane >= HEAD)
                free = HEAD * (1 - head)
                minus = jnp.where((lane >= free) & (lane < free + 3), -jnp.ones((), BF16), zero)
                scores = outer_t(jnp.where(own, keys, minus), left[head, :size, :])
                probs = jnp.exp(scores)
                grad_scores = outer_t(jnp.where(own, values, minus), right[head, :size, :])
                grad_scores = (probs * grad_scores).astype(BF16)
                grad_value.append(jnp.dot(probs.astype(BF16), grads, preferred_element_type=F32))
                grad_key.append(jnp.dot(grad_scores, queries, preferred_element_type=F32))
                acc[head, :size, :] += lax.dot_general(grad_scores, keys, (((0,), (0,)), ((), ())), preferred_element_type=F32)
            out_ref[1, rows, :] = (jnp.where(lane < HEAD, *grad_key) * scale).astype(BF16)
            out_ref[2, rows, :] = jnp.where(lane < HEAD, *grad_value).astype(BF16)
        lane = lax.broadcasted_iota(jnp.int32, (size, 128), 1)
        out_ref[0, begin:end, :] = (jnp.where(lane < HEAD, acc[0, :size, :], acc[1, :size, :]) * scale).astype(BF16)

def attend_backward(qkv, mixed, totals, grad_mixed, starts, chunk=400):
    rows, width = mixed.shape
    pairs = width // 128
    longest = max(e - s for s, e in zip(starts, starts[1:]))
    block = lambda first: pl.BlockSpec((rows, 128), lambda j: (0, first * pairs + j))
    return pl.pallas_call(
        functools.partial(attend_back_kernel, starts, chunk),
        grid=(pairs,),
        out_shape=jax.ShapeDtypeStruct((3, rows, width), BF16),
        in_specs=[block(0), block(1), block(2), block(0), block(0), pl.BlockSpec((rows, 128), lambda j: (0, 0))],
        out_specs=pl.BlockSpec((3, rows, 128), lambda j: (0, 0, j)),
        scratch_shapes=[pltpu.VMEM((2, longest, 128), BF16), pltpu.VMEM((2, longest, 128), BF16), pltpu.VMEM((2, longest, 128), F32)],
        compiler_params=pltpu.CompilerParams(vmem_limit_bytes=32 * 2**20),
        cost_estimate=pl.CostEstimate(flops=40 * 10**9, bytes_accessed=16 * rows * width, transcendentals=0),
    )(qkv, qkv, qkv, mixed, grad_mixed, totals)


def dot(first, second):
    return jnp.dot(first, second, preferred_element_type=F32)


def dot_t(first, second):
    return lax.dot_general(first, second, (((1,), (1,)), ((), ())), preferred_element_type=F32)


def t_dot(first, second):
    return lax.dot_general(first, second, (((0,), (0,)), ((), ())), preferred_element_type=F32)


def body(count, pixels, resizes, posmaps, weights, cotangents):
    base_kernel, patch_bias, posemb = weights[:3]
    ln1_gain, ln1_bias, qkv_weight, qv_bias, out_weight, out_bias = weights[3:9]
    ln2_gain, ln2_bias, up_weight, up_bias, down_weight, down_bias = weights[9:]
    channels, base_pixels, share = base_kernel.shape
    width = share * count
    spots = posemb.shape[0]
    where = jnp.stack([lax.axis_index("fsdp"), lax.axis_index("rep")]).astype(jnp.int32)
    tokens = [c.shape[1] for c in cotangents]
    starts = [sum(tokens[:i]) for i in range(4)]
    part = lambda rows, i: rows[starts[i] : starts[i + 1]]

    padded = []
    for resize, side in zip(resizes, SIDES):
        wide = jnp.pad(
            resize.reshape(side, side, base_pixels), ((0, 0), (0, SLOT - side), (0, 0))
        )
        padded.append(wide.reshape(side * SLOT, base_pixels))
    resize_all = jnp.concatenate(padded)
    pixel_rows = resize_all.shape[0]
    bounds = [0]
    for side in SIDES:
        bounds.append(bounds[-1] + side * SLOT)
    base_rows = base_kernel.transpose(1, 0, 2).reshape(base_pixels, channels * share)
    resized = exact_dot(resize_all, base_rows, (((1,), (0,)), ((), ()))).astype(BF16)
    resized = resized.reshape(pixel_rows, channels, share).transpose(2, 1, 0)
    kernel_shard, kernel_bounds = [], [0]
    for i, side in enumerate(SIDES):
        columns = up_to(3 * side * SLOT, 128)
        own = resized[:, :, bounds[i] : bounds[i + 1]].reshape(share, -1)
        kernel_shard.append(jnp.pad(own, ((0, 0), (0, columns - own.shape[1]))))
        kernel_bounds.append(kernel_bounds[-1] + columns)
    kernel_shard = jnp.concatenate(kernel_shard, axis=1)
    up_per = up_bias.shape[0] // share
    smalls = [posemb.T] + [
        v.reshape(share, 1)
        for v in (
            patch_bias,
            ln1_gain,
            ln1_bias,
            qv_bias[0],
            qv_bias[1],
            out_bias,
            ln2_gain,
            ln2_bias,
            down_bias,
        )
    ]
    smalls.append(up_bias.reshape(share, up_per))
    used = spots + 9 + up_per
    kernel_columns = kernel_shard.shape[1]
    tail = (-(kernel_columns + used)) % 256
    smalls.append(jnp.zeros((share, tail), BF16))
    embed_shard = jnp.concatenate([kernel_shard] + smalls, axis=1)

    embed_whole = gather(embed_shard, where, count, True)
    w_qkv = gather(qkv_weight, where, count, True)
    w_out = gather(out_weight, where, count, True)
    w_up = gather(up_weight, where, count, True)
    w_down = gather(down_weight, where, count, False)

    kernels = [embed_whole[:, kernel_bounds[i] : kernel_bounds[i + 1]] for i in range(3)]
    table = embed_whole[:, kernel_columns : kernel_columns + used].astype(F32)
    pos_table = table[:, :spots]
    lines = table[:, spots : spots + 9].T
    b_up = table[:, spots + 9 :].reshape(-1)

    patches = patch_all(pixels)
    positions = exact_dot(
        jnp.concatenate(posmaps), pos_table.astype(BF16), (((1,), (1,)), ((), ()))
    )
    embedded = (
        jnp.concatenate([dot_t(p, k) for p, k in zip(patches, kernels)]) + lines[0] + positions
    )
    unit_in, inverse_in = unit(embedded)
    normed_in = (unit_in * lines[1] + lines[2]).astype(BF16)
    bias_three = jnp.concatenate([lines[3], jnp.zeros_like(lines[3]), lines[4]])
    qkv = (dot(normed_in, w_qkv) + bias_three).astype(BF16)
    mixed, totals = attend_forward(qkv, starts)
    middle = embedded + dot(mixed, w_out) + lines[5]
    unit_mid, inverse_mid = unit(middle)
    normed_mid = (unit_mid * lines[6] + lines[7]).astype(BF16)
    up_pre = dot(normed_mid, w_up) + b_up
    act, gelu_back = jax.vjp(jax.nn.gelu, up_pre)
    act = act.astype(BF16)
    final = (middle + dot(act, w_down) + lines[8]).astype(BF16)

    grad_down = jnp.concatenate([c[0] for c in cotangents])
    grad_final = grad_down.astype(F32)
    grad_w_down = t_dot(act, grad_down).astype(BF16)
    sum_down = scatter(grad_w_down, where, count, False)
    grad_up = gelu_back(dot_t(grad_down, w_down))[0].astype(BF16)
    grad_w_up = t_dot(normed_mid, grad_up).astype(BF16)
    sum_up = scatter(grad_w_up, where, count, True)
    grad_normed_mid = dot_t(grad_up, w_up)
    grad_mid, grad_gain2, grad_bias2 = norm_backward(
        grad_normed_mid, unit_mid, inverse_mid, lines[6]
    )
    grad_middle = grad_final + grad_mid
    grad_branch = grad_middle.astype(BF16)
    grad_w_out = t_dot(mixed, grad_branch).astype(BF16)
    grad_mixed = dot_t(grad_branch, w_out).astype(BF16)
    grad_qkv = attend_backward(qkv, mixed, totals, grad_mixed, starts)
    grad_w_qkv = [t_dot(normed_in, grad_qkv[i]).astype(BF16) for i in range(3)]
    sum_attn = scatter(
        jnp.concatenate(grad_w_qkv + [grad_w_out], axis=1), where, count, True
    )
    grad_normed_in = sum(
        dot_t(grad_qkv[i], w_qkv[:, i * width : (i + 1) * width]) for i in range(3)
    )
    grad_in, grad_gain1, grad_bias1 = norm_backward(
        grad_normed_in, unit_in, inverse_in, lines[1]
    )
    grad_embedded = grad_middle + grad_in
    grad_low = grad_embedded.astype(BF16)
    grad_kernel = [t_dot(part(grad_low, i), patches[i]) for i in range(3)]
    grad_table = lax.dot_general(
        grad_embedded,
        jnp.concatenate(posmaps),
        (((0,), (0,)), ((), ())),
        precision=lax.Precision.HIGHEST,
    )
    column_sums = [jnp.sum(grad_qkv[i].astype(F32), axis=0) for i in (0, 2)]
    grad_lines = jnp.stack(
        [
            jnp.sum(grad_embedded, axis=0),
            grad_gain1,
            grad_bias1,
            column_sums[0],
            column_sums[1],
            jnp.sum(grad_branch.astype(F32), axis=0),
            grad_gain2,
            grad_bias2,
            jnp.sum(grad_final, axis=0),
        ]
    )
    grad_b_up = jnp.sum(grad_up.astype(F32), axis=0).reshape(width, up_per)
    grad_embed = jnp.concatenate(
        grad_kernel + [grad_table, grad_lines.T, grad_b_up, jnp.zeros((width, tail), F32)], axis=1
    ).astype(BF16)
    sum_embed = scatter(grad_embed, where, count, True)
    pixel_grads = unpatch_all(
        grad_low, embed_whole, starts, kernel_bounds, [p.shape[2] for p in pixels]
    )

    kernel_sum = jnp.concatenate(
        [
            sum_embed[:, start : start + channels * side * SLOT].reshape(share, channels, -1)
            for start, side in zip(kernel_bounds, SIDES)
        ],
        axis=2,
    )
    base_grad = exact_dot(
        resize_all, kernel_sum.astype(BF16).transpose(2, 1, 0).reshape(pixel_rows, -1),
        (((0,), (0,)), ((), ())),
    )
    base_grad = base_grad.reshape(base_pixels, channels, share).transpose(1, 0, 2)
    small_sum = sum_embed[:, kernel_columns : kernel_columns + used]
    columns = small_sum[:, spots : spots + 9].T
    results = [part(final, i)[None] for i in range(3)]
    return (
        *results,
        *pixel_grads,
        base_grad,
        columns[0],
        small_sum[:, :spots].T,
        columns[1],
        columns[2],
        sum_attn[:, : 3 * width],
        columns[3:5],
        sum_attn[:, 3 * width :],
        columns[5],
        columns[6],
        columns[7],
        sum_up,
        small_sum[:, spots + 9 :].reshape(-1),
        sum_down,
        columns[8],
    )


def solution(mesh):
    count = mesh.shape["fsdp"]

    def run(*args):
        return body(count, args[:3], args[3:6], args[6:9], args[9:24], args[24:])

    images = ("rep", "fsdp")
    weight_specs = (
        P(None, None, "fsdp"),
        P("fsdp"),
        P(None, "fsdp"),
        P("fsdp"),
        P("fsdp"),
        P("fsdp", None),
        P(None, "fsdp"),
        P("fsdp", None),
        P("fsdp"),
        P("fsdp"),
        P("fsdp"),
        P("fsdp", None),
        P("fsdp"),
        P("fsdp", None),
        P("fsdp"),
    )
    return jax.shard_map(
        run,
        mesh=mesh,
        in_specs=(P(images, None, None, None),) * 3
        + (P(),) * 6
        + weight_specs
        + (P(images, None, None),) * 3,
        out_specs=(P(images, None, None),) * 3
        + (P(images, None, None, None),) * 3
        + weight_specs,
        check_vma=False,
    )
```

```python
import functools
import math

import jax
import jax.numpy as jnp
from jax import lax
from jax.experimental import pallas as pl
from jax.experimental.pallas import tpu as pltpu
from jax.sharding import PartitionSpec as P

HEADS = 12
HEAD = 64
SIDES = (10, 12, 16)
SLOT = 16
F32 = jnp.float32
BF16 = jnp.bfloat16


def swap(value, axis, size, bit):
    return lax.ppermute(value, axis, [(i, i ^ bit) for i in range(size)])


def after(first, *rest):
    return lax.optimization_barrier((first, *rest))


class Gather:
    def __init__(self, shard, where, count, steps, split=False):
        self.count, self.split, self.columns = count, split, shard.shape[1]
        if split:
            width = shard.shape[1] // 2
            shard = lax.dynamic_slice_in_dim(shard, where[1] * width, width, 1)
        self.held = [(shard[None], [0])]
        self.steps = list(steps) + (["rep"] if split else []) + ["core"]
        self.step = None
        self.pieces = []

    def send(self):
        self.step, self.steps = self.steps[0], self.steps[1:]
        if len(self.held) > 1 and len(self.held[0]) == 2:
            offsets = [o for _, offsets in self.held for o in offsets]
            self.held = [(jnp.concatenate([blocks for blocks, _ in self.held]), offsets)]
        if self.step in ("rep", "core"):
            axis, size = ("rep", 2) if self.step == "rep" else ("fsdp", self.count)
            self.sent = [swap(blocks, axis, size, 1) for blocks, *_ in self.held]
        else:
            self.sent = [swap(self.held[0][0], "fsdp", self.count, offset) for offset in self.step]
        return self

    def take(self, arrived):
        if self.step == "rep":
            self.held = [(*h, 0) for h in self.held] + [
                (blocks, h[1], 1) for blocks, h in zip(arrived, self.held)
            ]
        elif self.step == "core":
            held = [h if len(h) == 3 else (*h, None) for h in self.held]
            self.held = held + [
                (blocks, [o ^ 1 for o in h[1]], h[2]) for blocks, h in zip(arrived, held)
            ]
        else:
            offsets = self.held[0][1]
            self.held = self.held + [
                (blocks, [o ^ offset for o in offsets])
                for blocks, offset in zip(arrived, self.step)
            ]


def finish(anchor, *chains):
    sizes = [len(chain.sent) for chain in chains]
    anchor, *flat = after(anchor, *[part for chain in chains for part in chain.sent])
    for chain, size in zip(chains, sizes):
        chain.take(flat[:size])
        flat = flat[size:]
    return anchor


def complete(anchor, *chains):
    while chains:
        for chain in chains:
            anchor = finish(anchor, chain)
        chains = [chain.send() for chain in chains if chain.steps]
    return anchor


def place_kernel(pieces, me_ref, *refs):
    parts, whole, sems = refs[: len(pieces)], refs[len(pieces)], refs[len(pieces) + 1]
    me, other = me_ref[0], me_ref[1]
    copies = []
    for part, (offsets, half, first, columns) in zip(parts, pieces):
        for k, offset in enumerate(offsets):
            row = lax.bitwise_xor(me, offset)
            if half is None:
                target = whole.at[row, :, pl.ds(first, columns)]
            else:
                width = columns // 2
                start = pl.multiple_of(first + lax.bitwise_xor(other, half) * width, 128)
                target = whole.at[row, :, pl.ds(start, width)]
            copies.append(pltpu.make_async_copy(part.at[k], target, sems.at[len(copies)]))
    for copy in copies:
        copy.start()
    for copy in copies:
        copy.wait()


def place(gathers, where, count):
    pieces, first = [], 0
    for g in gathers:
        pieces += [(blocks, offsets, half, first, g.columns) for blocks, offsets, half in g.held]
        first += g.columns
    rows, kind = pieces[0][0].shape[1], pieces[0][0].dtype
    whole = pl.pallas_call(
        functools.partial(place_kernel, [piece[1:] for piece in pieces]),
        out_shape=jax.ShapeDtypeStruct((count, rows, first), kind),
        in_specs=[pl.BlockSpec(memory_space=pltpu.SMEM)]
        + [pl.BlockSpec(memory_space=pl.ANY)] * len(pieces),
        out_specs=pl.BlockSpec(memory_space=pltpu.VMEM),
        scratch_shapes=[pltpu.SemaphoreType.DMA((sum(len(p[1]) for p in pieces),))],
        compiler_params=pltpu.CompilerParams(vmem_limit_bytes=16 * 2**20),
        cost_estimate=pl.CostEstimate(
            flops=0, bytes_accessed=4 * count * rows * first, transcendentals=0
        ),
    )(where, *[piece[0] for piece in pieces])
    return whole.reshape(count * rows, first)


def take_kernel(count, split, segments, me_ref, *refs):
    inputs = max(which for which, *_ in segments) + 1
    wholes, outs, sems = refs[:inputs], refs[inputs:-1], refs[-1]
    me, other = me_ref[0], me_ref[1]
    half = outs[0].shape[2]

    def copies(switch):
        found = []
        for which, start, columns, first in segments:
            for d in range(count):
                source = wholes[which].at[lax.bitwise_xor(me, d), :, pl.ds(start, columns)]
                side = (first // half) ^ switch
                target = outs[2 * (d % 2) + side] if split else outs[d % 2]
                target = target.at[d // 2, :, pl.ds(first % half, columns)]
                found.append(pltpu.make_async_copy(source, target, sems.at[len(found)]))
        return found

    def run(switch):
        found = copies(switch)
        for copy in found:
            copy.start()
        for copy in found:
            copy.wait()

    if split:
        for switch in range(2):
            pl.when(other == switch)(functools.partial(run, switch))
    else:
        run(0)


def take(wholes, segments, where, count, split):
    rows = wholes[0].shape[0] // count
    blocks = [w.reshape(count, rows, w.shape[1]) for w in wholes]
    columns = sum(segment[2] for segment in segments)
    half = columns // 2 if split else columns
    ends, first = [], 0
    for which, start, size in segments:
        while size:
            room = min(size, half - first % half)
            ends.append((which, start, room, first))
            first, start, size = first + room, start + room, size - room
    shape = jax.ShapeDtypeStruct((count // 2, rows, half), wholes[0].dtype)
    outs = 4 if split else 2
    return pl.pallas_call(
        functools.partial(take_kernel, count, split, ends),
        out_shape=(shape,) * outs,
        in_specs=[pl.BlockSpec(memory_space=pltpu.SMEM)]
        + [pl.BlockSpec(memory_space=pltpu.VMEM)] * len(blocks),
        out_specs=[pl.BlockSpec(memory_space=pl.ANY)] * outs,
        scratch_shapes=[pltpu.SemaphoreType.DMA((count * len(ends),))],
        compiler_params=pltpu.CompilerParams(vmem_limit_bytes=16 * 2**20),
        cost_estimate=pl.CostEstimate(
            flops=0, bytes_accessed=4 * count * rows * columns, transcendentals=0
        ),
    )(where, *blocks)


def add(*values):
    return sum(value.astype(F32) for value in values).astype(BF16)


class Scatter:
    def __init__(self, wholes, segments, where, count, steps, split=False):
        self.where, self.count, self.split = where, count, split
        parts = take(wholes, segments, where, count, split)
        self.keep, self.give = parts[: len(parts) // 2], parts[len(parts) // 2 :]
        self.steps = ["core"] + (["half"] if split else []) + list(steps) + ["rep"]
        self.offsets = list(range(0, count, 2))
        self.step = None

    def send(self):
        self.step, self.steps = self.steps[0], self.steps[1:]
        if self.step == "core":
            self.sent = [swap(part, "fsdp", self.count, 1) for part in self.give]
        elif self.step == "half":
            self.sent = [swap(add(*self.away), "rep", 2, 1)]
        elif self.step == "rep":
            self.held = add(*[part[0] for part in self.parts])
            self.sent = [swap(self.held, "rep", 2, 1)]
        else:
            mask = 0
            for offset in self.step:
                mask |= offset
            stay = [o for o in self.offsets if o & mask == 0]
            pick = lambda offset: [self.offsets.index(o | offset) for o in stay]
            self.sent = [
                swap(add(*self.chosen(pick(offset))), "fsdp", self.count, offset)
                for offset in self.step
            ]
            self.parts = self.chosen(pick(0))
            self.offsets = stay
        return self

    def chosen(self, places):
        stride = places[1] - places[0] if len(places) > 1 else 1
        assert places == list(range(places[0], places[-1] + 1, stride))
        return [part[places[0] : places[-1] + 1 : stride] for part in self.parts]

    def take(self, arrived):
        if self.step == "core":
            self.parts = [self.keep[0], arrived[0]]
            if self.split:
                self.away = [self.keep[1], arrived[1]]
        elif self.step == "rep":
            if self.split:
                low = self.where[1] == 0
                self.result = jnp.concatenate(
                    [jnp.where(low, self.held, arrived[0]), jnp.where(low, arrived[0], self.held)],
                    axis=1,
                )
            else:
                self.result = add(self.held, arrived[0])
        else:
            self.parts = self.parts + list(arrived)


def up_to(value, unit):
    return -(-value // unit) * unit

def swap_chunks(lines):
    chunk = lax.broadcasted_iota(jnp.int32, lines[0].shape, 1) // SLOT
    for step in (1, 2, 4):
        stays = (chunk & step) == 0
        for i in range(8):
            if i & step == 0:
                low, high = lines[i], lines[i + step]
                lines[i] = jnp.where(stays, low, pltpu.roll(high, step * SLOT, 1))
                lines[i + step] = jnp.where(stays, pltpu.roll(low, 128 - step * SLOT, 1), high)
    return lines

def spread(side, grid, columns):
    pixel = lax.broadcasted_iota(jnp.int32, (grid * side, columns), 0)
    column = lax.broadcasted_iota(jnp.int32, (grid * side, columns), 1)
    place = column % SLOT
    return ((pixel == column // SLOT * side + place) & (place < side)).astype(BF16)

def patch_kernel(*refs):
    pixels, outs, rows_ref, flat_ref = refs[:3], refs[3:6], refs[6], refs[7]
    for side, pixel_ref, out in zip(SIDES, pixels, outs):
        high = pixel_ref.shape[2]
        grid = high // side
        columns = up_to(grid * SLOT, 128)
        table = None if side == SLOT else spread(side, grid, columns)
        for c in range(3):
            picture = pixel_ref[0, c]
            if table is None:
                wide = picture.astype(F32)
            else:
                wide = jnp.dot(picture, table, preferred_element_type=F32)
            for block in range(columns // 128):
                rows_ref[3 * c + block, :high, :] = wide[:, 128 * block:128 * block + 128]
        slots = 3 * side
        for group in range(out.shape[1] // 128):
            for block in range(columns // 128):
                lines = []
                for q in range(8 * group, 8 * group + 8):
                    if q < slots:
                        lines.append(rows_ref[q // side * 3 + block, pl.ds(q % side, grid, stride=side), :])
                    else:
                        lines.append(jnp.zeros((grid, 128), F32))
                lines = swap_chunks(lines)
                for g in range(8):
                    if 8 * block + g < grid:
                        flat_ref[group, pl.ds(8 * block + g, grid, stride=grid), :] = lines[g]
        for group in range(out.shape[1] // 128):
            out[:, 128 * group:128 * group + 128] = flat_ref[group, :grid * grid, :].astype(BF16)

def patch_all(pixels):
    shapes = []
    for picture, side in zip(pixels, SIDES):
        grid = picture.shape[2] // side
        shapes.append(jax.ShapeDtypeStruct((grid * grid, up_to(3 * side * SLOT, 128)), BF16))
    high = max(p.shape[2] for p in pixels)
    return pl.pallas_call(
        patch_kernel,
        out_shape=shapes,
        in_specs=[pl.BlockSpec(memory_space=pltpu.VMEM)] * 3,
        out_specs=[pl.BlockSpec(memory_space=pltpu.VMEM)] * 3,
        scratch_shapes=[pltpu.VMEM((9, high, 128), F32), pltpu.VMEM((max(s.shape[1] for s in shapes) // 128, max(s.shape[0] for s in shapes), 128), F32)],
        compiler_params=pltpu.CompilerParams(vmem_limit_bytes=24 * 2**20),
        cost_estimate=pl.CostEstimate(flops=5 * 10**9, bytes_accessed=4 * 10**6, transcendentals=0),
    )(*pixels)

def unpatch_kernel(starts, bounds, grad_ref, kernel_ref, *refs):
    outs, flat_ref, rows_ref = refs[:3], refs[3], refs[4]
    for i, side in enumerate(SIDES):
        out = outs[i]
        high = out.shape[2]
        grid = high // side
        columns = up_to(grid * SLOT, 128)
        width = bounds[i + 1] - bounds[i]
        grads = grad_ref[starts[i]:starts[i + 1], :]
        flat = jnp.dot(grads, kernel_ref[:, bounds[i]:bounds[i + 1]], preferred_element_type=F32)
        for group in range(width // 128):
            flat_ref[group, :grid * grid, :] = flat[:, 128 * group:128 * group + 128]
        slots = 3 * side
        for group in range(width // 128):
            for block in range(columns // 128):
                lines = []
                for g in range(8):
                    if 8 * block + g < grid:
                        lines.append(flat_ref[group, pl.ds(8 * block + g, grid, stride=grid), :])
                    else:
                        lines.append(jnp.zeros((grid, 128), F32))
                lines = swap_chunks(lines)
                for q in range(8 * group, min(8 * group + 8, slots)):
                    rows_ref[q // side * 3 + block, pl.ds(q % side, grid, stride=side), :] = lines[q % 8]
        table = None if side == SLOT else spread(side, grid, columns)
        for c in range(3):
            picture = jnp.concatenate([rows_ref[3 * c + block, :high, :] for block in range(columns // 128)], axis=1).astype(BF16)
            if table is not None:
                picture = lax.dot_general(picture, table, (((1,), (1,)), ((), ())), preferred_element_type=F32).astype(BF16)
            out[0, c] = picture

def unpatch_all(grads, kernels, starts, bounds, sides):
    high = max(sides)
    whole = pl.BlockSpec(memory_space=pltpu.VMEM)
    return pl.pallas_call(
        functools.partial(unpatch_kernel, starts, bounds),
        out_shape=[jax.ShapeDtypeStruct((1, 3, s, s), BF16) for s in sides],
        in_specs=[whole] * 2,
        out_specs=[whole] * 3,
        scratch_shapes=[pltpu.VMEM((max(e - s for s, e in zip(bounds, bounds[1:])) // 128, max(e - s for s, e in zip(starts, starts[1:])), 128), F32),
            pltpu.VMEM((9, high, 128), F32)],
        compiler_params=pltpu.CompilerParams(vmem_limit_bytes=32 * 2**20),
        cost_estimate=pl.CostEstimate(flops=5 * 10**9, bytes_accessed=10 * 10**6, transcendentals=0),
    )(grads, kernels)


def unit(values):
    mean_row = jnp.mean(values, axis=-1, keepdims=True)
    centred = values - mean_row
    inverse = lax.rsqrt(jnp.mean(centred * centred, axis=-1, keepdims=True) + 1e-06)
    return centred * inverse, inverse


def norm_backward(grad_out, unit_rows, inverse, gain):
    grad_unit = grad_out * gain
    inner = jnp.mean(grad_unit * unit_rows, axis=-1, keepdims=True)
    grad_in = inverse * (
        grad_unit - jnp.mean(grad_unit, axis=-1, keepdims=True) - unit_rows * inner
    )
    return grad_in, jnp.sum(grad_out * unit_rows, axis=0), jnp.sum(grad_out, axis=0)


def chunks(total, most):
    pieces = -(-total // most)
    size = -(-total // pieces)
    size = -(-size // 16) * 16
    return [(s, min(size, total - s)) for s in range(0, total, size)]

def outer_t(first, second):
    return lax.dot_general(first, second, (((1,), (1,)), ((), ())), preferred_element_type=F32)

def attend_kernel(starts, chunk, q_ref, k_ref, v_ref, *refs):
    pair = pl.program_id(0)
    mixed_ref, total_ref = refs[-2:]
    if len(refs) > 2:
        mixed_ref[: starts[0], :] = refs[0][: starts[0], :]

    @pl.when(pair == 0)
    def _():
        total_ref[...] = refs[1][...] if len(refs) > 2 else jnp.zeros_like(total_ref)

    for begin, end in zip(starts, starts[1:]):
        keys, values = k_ref[begin:end, :], v_ref[begin:end, :]
        for offset, size in chunks(end - begin, chunk):
            rows = slice(begin + offset, begin + offset + size)
            queries = q_ref[rows, :] * (HEAD ** -0.5)
            lane = lax.broadcasted_iota(jnp.int32, (size, 128), 1)
            mixed, totals = [], []
            for head in range(2):
                own = (lane < HEAD) if head == 0 else (lane >= HEAD)
                scores = outer_t(jnp.where(own, queries, jnp.zeros_like(queries)), keys)
                top = jnp.max(scores, axis=1, keepdims=True)
                expo = jnp.exp(scores - top)
                total = jnp.sum(expo, axis=1, keepdims=True)
                out = jnp.dot(expo.astype(BF16), values, preferred_element_type=F32)
                mixed.append(out / total)
                totals.append(top + jnp.log(total))
            mixed_ref[rows, :] = jnp.where(lane < HEAD, mixed[0], mixed[1]).astype(BF16)
            held = total_ref[rows, :]
            held = jnp.where(lane == 2 * pair, totals[0], held)
            total_ref[rows, :] = jnp.where(lane == 2 * pair + 1, totals[1], held)

def attend_forward(qkv, starts, done=(), chunk=576):
    rows, width = qkv.shape[0], qkv.shape[1] // 3
    pairs = width // 128
    block = lambda first: pl.BlockSpec((rows, 128), lambda j: (0, first * pairs + j))
    return pl.pallas_call(
        functools.partial(attend_kernel, starts, chunk),
        grid=(pairs,),
        out_shape=(jax.ShapeDtypeStruct((rows, width), BF16), jax.ShapeDtypeStruct((rows, 128), F32)),
        in_specs=[block(0), block(1), block(2)]
        + [block(0), pl.BlockSpec((rows, 128), lambda j: (0, 0))][: len(done)],
        out_specs=[pl.BlockSpec((rows, 128), lambda j: (0, j)), pl.BlockSpec((rows, 128), lambda j: (0, 0))],
        compiler_params=pltpu.CompilerParams(vmem_limit_bytes=32 * 2**20),
        cost_estimate=pl.CostEstimate(flops=10 * 10**9, bytes_accessed=8 * rows * width, transcendentals=0),
    )(qkv, qkv, qkv, *done)

def terms(value):
    first = value.astype(BF16)
    rest = value - first.astype(F32)
    second = rest.astype(BF16)
    return first, second, (rest - second.astype(F32)).astype(BF16)

def attend_back_kernel(starts, chunk, q_ref, k_ref, v_ref, mixed_ref, grad_ref, total_ref, out_ref, left, right, acc):
    pair = pl.program_id(0)
    scale = HEAD ** -0.5
    zero = jnp.zeros((), BF16)
    for begin, end in zip(starts, starts[1:]):
        size = end - begin
        for offset, part in chunks(size, chunk):
            rows = slice(begin + offset, begin + offset + part)
            lane = lax.broadcasted_iota(jnp.int32, (part, 128), 1)
            queries, grads = q_ref[rows, :] * scale, grad_ref[rows, :]
            product = grads.astype(F32) * mixed_ref[rows, :].astype(F32)
            total_all = total_ref[rows, :]
            for head in range(2):
                own = (lane < HEAD) if head == 0 else (lane >= HEAD)
                free = HEAD * (1 - head)
                inner = jnp.sum(jnp.where(own, product, 0.0), axis=1, keepdims=True)
                total = jnp.sum(jnp.where(lane == 2 * pair + head, total_all, 0.0), axis=1, keepdims=True)
                for target, value, line in ((left, queries, total), (right, grads, inner)):
                    wide = jnp.where(own, value, zero)
                    for i, term in enumerate(terms(line)):
                        wide = jnp.where(lane == free + i, term, wide)
                    target[head, offset:offset + part, :] = wide
        queries, grads = q_ref[begin:end, :], grad_ref[begin:end, :]
        acc[...] = jnp.zeros_like(acc)
        for offset, part in chunks(size, chunk):
            rows = slice(begin + offset, begin + offset + part)
            lane = lax.broadcasted_iota(jnp.int32, (part, 128), 1)
            keys, values = k_ref[rows, :], v_ref[rows, :]
            grad_key, grad_value = [], []
            for head in range(2):
                own = (lane < HEAD) if head == 0 else (lane >= HEAD)
                free = HEAD * (1 - head)
                minus = jnp.where((lane >= free) & (lane < free + 3), -jnp.ones((), BF16), zero)
                scores = outer_t(jnp.where(own, keys, minus), left[head, :size, :])
                probs = jnp.exp(scores)
                grad_scores = outer_t(jnp.where(own, values, minus), right[head, :size, :])
                grad_scores = (probs * grad_scores).astype(BF16)
                grad_value.append(jnp.dot(probs.astype(BF16), grads, preferred_element_type=F32))
                grad_key.append(jnp.dot(grad_scores, queries, preferred_element_type=F32))
                acc[head, :size, :] += lax.dot_general(grad_scores, keys, (((0,), (0,)), ((), ())), preferred_element_type=F32)
            out_ref[1, rows, :] = (jnp.where(lane < HEAD, *grad_key) * scale).astype(BF16)
            out_ref[2, rows, :] = jnp.where(lane < HEAD, *grad_value).astype(BF16)
        lane = lax.broadcasted_iota(jnp.int32, (size, 128), 1)
        out_ref[0, begin:end, :] = (jnp.where(lane < HEAD, acc[0, :size, :], acc[1, :size, :]) * scale).astype(BF16)

def attend_backward(qkv, mixed, totals, grad_mixed, starts, chunk=400):
    rows, width = mixed.shape
    pairs = width // 128
    longest = max(e - s for s, e in zip(starts, starts[1:]))
    block = lambda first: pl.BlockSpec((rows, 128), lambda j: (0, first * pairs + j))
    return pl.pallas_call(
        functools.partial(attend_back_kernel, starts, chunk),
        grid=(pairs,),
        out_shape=jax.ShapeDtypeStruct((3, rows, width), BF16),
        in_specs=[block(0), block(1), block(2), block(0), block(0), pl.BlockSpec((rows, 128), lambda j: (0, 0))],
        out_specs=pl.BlockSpec((3, rows, 128), lambda j: (0, 0, j)),
        scratch_shapes=[pltpu.VMEM((2, longest, 128), BF16), pltpu.VMEM((2, longest, 128), BF16), pltpu.VMEM((2, longest, 128), F32)],
        compiler_params=pltpu.CompilerParams(vmem_limit_bytes=32 * 2**20),
        cost_estimate=pl.CostEstimate(flops=40 * 10**9, bytes_accessed=16 * rows * width, transcendentals=0),
    )(qkv, qkv, qkv, mixed, grad_mixed, totals)


def slot_table(side, size, c):
    pixel = lax.broadcasted_iota(jnp.int32, (side * side, size), 0)
    column = lax.broadcasted_iota(jnp.int32, (side * side, size), 1)
    row, spot = column // SLOT - c * side, column % SLOT
    table = (row >= 0) & (row < side) & (spot < side) & (pixel == row * side + spot)
    return table.astype(BF16)


def two_terms(value):
    first = value.astype(BF16)
    return first, (value - first.astype(F32)).astype(BF16)


def resize_kernel(starts, *refs):
    sources, base_ref, pos_ref, small_ref, out_ref = refs[:3], refs[3], refs[4], refs[5], refs[6]
    resizes, sems = refs[7:10], refs[10]
    copies = [
        pltpu.make_async_copy(source, target, sems.at[i])
        for i, (source, target) in enumerate(zip(sources, resizes))
    ]
    for copy in copies:
        copy.start()
    share = base_ref.shape[1]
    base = jnp.concatenate([base_ref[c] for c in range(3)])
    for start, side, resize_ref, copy in zip(starts, SIDES, resizes, copies):
        copy.wait()
        size = up_to(3 * side * SLOT, 128)
        own = sum(outer_t(base, term) for term in two_terms(resize_ref[...])[::-1]).astype(BF16)
        if side == SLOT:
            for c in range(3):
                first = start + c * side * SLOT
                out_ref[:, first : first + side * SLOT] = own[c * share : (c + 1) * share]
        else:
            out_ref[:, start : start + size] = sum(
                dot(own[c * share : (c + 1) * share], slot_table(side, size, c)) for c in range(3)
            ).astype(BF16)
    spots, width = pos_ref.shape[1], out_ref.shape[1] - starts[3]

    def shift(rows, by):
        row = lax.broadcasted_iota(jnp.int32, (rows, width), 0)
        column = lax.broadcasted_iota(jnp.int32, (rows, width), 1)
        return (row + by == column).astype(BF16)

    out_ref[:, starts[3] :] = (
        dot(pos_ref[...], shift(spots, 0))
        + inner_t(small_ref[...], shift(small_ref.shape[0], spots))
    ).astype(BF16)


def resize_all(resizes, base_kernel, posemb, smalls, starts, columns):
    whole = pl.BlockSpec(memory_space=pltpu.VMEM)
    return pl.pallas_call(
        functools.partial(resize_kernel, starts),
        out_shape=jax.ShapeDtypeStruct((base_kernel.shape[1], columns), BF16),
        in_specs=[pl.BlockSpec(memory_space=pl.ANY)] * 3 + [whole] * 3,
        out_specs=whole,
        scratch_shapes=[pltpu.VMEM(r.shape, F32) for r in resizes] + [pltpu.SemaphoreType.DMA((3,))],
        compiler_params=pltpu.CompilerParams(vmem_limit_bytes=24 * 2**20),
        cost_estimate=pl.CostEstimate(flops=3 * 10**9, bytes_accessed=4 * 10**6, transcendentals=0),
    )(*resizes, base_kernel, posemb, smalls)


def embed_kernel(starts, bounds, spots, *refs):
    patches, table_ref, map_ref = refs[:3], refs[3], refs[4]
    embedded_ref, normed_ref, lines_ref = refs[5:]
    smalls = table_ref[:, bounds[3] :]
    row = lax.broadcasted_iota(jnp.int32, (16, 128), 0)
    lane = lax.broadcasted_iota(jnp.int32, (16, 128), 1)
    lines = outer_t(((lane == row + spots) & (row < 9)).astype(BF16), smalls)
    lines_ref[...] = lines
    for i, patch_ref in enumerate(patches):
        rows = slice(starts[i], starts[i + 1])
        value = outer_t(patch_ref[...], table_ref[:, bounds[i] : bounds[i + 1]])
        for part in reversed(terms(map_ref[rows, :])):
            value = value + outer_t(part, smalls)
        embedded_ref[rows, :] = value
        unit_rows, _ = unit(value)
        normed_ref[rows, :] = (unit_rows * lines[1:2] + lines[2:3]).astype(BF16)


def embed_all(patches, table, maps, starts, bounds, spots):
    whole = pl.BlockSpec(memory_space=pltpu.VMEM)
    rows, width = maps.shape[0], table.shape[0]
    return pl.pallas_call(
        functools.partial(embed_kernel, starts, bounds, spots),
        out_shape=(
            jax.ShapeDtypeStruct((rows, width), F32),
            jax.ShapeDtypeStruct((rows, width), BF16),
            jax.ShapeDtypeStruct((16, width), F32),
        ),
        in_specs=[whole] * 5,
        out_specs=[whole] * 3,
        compiler_params=pltpu.CompilerParams(vmem_limit_bytes=32 * 2**20),
        cost_estimate=pl.CostEstimate(flops=4 * 10**9, bytes_accessed=15 * 10**6, transcendentals=0),
    )(*patches, table, maps)


def base_gradient_kernel(starts, *refs):
    resizes, sum_ref, out_ref = refs[:3], refs[3], refs[4]
    share = sum_ref.shape[0]
    total = None
    for start, side, resize_ref in zip(starts, SIDES, resizes):
        size = up_to(3 * side * SLOT, 128)
        given = sum_ref[:, start : start + size]
        if side == SLOT:
            own = [given[:, c * side * SLOT : (c + 1) * side * SLOT] for c in range(3)]
        else:
            own = [outer_t(given, slot_table(side, size, c)).astype(BF16) for c in range(3)]
        own = jnp.concatenate(own)
        for term in two_terms(resize_ref[...])[::-1]:
            value = dot(own, term)
            total = value if total is None else total + value
    for c in range(3):
        out_ref[c] = total[c * share : (c + 1) * share]


def base_gradient(resizes, embed_sum, shape, starts):
    whole = pl.BlockSpec(memory_space=pltpu.VMEM)
    return pl.pallas_call(
        functools.partial(base_gradient_kernel, starts),
        out_shape=jax.ShapeDtypeStruct(shape, F32),
        in_specs=[whole] * 4,
        out_specs=whole,
        compiler_params=pltpu.CompilerParams(vmem_limit_bytes=24 * 2**20),
        cost_estimate=pl.CostEstimate(flops=3 * 10**9, bytes_accessed=4 * 10**6, transcendentals=0),
    )(*resizes, embed_sum)


def gelu_pair(value):
    slope = math.sqrt(2 / math.pi)
    square = value * value
    curve = jnp.tanh(value * (slope + (slope * 0.044715) * square))
    half = 0.5 * value
    rise = 0.5 + 0.5 * curve
    bend = (half - half * (curve * curve)) * (slope + (3 * slope * 0.044715) * square)
    return value * rise, rise + bend


def feed_kernel(starts, chunk, *refs):
    mixed_ref, w_out_ref, embedded_ref, lines_ref, b_up_ref, w_up_ref, w_down_ref = refs[:7]
    cotangents, finals = refs[7:10], refs[10:13]
    g_up_ref, g_down_ref, g_bias_ref = refs[13:16]
    middle_out, branch_ref, g_mixed_ref, g_out_ref, sums_ref = refs[16:21]
    middle, normed, grads, act, grad_up, total, back, sems = refs[21:]
    step, steps = pl.program_id(0), pl.num_programs(0)
    rows = middle.shape[0]

    @pl.when(step == 0)
    def _():
        copy = pltpu.make_async_copy(embedded_ref, middle, sems.at[0])
        copy.start()
        for i, ref in enumerate(cotangents):
            grads[starts[i] : starts[i + 1], :] = ref[0]
        copy.wait()
        for first, size in chunks(rows, chunk):
            part = slice(first, first + size)
            value = middle[part, :] + dot(mixed_ref[part, :], w_out_ref[...]) + lines_ref[5:6, :]
            middle[part, :] = value
            unit_rows, _ = unit(value)
            normed[part, :] = (unit_rows * lines_ref[6:7, :] + lines_ref[7:8, :]).astype(BF16)
            total[part, :] = value + lines_ref[8:9, :]
            back[part, :] = jnp.zeros((size, back.shape[1]), F32)

    column = jnp.zeros((1, w_up_ref.shape[1]), F32)
    for first, size in chunks(rows, chunk):
        part = slice(first, first + size)
        up = dot(normed[part, :], w_up_ref[...]) + b_up_ref[...]
        value, slope = gelu_pair(up)
        value = value.astype(BF16)
        act[part, :] = value
        grad = (slope * outer_t(grads[part, :], w_down_ref[...])).astype(BF16)
        grad_up[part, :] = grad
        column += jnp.sum(grad.astype(F32), axis=0, keepdims=True)
        total[part, :] += dot(value, w_down_ref[...])
        back[part, :] += outer_t(grad, w_up_ref[...])
    g_bias_ref[...] = column
    g_down_ref[...] = inner_t(act[...], grads[...]).astype(BF16)
    g_up_ref[...] = inner_t(normed[...], grad_up[...]).astype(BF16)

    @pl.when(step == steps - 1)
    def _():
        for i, ref in enumerate(finals):
            ref[0] = total[starts[i] : starts[i + 1], :].astype(BF16)
        width = middle.shape[1]
        sums = [jnp.zeros((1, width), F32)] * 4
        for first, size in chunks(rows, chunk):
            part = slice(first, first + size)
            unit_rows, inverse = unit(middle[part, :])
            out = back[part, :]
            down = grads[part, :].astype(F32)
            grad, gain, bias = norm_backward(out, unit_rows, inverse, lines_ref[6:7, :])
            grad = grad + down
            middle[part, :] = grad
            low = grad.astype(BF16)
            branch_ref[part, :] = low
            g_mixed_ref[part, :] = outer_t(low, w_out_ref[...]).astype(BF16)
            found = (gain[None], bias[None], jnp.sum(down, axis=0, keepdims=True),
                     jnp.sum(low.astype(F32), axis=0, keepdims=True))
            sums = [a + b for a, b in zip(sums, found)]
        copy = pltpu.make_async_copy(middle, middle_out, sems.at[0])
        copy.start()
        g_out_ref[...] = inner_t(mixed_ref[...], branch_ref[...]).astype(BF16)
        sums_ref[...] = jnp.concatenate(sums + [jnp.zeros((4, width), F32)])
        copy.wait()


def feed_all(mixed, w_up_out, embedded, lines, b_up, w_down, cotangents, starts, tile=512, chunk=1232):
    rows, width = mixed.shape
    hidden = w_down.shape[0]
    fixed = lambda *shape: pl.BlockSpec(shape, lambda t: (0,) * len(shape), pipeline_mode=pl.Buffered(1))
    whole = lambda *shape: pl.BlockSpec(shape, lambda t: (0,) * len(shape))
    anywhere = pl.BlockSpec(memory_space=pl.ANY)
    like = lambda shape, kind: jax.ShapeDtypeStruct(shape, kind)
    return pl.pallas_call(
        functools.partial(feed_kernel, starts, chunk),
        grid=(hidden // tile,),
        out_shape=[like(c.shape, BF16) for c in cotangents]
        + [
            like((width, hidden), BF16),
            like((hidden, width), BF16),
            like((1, hidden), F32),
            like((rows, width), F32),
            like((rows, width), BF16),
            like((rows, width), BF16),
            like((width, width), BF16),
            like((8, width), F32),
        ],
        in_specs=[
            fixed(rows, width),
            pl.BlockSpec((width, width), lambda t: (0, hidden // width), pipeline_mode=pl.Buffered(1)),
            anywhere,
            fixed(16, width),
            pl.BlockSpec((1, tile), lambda t: (0, t)),
            pl.BlockSpec((width, tile), lambda t: (0, t)),
            pl.BlockSpec((tile, width), lambda t: (t, 0)),
        ]
        + [fixed(*c.shape) for c in cotangents],
        out_specs=[whole(*c.shape) for c in cotangents]
        + [
            pl.BlockSpec((width, tile), lambda t: (0, t)),
            pl.BlockSpec((tile, width), lambda t: (t, 0)),
            pl.BlockSpec((1, tile), lambda t: (0, t)),
            anywhere,
            whole(rows, width),
            whole(rows, width),
            whole(width, width),
            whole(8, width),
        ],
        scratch_shapes=[
            pltpu.VMEM((rows, width), F32),
            pltpu.VMEM((rows, width), BF16),
            pltpu.VMEM((rows, width), BF16),
            pltpu.VMEM((rows, tile), BF16),
            pltpu.VMEM((rows, tile), BF16),
            pltpu.VMEM((rows, width), F32),
            pltpu.VMEM((rows, width), F32),
            pltpu.SemaphoreType.DMA((1,)),
        ],
        compiler_params=pltpu.CompilerParams(vmem_limit_bytes=60 * 2**20),
        cost_estimate=pl.CostEstimate(flops=40 * 10**9, bytes_accessed=50 * 10**6, transcendentals=0),
    )(mixed, w_up_out, embedded, lines, b_up, w_up_out, w_down, *cotangents)

def back_kernel(starts, bounds, spots, chunk, *refs):
    grad_ref, w_ref, embedded_ref, middle_ref, lines_ref, rows_ref, map_ref = refs[:7]
    patches, low_ref, out_ref, sums = refs[7:10], refs[10], refs[11], refs[12]
    rows, width = low_ref.shape
    sums[...] = rows_ref[...]
    totals = [jnp.zeros((1, width), F32)] * 4
    for first, size in chunks(rows, chunk):
        part = slice(first, first + size)
        out = sum(
            outer_t(grad_ref[i, part, :], w_ref[:, i * width : (i + 1) * width]) for i in range(3)
        )
        unit_rows, inverse = unit(embedded_ref[part, :])
        grad, gain, bias = norm_backward(out, unit_rows, inverse, lines_ref[1:2, :])
        low_ref[part, :] = (grad + middle_ref[part, :]).astype(BF16)
        found = [gain[None], bias[None]] + [
            jnp.sum(grad_ref[i, part, :].astype(F32), axis=0, keepdims=True) for i in (0, 2)
        ]
        totals = [a + b for a, b in zip(totals, found)]
    for i, value in enumerate(totals):
        sums[i + 1 : i + 2, :] = value
    for i, patch_ref in enumerate(patches):
        part = slice(starts[i], starts[i + 1])
        out_ref[:, bounds[i] : bounds[i + 1]] = inner_t(low_ref[part, :], patch_ref[...]).astype(BF16)
    row = lax.broadcasted_iota(jnp.int32, (16, 128), 0)
    lane = lax.broadcasted_iota(jnp.int32, (16, 128), 1)
    table = ((lane == row + spots) & (row < 13)).astype(BF16)
    smalls = inner_t(sums[...].astype(BF16), table)
    for term in reversed(terms(map_ref[...])[:2]):
        smalls = smalls + inner_t(low_ref[...], term)
    out_ref[:, bounds[3] :] = smalls.astype(BF16)


def back_all(grad_qkv, w_qkv, embedded, grad_middle, lines, rows_given, maps, patches, starts, bounds, spots, chunk=416):
    _, rows, width = grad_qkv.shape
    whole = pl.BlockSpec(memory_space=pltpu.VMEM)
    return pl.pallas_call(
        functools.partial(back_kernel, starts, bounds, spots, chunk),
        out_shape=(
            jax.ShapeDtypeStruct((rows, width), BF16),
            jax.ShapeDtypeStruct((width, bounds[3] + 128), BF16),
        ),
        in_specs=[whole] * 10,
        out_specs=[whole] * 2,
        scratch_shapes=[pltpu.VMEM((16, width), F32)],
        compiler_params=pltpu.CompilerParams(vmem_limit_bytes=48 * 2**20),
        cost_estimate=pl.CostEstimate(flops=8 * 10**9, bytes_accessed=25 * 10**6, transcendentals=0),
    )(grad_qkv, w_qkv, embedded, grad_middle, lines, rows_given, maps, *patches)


def dot(first, second):
    return jnp.dot(first, second, preferred_element_type=F32)


def inner_t(first, second):
    return lax.dot_general(first, second, (((0,), (0,)), ((), ())), preferred_element_type=F32)


def body(count, pixels, resizes, posmaps, weights, cotangents):
    base_kernel, patch_bias, posemb = weights[:3]
    ln1_gain, ln1_bias, qkv_weight, qv_bias, out_weight, out_bias = weights[3:9]
    ln2_gain, ln2_bias, up_weight, up_bias, down_weight, down_bias = weights[9:]
    channels, base_pixels, share = base_kernel.shape
    width = share * count
    spots = posemb.shape[0]
    where = jnp.stack([lax.axis_index("fsdp"), lax.axis_index("rep")]).astype(jnp.int32)
    tokens = [c.shape[1] for c in cotangents]
    starts = [sum(tokens[:i]) for i in range(4)]
    bits = [2**i for i in range(1, count.bit_length() - 1)]
    inward = [(bit,) for bit in bits]
    outward = inward[::-1]
    turned = inward[:1] + outward[:-1]
    short = inward[:-2] + [(bits[-2], bits[-1], bits[-2] + bits[-1])]

    up_per = up_bias.shape[0] // share
    used = spots + 9 + up_per
    bounds = [0]
    for side in SIDES:
        bounds.append(bounds[-1] + up_to(3 * side * SLOT, 128))
    columns = bounds[3] + 128
    smalls = jnp.concatenate(
        [
            v.reshape(1, share)
            for v in (
                patch_bias,
                ln1_gain,
                ln1_bias,
                qv_bias[0],
                qv_bias[1],
                out_bias,
                ln2_gain,
                ln2_bias,
                down_bias,
            )
        ]
        + [up_bias.reshape(share, up_per).T, jnp.zeros((16 - 9 - up_per, share), BF16)]
    )
    maps = jnp.concatenate(posmaps)
    maps = jnp.concatenate(
        [maps, jnp.ones((maps.shape[0], 1), F32), jnp.zeros((maps.shape[0], 127 - spots), F32)],
        axis=1,
    )

    base_turned = base_kernel.swapaxes(1, 2)
    qkv_all = Gather(qkv_weight, where, count, outward, split=True).send()
    embed_shard = resize_all(resizes, base_turned, posemb.T, smalls, bounds, columns)
    cut = 1280
    embed_low = Gather(embed_shard[:, :cut], where, count, outward).send()
    embed_high = Gather(embed_shard[:, cut:], where, count, turned).send()
    patches = patch_all(pixels)
    for chain in (qkv_all, embed_high, embed_low):
        patches = finish(patches, chain)
        chain.send()
    patches, up_weight, out_weight = after(patches, up_weight, out_weight)
    up_high = Gather(
        jnp.concatenate([up_weight[:, 2 * width :], out_weight], axis=1),
        where,
        count,
        outward,
        split=True,
    ).send()
    for chain in (qkv_all, embed_low, embed_high):
        patches = finish(patches, chain)
        chain.send()
    patches, up_weight, down_weight = after(patches, up_weight, down_weight)
    up_low = Gather(up_weight[:, : 2 * width], where, count, outward).send()
    for chain in (up_high, qkv_all, embed_high, embed_low):
        patches = finish(patches, chain)
        chain.send()
    patches, down_weight = after(patches, down_weight)
    down_all = Gather(down_weight, where, count, outward).send()
    patches = finish(patches, up_high)
    up_high.send()
    patches = finish(patches, up_low)
    up_low.send()
    patches = complete(patches, embed_low, embed_high)
    embed_whole = place([embed_low, embed_high], where, count)
    embedded, normed_in, lines = embed_all(patches, embed_whole, maps, starts, bounds, spots)
    normed_in = finish(normed_in, down_all)
    down_all.send()
    normed_in = finish(normed_in, qkv_all)
    qkv_all.send()
    normed_in = finish(normed_in, up_low)
    up_low.send()
    normed_in = complete(normed_in, qkv_all)
    w_qkv = place([qkv_all], where, count)
    bias_three = jnp.concatenate([lines[3], jnp.zeros_like(lines[3]), lines[4]])
    qkv = (dot(normed_in, w_qkv) + bias_three).astype(BF16)
    qkv = finish(qkv, up_high)
    up_high.send()
    qkv = finish(qkv, down_all)
    down_all.send()
    mixed, totals = attend_forward(qkv, starts[:3])
    mixed, totals = finish((mixed, totals), up_low)
    up_low.send()
    mixed, totals = attend_forward(qkv, starts[2:], (mixed, totals))
    mixed = finish(mixed, up_high, up_low)
    up_high.send()
    mixed = finish(mixed, down_all)
    down_all.send()
    mixed = complete(mixed, up_high)
    if up_low.steps:
        mixed = complete(mixed, up_low.send())
    w_up_out = place([up_low, up_high], where, count)
    mixed = complete(mixed, down_all)
    w_down = place([down_all], where, count)
    b_up = embed_whole[:, bounds[3] + spots + 9 : bounds[3] + used].astype(F32).reshape(1, -1)
    (
        *results,
        grad_w_up,
        grad_w_down,
        grad_b_up,
        grad_middle,
        grad_branch,
        grad_mixed,
        grad_w_out,
        sums,
    ) = feed_all(mixed, w_up_out, embedded, lines, b_up, w_down, cotangents, starts)
    hidden = grad_w_up.shape[1]
    sum_down = Scatter([grad_w_down], [(0, 0, width)], where, count, inward).send()
    sum_up = Scatter(
        [grad_w_up, grad_w_out], [(0, 0, hidden), (1, 0, width)], where, count, inward, split=True
    ).send()
    grad_mixed = finish(grad_mixed, sum_down)
    sum_down.send()
    grad_mixed = finish(grad_mixed, sum_up)
    sum_up.send()
    grad_qkv = attend_backward(qkv, mixed, totals, grad_mixed, starts)
    rows_given = jnp.concatenate(
        [
            jnp.zeros((5, width), F32),
            sums[3:4],
            sums[:3],
            grad_b_up.reshape(width, up_per).T,
            jnp.zeros((7 - up_per, width), F32),
        ]
    )
    grad_qkv = finish(grad_qkv, sum_down)
    sum_down.send()
    grad_qkv = finish(grad_qkv, sum_up)
    sum_up.send()
    grad_low, grad_embed = back_all(
        grad_qkv, w_qkv, embedded, grad_middle, lines, rows_given, maps, patches, starts, bounds, spots
    )
    for chain in (sum_down, sum_up):
        grad_low = finish(grad_low, chain)
        chain.send()
    grad_qkv, grad_low = after(grad_qkv, grad_low)
    grad_w_qkv = [inner_t(normed_in, grad_qkv[i]).astype(BF16) for i in range(3)]
    half = columns // 2
    cut_low = 5 * width // 3
    low_segments = [(0, 0, half), (1, 0, width), (2, 0, cut_low - width)]
    high_segments = [(0, half, half), (1, cut_low - width, 2 * width - cut_low), (2, 0, width)]
    sum_low = Scatter([grad_embed, *grad_w_qkv[:2]], low_segments, where, count, short).send()
    sum_high = Scatter(
        [grad_embed, *grad_w_qkv[1:]], high_segments, where, count, short, split=True
    ).send()
    grad_low = finish(grad_low, sum_low)
    sum_low.send()
    grad_low = finish(grad_low, sum_high)
    sum_high.send()
    pixel_grads = unpatch_all(grad_low, embed_whole, starts, bounds, [p.shape[2] for p in pixels])
    pixel_grads = complete(pixel_grads, sum_down, sum_up, sum_low, sum_high)

    low, high = sum_low.result, sum_high.result
    embed_sum = jnp.concatenate([low[:, :half], high[:, :half]], axis=1)
    qkv_sum = jnp.concatenate([low[:, half:], high[:, half:]], axis=1).astype(F32)
    up_sum = sum_up.result.astype(F32)
    base_grad = base_gradient(resizes, embed_sum, base_turned.shape, bounds).swapaxes(1, 2)
    small_sum = embed_sum[:, bounds[3] : bounds[3] + used].astype(F32)
    vectors = small_sum[:, spots : spots + 9].T
    return (
        *results,
        *pixel_grads,
        base_grad,
        vectors[0],
        small_sum[:, :spots].T,
        vectors[1],
        vectors[2],
        qkv_sum,
        vectors[3:5],
        up_sum[:, hidden:],
        vectors[5],
        vectors[6],
        vectors[7],
        up_sum[:, :hidden],
        small_sum[:, spots + 9 :].reshape(-1),
        sum_down.result.astype(F32),
        vectors[8],
    )


def solution(mesh):
    count = mesh.shape["fsdp"]

    def run(*args):
        return body(count, args[:3], args[3:6], args[6:9], args[9:24], args[24:])

    images = ("rep", "fsdp")
    weight_specs = (
        P(None, None, "fsdp"),
        P("fsdp"),
        P(None, "fsdp"),
        P("fsdp"),
        P("fsdp"),
        P("fsdp", None),
        P(None, "fsdp"),
        P("fsdp", None),
        P("fsdp"),
        P("fsdp"),
        P("fsdp"),
        P("fsdp", None),
        P("fsdp"),
        P("fsdp", None),
        P("fsdp"),
    )
    return jax.shard_map(
        run,
        mesh=mesh,
        in_specs=(P(images, None, None, None),) * 3
        + (P(),) * 6
        + weight_specs
        + (P(images, None, None),) * 3,
        out_specs=(P(images, None, None),) * 3
        + (P(images, None, None, None),) * 3
        + weight_specs,
        check_vma=False,
    )
```

```python
import functools
import math

import jax
import jax.numpy as jnp
from jax import lax
from jax.experimental import pallas as pl
from jax.experimental.pallas import tpu as pltpu
from jax.sharding import PartitionSpec as P

HEADS = 12
HEAD = 64
SIDES = (10, 12, 16)
SLOT = 16
F32 = jnp.float32
BF16 = jnp.bfloat16
BRIEF = pl.CostEstimate(flops=1, bytes_accessed=1, transcendentals=0)


def swap(value, axis, size, bit):
    return lax.ppermute(value, axis, [(i, i ^ bit) for i in range(size)])


def after(first, *rest):
    return lax.optimization_barrier((first, *rest))


class Gather:
    def __init__(self, shard, where, count, steps, split=False):
        self.count, self.split, self.columns = count, split, shard.shape[1]
        if split:
            width = shard.shape[1] // 2
            shard = lax.dynamic_slice_in_dim(shard, where[1] * width, width, 1)
        self.held = [(shard[None], [0])]
        self.steps = list(steps) + (["rep"] if split else []) + ["core"]
        self.step = None
        self.pieces = []
        self.ready = [shard[None]]

    def prepare(self):
        if not self.steps:
            self.ready = []
            return
        if len(self.held) > 1 and len(self.held[0]) == 2:
            offsets = [o for _, offsets in self.held for o in offsets]
            self.held = [(join([blocks for blocks, _ in self.held]), offsets)]
        self.ready = [blocks for blocks, *_ in self.held]

    def renew(self, ready):
        if ready:
            self.held = [(blocks, *h[1:]) for blocks, h in zip(ready, self.held)]
        self.ready = ready

    def send(self):
        self.step, self.steps = self.steps[0], self.steps[1:]
        if self.step in ("rep", "core"):
            axis, size = ("rep", 2) if self.step == "rep" else ("fsdp", self.count)
            self.sent = [swap(blocks, axis, size, 1) for blocks in self.ready]
        else:
            self.sent = [swap(self.ready[0], "fsdp", self.count, offset) for offset in self.step]
        return self

    def take(self, arrived):
        if self.step == "rep":
            self.held = [(*h, 0) for h in self.held] + [
                (blocks, h[1], 1) for blocks, h in zip(arrived, self.held)
            ]
        elif self.step == "core":
            held = [h if len(h) == 3 else (*h, None) for h in self.held]
            self.held = held + [
                (blocks, [o ^ 1 for o in h[1]], h[2]) for blocks, h in zip(arrived, held)
            ]
        else:
            offsets = self.held[0][1]
            self.held = self.held + [
                (blocks, [o ^ offset for o in offsets])
                for blocks, offset in zip(arrived, self.step)
            ]


def finish(anchor, *chains):
    sizes = [len(chain.sent) for chain in chains]
    anchor, *flat = after(anchor, *[part for chain in chains for part in chain.sent])
    for chain, size in zip(chains, sizes):
        chain.take(flat[:size])
        chain.prepare()
        flat = flat[size:]
    sizes = [len(chain.ready) for chain in chains]
    anchor, *flat = after(anchor, *[part for chain in chains for part in chain.ready])
    for chain, size in zip(chains, sizes):
        chain.renew(flat[:size])
        flat = flat[size:]
    return anchor


def together(anchor, *chains):
    anchor = finish(anchor, *chains)
    for chain in chains:
        if chain.steps:
            chain.send()
    return anchor


def go_on(anchor, *chains):
    for chain in chains:
        anchor = together(anchor, chain)
    return anchor


def complete(anchor, *chains):
    while chains:
        left = [chain for chain in chains if chain.steps]
        anchor = go_on(anchor, *chains)
        chains = left
    return anchor


def place_copies(pieces, parts, whole, where_ref, sems):
    me, other = where_ref[0], where_ref[1]
    copies = []
    for part, (offsets, half, first, columns) in zip(parts, pieces):
        rows = part.shape[1]
        for k, offset in enumerate(offsets):
            row = pl.ds(pl.multiple_of(lax.bitwise_xor(me, offset) * rows, rows), rows)
            if half is None:
                target = whole.at[row, pl.ds(first, columns)]
            else:
                width = columns // 2
                start = pl.multiple_of(first + lax.bitwise_xor(other, half) * width, 128)
                target = whole.at[row, pl.ds(start, width)]
            copies.append(pltpu.make_async_copy(part.at[k], target, sems.at[len(copies)]))
    return copies


def copies_of(pieces):
    return sum(len(offsets) for offsets, *_ in pieces)


def place_kernel(pieces, me_ref, *refs):
    parts, whole, sems = refs[: len(pieces)], refs[len(pieces)], refs[len(pieces) + 1]
    me, other = me_ref[0], me_ref[1]
    copies = []
    for part, (offsets, half, first, columns) in zip(parts, pieces):
        for k, offset in enumerate(offsets):
            row = lax.bitwise_xor(me, offset)
            if half is None:
                target = whole.at[row, :, pl.ds(first, columns)]
            else:
                width = columns // 2
                start = pl.multiple_of(first + lax.bitwise_xor(other, half) * width, 128)
                target = whole.at[row, :, pl.ds(start, width)]
            copies.append(pltpu.make_async_copy(part.at[k], target, sems.at[len(copies)]))
    for copy in copies:
        copy.start()
    for copy in copies:
        copy.wait()


def place(gathers, where, count):
    parts, pieces = parts_of(gathers)
    rows, kind = parts[0].shape[1], parts[0].dtype
    columns = sum(g.columns for g in gathers)
    whole = pl.pallas_call(
        functools.partial(place_kernel, pieces),
        out_shape=jax.ShapeDtypeStruct((count, rows, columns), kind),
        in_specs=[pl.BlockSpec(memory_space=pltpu.SMEM)]
        + [pl.BlockSpec(memory_space=pl.ANY)] * len(pieces),
        out_specs=pl.BlockSpec(memory_space=pltpu.VMEM),
        scratch_shapes=[pltpu.SemaphoreType.DMA((copies_of(pieces),))],
        compiler_params=pltpu.CompilerParams(vmem_limit_bytes=16 * 2**20),
        cost_estimate=BRIEF,
    )(where, *parts)
    return whole.reshape(count * rows, columns)


def parts_of(gathers):
    parts, pieces, first = [], [], 0
    for g in gathers:
        for blocks, offsets, half in g.held:
            parts.append(blocks)
            pieces.append((tuple(offsets), half, first, g.columns))
        first += g.columns
    return parts, pieces


def regroup(blocks, rows, count):
    parts, first = [], 0
    for size in rows:
        part = blocks[:, first : first + size]
        parts.append(part.reshape(count, -1, blocks.shape[2]))
        first += size
    return jnp.concatenate(parts, axis=1)


class Parts:
    def __init__(self, gathers, where, count, rows=None):
        self.columns = sum(g.columns for g in gathers)
        self.where = where
        if count == 16:
            self.parts, self.pieces = parts_of(gathers)
        else:
            whole = place(gathers, where, count).reshape(count, -1, self.columns)
            rows = rows or (whole.shape[1],)
            self.parts = [regroup(whole, rows, 16)]
            self.pieces = [(tuple(range(16)), None, 0, self.columns)]
            self.where = jnp.zeros_like(where)

    def pairs(self, halves):
        if len(self.parts) > 1:
            near = len(self.parts) // 2
            assert near == halves and all(piece[0] == ORDER for piece in self.pieces[:near])
            return self.parts
        size = self.columns // halves
        return [
            jnp.stack([self.parts[0][o + core, :, h * size : (h + 1) * size] for o in ORDER])
            for core in range(2)
            for h in range(halves)
        ]


def ordered(keep, give, where, count, rows=None, split=False):
    if count == 16:
        return keep, give
    if not split:
        keep, give = keep[None], give[None]
    whole = jnp.stack([keep, give], axis=2)
    halves, blocks, _, size, columns = whole.shape
    whole = whole.reshape(halves, 2 * blocks, size, columns)
    whole = jnp.concatenate([whole[h] for h in range(halves)], axis=2)
    columns = whole.shape[2]
    whole = regroup(whole, rows or (size,), count).reshape(-1, columns)
    found = take([whole], [(0, 0, columns)], where, count, split)
    if split:
        return jnp.stack(found[:2]), jnp.stack(found[2:])
    return found


def take_kernel(count, split, segments, me_ref, *refs):
    inputs = max(which for which, *_ in segments) + 1
    wholes, outs, sems = refs[:inputs], refs[inputs:-1], refs[-1]
    me, other = me_ref[0], me_ref[1]
    half = outs[0].shape[2]

    def copies(switch):
        found = []
        for which, start, columns, first in segments:
            for d in range(count):
                source = wholes[which].at[lax.bitwise_xor(me, d), :, pl.ds(start, columns)]
                side = (first // half) ^ switch
                target = outs[2 * (d % 2) + side] if split else outs[d % 2]
                target = target.at[d // 2, :, pl.ds(first % half, columns)]
                found.append(pltpu.make_async_copy(source, target, sems.at[len(found)]))
        return found

    def run(switch):
        found = copies(switch)
        for copy in found:
            copy.start()
        for copy in found:
            copy.wait()

    if split:
        for switch in range(2):
            pl.when(other == switch)(functools.partial(run, switch))
    else:
        run(0)


def take(wholes, segments, where, count, split):
    rows = wholes[0].shape[0] // count
    blocks = [w.reshape(count, rows, w.shape[1]) for w in wholes]
    columns = sum(segment[2] for segment in segments)
    half = columns // 2 if split else columns
    ends, first = [], 0
    for which, start, size in segments:
        while size:
            room = min(size, half - first % half)
            ends.append((which, start, room, first))
            first, start, size = first + room, start + room, size - room
    shape = jax.ShapeDtypeStruct((count // 2, rows, half), wholes[0].dtype)
    outs = 4 if split else 2
    return pl.pallas_call(
        functools.partial(take_kernel, count, split, ends),
        out_shape=(shape,) * outs,
        in_specs=[pl.BlockSpec(memory_space=pltpu.SMEM)]
        + [pl.BlockSpec(memory_space=pltpu.VMEM)] * len(blocks),
        out_specs=[pl.BlockSpec(memory_space=pl.ANY)] * outs,
        scratch_shapes=[pltpu.SemaphoreType.DMA((count * len(ends),))],
        compiler_params=pltpu.CompilerParams(vmem_limit_bytes=16 * 2**20),
        cost_estimate=BRIEF,
    )(where, *blocks)


def add(*values):
    return sum(value.astype(F32) for value in values).astype(BF16)


def join_kernel(*refs):
    *parts, whole = refs
    first = 0
    for part in parts:
        whole[first : first + part.shape[0]] = part[...]
        first += part.shape[0]


def join(parts):
    blocks = sum(part.shape[0] for part in parts)
    whole = pl.BlockSpec(memory_space=pltpu.VMEM)
    return pl.pallas_call(
        join_kernel,
        out_shape=jax.ShapeDtypeStruct((blocks, *parts[0].shape[1:]), parts[0].dtype),
        in_specs=[whole] * len(parts),
        out_specs=whole,
        compiler_params=pltpu.CompilerParams(vmem_limit_bytes=16 * 2**20),
        cost_estimate=BRIEF,
    )(*parts)


def merge_kernel(groups, parts, *refs):
    outs = refs[parts:]
    for group, out in zip(groups, outs):
        for j, index in enumerate(group):
            out[j] = sum(ref[index].astype(F32) for ref in refs[:parts]).astype(BF16)


def merge(parts, groups):
    rest = parts[0].shape[-2:]
    whole = pl.BlockSpec(memory_space=pltpu.VMEM)
    return pl.pallas_call(
        functools.partial(merge_kernel, groups, len(parts)),
        out_shape=[jax.ShapeDtypeStruct((len(group), *rest), BF16) for group in groups],
        in_specs=[whole] * len(parts),
        out_specs=[whole] * len(groups),
        compiler_params=pltpu.CompilerParams(vmem_limit_bytes=24 * 2**20),
        cost_estimate=BRIEF,
    )(*parts)


class Scatter:
    def __init__(self, keep, give, where, count, steps, split=False):
        self.where, self.count, self.split = where, count, split
        self.keep, self.give = keep, give
        self.steps = ["core"] + (["half"] if split else []) + list(steps) + ["rep"]
        self.offsets = list(range(0, count, 2))
        self.step = None

        self.ready = [give]

    def prepare(self):
        pass

    def renew(self, ready):
        self.ready = ready

    def send(self):
        self.step, self.steps = self.steps[0], self.steps[1:]
        if self.step in ("half", "rep"):
            self.sent = [swap(self.ready[0], "rep", 2, 1)]
        else:
            offsets = [1] if self.step == "core" else self.step
            self.sent = [
                swap(part, "fsdp", self.count, offset)
                for part, offset in zip(self.ready, offsets)
            ]
        return self

    def share_out(self, parts):
        step = self.steps[0]
        if step == "rep":
            self.held = merge(parts, [[0]])[0][0]
            self.ready = [self.held]
            return
        mask = 0
        for offset in step:
            mask |= offset
        stay = [o for o in self.offsets if o & mask == 0]
        groups = [[self.offsets.index(o | offset) for o in stay] for offset in (0, *step)]
        self.staying, *self.ready = merge(parts, groups)
        self.offsets = stay

    def take(self, arrived):
        if self.step == "core" and self.split:
            blocks = len(self.offsets)
            flat = [a.reshape(2 * blocks, *a.shape[2:]) for a in (self.keep, *arrived)]
            away, self.staying = merge(
                flat, [list(range(blocks, 2 * blocks)), list(range(blocks))]
            )
            self.ready = [away]
        elif self.step == "core":
            self.share_out([self.keep, *arrived])
        elif self.step == "rep":
            if self.split:
                low = self.where[1] == 0
                self.result = [
                    jnp.where(low, self.held, arrived[0]),
                    jnp.where(low, arrived[0], self.held),
                ]
            else:
                self.result = add(self.held, arrived[0])
            self.ready = []
        else:
            self.share_out([self.staying, *arrived])


def up_to(value, unit):
    return -(-value // unit) * unit

def swap_chunks(lines):
    chunk = lax.broadcasted_iota(jnp.int32, lines[0].shape, 1) // SLOT
    for step in (1, 2, 4):
        stays = (chunk & step) == 0
        for i in range(8):
            if i & step == 0:
                low, high = lines[i], lines[i + step]
                lines[i] = jnp.where(stays, low, pltpu.roll(high, step * SLOT, 1))
                lines[i + step] = jnp.where(stays, pltpu.roll(low, 128 - step * SLOT, 1), high)
    return lines

def spread(side, grid, columns):
    pixel = lax.broadcasted_iota(jnp.int32, (grid * side, columns), 0)
    column = lax.broadcasted_iota(jnp.int32, (grid * side, columns), 1)
    place = column % SLOT
    return ((pixel == column // SLOT * side + place) & (place < side)).astype(BF16)

def patch_kernel(*refs):
    pixels, outs, rows_ref, flat_ref = refs[:3], refs[3:6], refs[6], refs[7]
    for side, pixel_ref, out in zip(SIDES, pixels, outs):
        high = pixel_ref.shape[2]
        grid = high // side
        columns = up_to(grid * SLOT, 128)
        table = None if side == SLOT else spread(side, grid, columns)
        for c in range(3):
            picture = pixel_ref[0, c]
            if table is None:
                wide = picture.astype(F32)
            else:
                wide = jnp.dot(picture, table, preferred_element_type=F32)
            for block in range(columns // 128):
                rows_ref[3 * c + block, :high, :] = wide[:, 128 * block:128 * block + 128]
        slots = 3 * side
        for group in range(out.shape[1] // 128):
            for block in range(columns // 128):
                lines = []
                for q in range(8 * group, 8 * group + 8):
                    if q < slots:
                        lines.append(rows_ref[q // side * 3 + block, pl.ds(q % side, grid, stride=side), :])
                    else:
                        lines.append(jnp.zeros((grid, 128), F32))
                lines = swap_chunks(lines)
                for g in range(8):
                    if 8 * block + g < grid:
                        flat_ref[group, pl.ds(8 * block + g, grid, stride=grid), :] = lines[g]
        for group in range(out.shape[1] // 128):
            out[:, 128 * group:128 * group + 128] = flat_ref[group, :grid * grid, :].astype(BF16)

def patch_all(pixels):
    shapes = []
    for picture, side in zip(pixels, SIDES):
        grid = picture.shape[2] // side
        shapes.append(jax.ShapeDtypeStruct((grid * grid, up_to(3 * side * SLOT, 128)), BF16))
    high = max(p.shape[2] for p in pixels)
    return pl.pallas_call(
        patch_kernel,
        out_shape=shapes,
        in_specs=[pl.BlockSpec(memory_space=pltpu.VMEM)] * 3,
        out_specs=[pl.BlockSpec(memory_space=pltpu.VMEM)] * 3,
        scratch_shapes=[pltpu.VMEM((9, high, 128), F32), pltpu.VMEM((max(s.shape[1] for s in shapes) // 128, max(s.shape[0] for s in shapes), 128), F32)],
        compiler_params=pltpu.CompilerParams(vmem_limit_bytes=40 * 2**20),
        cost_estimate=BRIEF,
    )(*pixels)

def unpatch_kernel(pieces, starts, bounds, where_ref, grad_ref, *refs):
    parts, refs = refs[: len(pieces)], refs[len(pieces) :]
    outs, flat_ref, rows_ref, kernel_ref, sems = refs[:3], *refs[3:]
    copies = place_copies(pieces, parts, kernel_ref, where_ref, sems)
    for copy in copies:
        copy.start()
    for copy in copies:
        copy.wait()
    for i, side in enumerate(SIDES):
        out = outs[i]
        high = out.shape[2]
        grid = high // side
        columns = up_to(grid * SLOT, 128)
        width = bounds[i + 1] - bounds[i]
        grads = grad_ref[starts[i]:starts[i + 1], :]
        flat = jnp.dot(grads, kernel_ref[:, bounds[i]:bounds[i + 1]], preferred_element_type=F32)
        for group in range(width // 128):
            flat_ref[group, :grid * grid, :] = flat[:, 128 * group:128 * group + 128]
        slots = 3 * side
        for group in range(width // 128):
            for block in range(columns // 128):
                lines = []
                for g in range(8):
                    if 8 * block + g < grid:
                        lines.append(flat_ref[group, pl.ds(8 * block + g, grid, stride=grid), :])
                    else:
                        lines.append(jnp.zeros((grid, 128), F32))
                lines = swap_chunks(lines)
                for q in range(8 * group, min(8 * group + 8, slots)):
                    rows_ref[q // side * 3 + block, pl.ds(q % side, grid, stride=side), :] = lines[q % 8]
        table = None if side == SLOT else spread(side, grid, columns)
        for c in range(3):
            picture = jnp.concatenate([rows_ref[3 * c + block, :high, :] for block in range(columns // 128)], axis=1).astype(BF16)
            if table is not None:
                picture = lax.dot_general(picture, table, (((1,), (1,)), ((), ())), preferred_element_type=F32).astype(BF16)
            out[0, c] = picture

def unpatch_all(grads, embed_parts, starts, bounds, sides):
    high = max(sides)
    whole = pl.BlockSpec(memory_space=pltpu.VMEM)
    parts = embed_parts.parts
    return pl.pallas_call(
        functools.partial(unpatch_kernel, embed_parts.pieces, starts, bounds),
        out_shape=[jax.ShapeDtypeStruct((1, 3, s, s), BF16) for s in sides],
        in_specs=[pl.BlockSpec(memory_space=pltpu.SMEM), whole]
        + [pl.BlockSpec(memory_space=pl.ANY)] * len(parts),
        out_specs=[whole] * 3,
        scratch_shapes=[
            pltpu.VMEM(
                (
                    max(e - s for s, e in zip(bounds, bounds[1:])) // 128,
                    max(e - s for s, e in zip(starts, starts[1:])),
                    128,
                ),
                F32,
            ),
            pltpu.VMEM((9, high, 128), F32),
            pltpu.VMEM((grads.shape[1], embed_parts.columns), BF16),
            pltpu.SemaphoreType.DMA((copies_of(embed_parts.pieces),)),
        ],
        compiler_params=pltpu.CompilerParams(vmem_limit_bytes=32 * 2**20),
        cost_estimate=BRIEF,
    )(embed_parts.where, grads, *parts)


def unit(values):
    mean_row = jnp.mean(values, axis=-1, keepdims=True)
    centred = values - mean_row
    inverse = lax.rsqrt(jnp.mean(centred * centred, axis=-1, keepdims=True) + 1e-06)
    return centred * inverse, inverse


def norm_backward(grad_out, unit_rows, inverse, gain):
    grad_unit = grad_out * gain
    inner = jnp.mean(grad_unit * unit_rows, axis=-1, keepdims=True)
    grad_in = inverse * (
        grad_unit - jnp.mean(grad_unit, axis=-1, keepdims=True) - unit_rows * inner
    )
    return grad_in, jnp.sum(grad_out * unit_rows, axis=0), jnp.sum(grad_out, axis=0)


def chunks(total, most):
    pieces = -(-total // most)
    size = -(-total // pieces)
    size = -(-size // 16) * 16
    return [(s, min(size, total - s)) for s in range(0, total, size)]

def outer_t(first, second):
    return lax.dot_general(first, second, (((1,), (1,)), ((), ())), preferred_element_type=F32)

def attend_kernel(starts, chunk, q_ref, k_ref, v_ref, *refs):
    pair = pl.program_id(0)
    mixed_ref, total_ref = refs[-2:]
    if len(refs) > 2:
        mixed_ref[: starts[0], :] = refs[0][: starts[0], :]

    @pl.when(pair == 0)
    def _():
        total_ref[...] = refs[1][...] if len(refs) > 2 else jnp.zeros_like(total_ref)

    for begin, end in zip(starts, starts[1:]):
        keys, values = k_ref[begin:end, :], v_ref[begin:end, :]
        for offset, size in chunks(end - begin, chunk):
            rows = slice(begin + offset, begin + offset + size)
            queries = q_ref[rows, :] * (HEAD ** -0.5)
            lane = lax.broadcasted_iota(jnp.int32, (size, 128), 1)
            mixed, totals = [], []
            for head in range(2):
                own = (lane < HEAD) if head == 0 else (lane >= HEAD)
                scores = outer_t(jnp.where(own, queries, jnp.zeros_like(queries)), keys)
                top = jnp.max(scores, axis=1, keepdims=True)
                expo = jnp.exp(scores - top)
                total = jnp.sum(expo, axis=1, keepdims=True)
                out = jnp.dot(expo.astype(BF16), values, preferred_element_type=F32)
                mixed.append(out / total)
                totals.append(top + jnp.log(total))
            mixed_ref[rows, :] = jnp.where(lane < HEAD, mixed[0], mixed[1]).astype(BF16)
            held = total_ref[rows, :]
            held = jnp.where(lane == 2 * pair, totals[0], held)
            total_ref[rows, :] = jnp.where(lane == 2 * pair + 1, totals[1], held)

def attend_forward(qkv, starts, done=(), chunk=576):
    rows, width = qkv.shape[0], qkv.shape[1] // 3
    pairs = width // 128
    block = lambda first: pl.BlockSpec((rows, 128), lambda j: (0, first * pairs + j))
    return pl.pallas_call(
        functools.partial(attend_kernel, starts, chunk),
        grid=(pairs,),
        out_shape=(jax.ShapeDtypeStruct((rows, width), BF16), jax.ShapeDtypeStruct((rows, 128), F32)),
        in_specs=[block(0), block(1), block(2)]
        + [block(0), pl.BlockSpec((rows, 128), lambda j: (0, 0))][: len(done)],
        out_specs=[pl.BlockSpec((rows, 128), lambda j: (0, j)), pl.BlockSpec((rows, 128), lambda j: (0, 0))],
        compiler_params=pltpu.CompilerParams(vmem_limit_bytes=24 * 2**20),
        cost_estimate=BRIEF,
    )(qkv, qkv, qkv, *done)

def terms(value):
    first = value.astype(BF16)
    rest = value - first.astype(F32)
    second = rest.astype(BF16)
    return first, second, (rest - second.astype(F32)).astype(BF16)

def attend_back_kernel(starts, chunk, q_ref, k_ref, v_ref, mixed_ref, grad_ref, total_ref, *refs):
    pair = pl.program_id(0)
    *done, out_ref, left, right, acc = refs
    if done:
        out_ref[:, : starts[0], :] = done[0][:, : starts[0], :]
    scale = HEAD ** -0.5
    zero = jnp.zeros((), BF16)
    for begin, end in zip(starts, starts[1:]):
        size = end - begin
        for offset, part in chunks(size, chunk):
            rows = slice(begin + offset, begin + offset + part)
            lane = lax.broadcasted_iota(jnp.int32, (part, 128), 1)
            queries, grads = q_ref[rows, :] * scale, grad_ref[rows, :]
            product = grads.astype(F32) * mixed_ref[rows, :].astype(F32)
            total_all = total_ref[rows, :]
            for head in range(2):
                own = (lane < HEAD) if head == 0 else (lane >= HEAD)
                free = HEAD * (1 - head)
                inner = jnp.sum(jnp.where(own, product, 0.0), axis=1, keepdims=True)
                total = jnp.sum(jnp.where(lane == 2 * pair + head, total_all, 0.0), axis=1, keepdims=True)
                for target, value, line in ((left, queries, total), (right, grads, inner)):
                    wide = jnp.where(own, value, zero)
                    for i, term in enumerate(terms(line)):
                        wide = jnp.where(lane == free + i, term, wide)
                    target[head, offset:offset + part, :] = wide
        queries, grads = q_ref[begin:end, :], grad_ref[begin:end, :]
        acc[...] = jnp.zeros_like(acc)
        for offset, part in chunks(size, chunk):
            rows = slice(begin + offset, begin + offset + part)
            lane = lax.broadcasted_iota(jnp.int32, (part, 128), 1)
            keys, values = k_ref[rows, :], v_ref[rows, :]
            grad_key, grad_value = [], []
            for head in range(2):
                own = (lane < HEAD) if head == 0 else (lane >= HEAD)
                free = HEAD * (1 - head)
                minus = jnp.where((lane >= free) & (lane < free + 3), -jnp.ones((), BF16), zero)
                scores = outer_t(jnp.where(own, keys, minus), left[head, :size, :])
                probs = jnp.exp(scores)
                grad_scores = outer_t(jnp.where(own, values, minus), right[head, :size, :])
                grad_scores = (probs * grad_scores).astype(BF16)
                grad_value.append(jnp.dot(probs.astype(BF16), grads, preferred_element_type=F32))
                grad_key.append(jnp.dot(grad_scores, queries, preferred_element_type=F32))
                acc[head, :size, :] += lax.dot_general(grad_scores, keys, (((0,), (0,)), ((), ())), preferred_element_type=F32)
            out_ref[1, rows, :] = (jnp.where(lane < HEAD, *grad_key) * scale).astype(BF16)
            out_ref[2, rows, :] = jnp.where(lane < HEAD, *grad_value).astype(BF16)
        lane = lax.broadcasted_iota(jnp.int32, (size, 128), 1)
        out_ref[0, begin:end, :] = (jnp.where(lane < HEAD, acc[0, :size, :], acc[1, :size, :]) * scale).astype(BF16)

def attend_backward(qkv, mixed, totals, grad_mixed, starts, done=(), chunk=400):
    rows, width = mixed.shape
    pairs = width // 128
    longest = max(e - s for s, e in zip(starts, starts[1:]))
    block = lambda first: pl.BlockSpec((rows, 128), lambda j: (0, first * pairs + j))
    return pl.pallas_call(
        functools.partial(attend_back_kernel, starts, chunk),
        grid=(pairs,),
        out_shape=jax.ShapeDtypeStruct((3, rows, width), BF16),
        in_specs=[block(0), block(1), block(2), block(0), block(0), pl.BlockSpec((rows, 128), lambda j: (0, 0))]
        + [pl.BlockSpec((3, rows, 128), lambda j: (0, 0, j))][: len(done)],
        out_specs=pl.BlockSpec((3, rows, 128), lambda j: (0, 0, j)),
        scratch_shapes=[pltpu.VMEM((2, longest, 128), BF16), pltpu.VMEM((2, longest, 128), BF16), pltpu.VMEM((2, longest, 128), F32)],
        compiler_params=pltpu.CompilerParams(vmem_limit_bytes=24 * 2**20),
        cost_estimate=BRIEF,
    )(qkv, qkv, qkv, mixed, grad_mixed, totals, *done)


def slot_table(side, size, c):
    pixel = lax.broadcasted_iota(jnp.int32, (side * side, size), 0)
    column = lax.broadcasted_iota(jnp.int32, (side * side, size), 1)
    row, spot = column // SLOT - c * side, column % SLOT
    table = (row >= 0) & (row < side) & (spot < side) & (pixel == row * side + spot)
    return table.astype(BF16)


def two_terms(value):
    first = value.astype(BF16)
    return first, (value - first.astype(F32)).astype(BF16)


def resize_kernel(starts, inputs, *refs):
    sources, base_ref, pos_ref, vectors = refs[:3], refs[3], refs[4], refs[5 : 5 + inputs]
    low_ref, high_ref, *resizes, sems, out_ref, small = refs[5 + inputs :]
    copies = [
        pltpu.make_async_copy(source, target, sems.at[i])
        for i, (source, target) in enumerate(zip(sources, resizes))
    ]
    for copy in copies:
        copy.start()
    share = base_ref.shape[1]
    base = jnp.concatenate([base_ref[c] for c in range(3)])
    for start, side, resize_ref, copy in zip(starts, SIDES, resizes, copies):
        copy.wait()
        size = up_to(3 * side * SLOT, 128)
        own = sum(outer_t(base, term) for term in two_terms(resize_ref[...])[::-1]).astype(BF16)
        if side == SLOT:
            for c in range(3):
                first = start + c * side * SLOT
                out_ref[:, first : first + side * SLOT] = own[c * share : (c + 1) * share]
        else:
            out_ref[:, start : start + size] = sum(
                dot(own[c * share : (c + 1) * share], slot_table(side, size, c)) for c in range(3)
            ).astype(BF16)
    spots, width = pos_ref.shape[1], out_ref.shape[1] - starts[3]
    rise = vectors[-1].shape[1] // share
    for i, ref in enumerate(vectors):
        rows = [ref[:, k * share : (k + 1) * share] for k in range(ref.shape[1] // share)]
        for k, row in enumerate(rows):
            small[i + k : i + k + 1, :] = row.astype(F32)
    count = len(vectors) - 1 + rise

    def shift(rows, by):
        row = lax.broadcasted_iota(jnp.int32, (rows, width), 0)
        column = lax.broadcasted_iota(jnp.int32, (rows, width), 1)
        return ((row + by == column) & (row < count + 64 * (by == 0))).astype(BF16)

    small[count:, :] = jnp.zeros((16 - count, share), F32)
    out_ref[:, starts[3] :] = (
        dot(pos_ref[...], shift(spots, 0)) + inner_t(small[...].astype(BF16), shift(16, spots))
    ).astype(BF16)
    low_ref[...] = out_ref[:, : low_ref.shape[1]]
    high_ref[...] = out_ref[:, low_ref.shape[1] :]


def resize_all(resizes, base_kernel, posemb, vectors, starts, columns):
    whole = pl.BlockSpec(memory_space=pltpu.VMEM)
    share = base_kernel.shape[1]
    half = jax.ShapeDtypeStruct((share, columns // 2), BF16)
    return pl.pallas_call(
        functools.partial(resize_kernel, starts, len(vectors)),
        out_shape=(half, half),
        in_specs=[pl.BlockSpec(memory_space=pl.ANY)] * 3 + [whole] * (2 + len(vectors)),
        out_specs=(whole, whole),
        scratch_shapes=[pltpu.VMEM(r.shape, F32) for r in resizes]
        + [
            pltpu.SemaphoreType.DMA((3,)),
            pltpu.VMEM((share, columns), BF16),
            pltpu.VMEM((16, share), F32),
        ],
        compiler_params=pltpu.CompilerParams(vmem_limit_bytes=60 * 2**20),
        cost_estimate=BRIEF,
    )(*resizes, base_kernel, posemb, *vectors)


def enter_kernel(embed_pieces, qkv_pieces, starts, bounds, spots, where_ref, *refs):
    patches, map_ref, refs = refs[:3], refs[3], refs[4:]
    embed_parts, refs = refs[: len(embed_pieces)], refs[len(embed_pieces) :]
    qkv_parts, refs = refs[: len(qkv_pieces)], refs[len(qkv_pieces) :]
    embedded, units, qkv, lines_ref, inverse_ref, small_ref = refs[:6]
    normed, table, weight, embed_sems, qkv_sems = refs[6:]
    width = embedded.shape[1]
    embed_copies = place_copies(embed_pieces, embed_parts, table, where_ref, embed_sems)
    qkv_copies = place_copies(qkv_pieces, qkv_parts, weight, where_ref, qkv_sems)
    for copy in embed_copies + qkv_copies:
        copy.start()
    for copy in embed_copies:
        copy.wait()
    smalls = table[:, bounds[3] :]
    small_ref[...] = smalls
    row = lax.broadcasted_iota(jnp.int32, (16, 128), 0)
    lane = lax.broadcasted_iota(jnp.int32, (16, 128), 1)
    lines = outer_t(((lane == row + spots) & (row < 9)).astype(BF16), smalls)
    lines_ref[...] = lines
    for i, patch_ref in enumerate(patches):
        rows = slice(starts[i], starts[i + 1])
        value = outer_t(patch_ref[...], table[:, bounds[i] : bounds[i + 1]])
        for part in reversed(terms(map_ref[rows, :])):
            value = value + outer_t(part, smalls)
        embedded[rows, :] = value
        unit_rows, inverse = unit(value)
        inverse_ref[rows, :] = inverse
        units[rows, :] = unit_rows.astype(BF16)
        normed[rows, :] = (unit_rows * lines[1:2] + lines[2:3]).astype(BF16)
    for copy in qkv_copies:
        copy.wait()
    for i in range(3):
        columns = slice(i * width, (i + 1) * width)
        value = dot(normed[...], weight[:, columns])
        if i != 1:
            value = value + lines[3 + i // 2 : 4 + i // 2]
        qkv[:, columns] = value.astype(BF16)


def enter_all(embed_parts, qkv_parts, patches, maps, starts, bounds, spots):
    whole = pl.BlockSpec(memory_space=pltpu.VMEM)
    anywhere = pl.BlockSpec(memory_space=pl.ANY)
    parts = [*embed_parts.parts, *qkv_parts.parts]
    rows, width = maps.shape[0], 16 * parts[0].shape[1]
    return pl.pallas_call(
        functools.partial(
            enter_kernel, embed_parts.pieces, qkv_parts.pieces, starts, bounds, spots
        ),
        out_shape=(
            jax.ShapeDtypeStruct((rows, width), F32),
            jax.ShapeDtypeStruct((rows, width), BF16),
            jax.ShapeDtypeStruct((rows, 3 * width), BF16),
            jax.ShapeDtypeStruct((16, width), F32),
            jax.ShapeDtypeStruct((rows, 1), F32),
            jax.ShapeDtypeStruct((width, embed_parts.columns - bounds[3]), BF16),
        ),
        in_specs=[pl.BlockSpec(memory_space=pltpu.SMEM)]
        + [whole] * 4
        + [anywhere] * len(parts),
        out_specs=[whole] * 6,
        scratch_shapes=[
            pltpu.VMEM((rows, width), BF16),
            pltpu.VMEM((width, embed_parts.columns), BF16),
            pltpu.VMEM((width, 3 * width), BF16),
            pltpu.SemaphoreType.DMA((copies_of(embed_parts.pieces),)),
            pltpu.SemaphoreType.DMA((copies_of(qkv_parts.pieces),)),
        ],
        compiler_params=pltpu.CompilerParams(vmem_limit_bytes=40 * 2**20),
        cost_estimate=BRIEF,
    )(embed_parts.where, *patches, maps, *parts)


def base_gradient_kernel(starts, *refs):
    resizes, sum_ref, out_ref = refs[:3], refs[3], refs[4]
    share = sum_ref.shape[0]
    total = None
    for start, side, resize_ref in zip(starts, SIDES, resizes):
        size = up_to(3 * side * SLOT, 128)
        given = sum_ref[:, start : start + size]
        if side == SLOT:
            own = [given[:, c * side * SLOT : (c + 1) * side * SLOT] for c in range(3)]
        else:
            own = [outer_t(given, slot_table(side, size, c)).astype(BF16) for c in range(3)]
        own = jnp.concatenate(own)
        for term in two_terms(resize_ref[...])[::-1]:
            value = dot(own, term)
            total = value if total is None else total + value
    for c in range(3):
        out_ref[c] = total[c * share : (c + 1) * share]


def base_gradient(resizes, embed_sum, shape, starts):
    whole = pl.BlockSpec(memory_space=pltpu.VMEM)
    return pl.pallas_call(
        functools.partial(base_gradient_kernel, starts),
        out_shape=jax.ShapeDtypeStruct(shape, F32),
        in_specs=[whole] * 4,
        out_specs=whole,
        compiler_params=pltpu.CompilerParams(vmem_limit_bytes=24 * 2**20),
        cost_estimate=BRIEF,
    )(*resizes, embed_sum)


def gelu_pair(value):
    slope = math.sqrt(2 / math.pi)
    square = value * value
    curve = jnp.tanh(value * (slope + (slope * 0.044715) * square))
    half = 0.5 * value
    rise = 0.5 + 0.5 * curve
    bend = (half - half * (curve * curve)) * (slope + (3 * slope * 0.044715) * square)
    return value * rise, rise + bend


ORDER = (0, 8, 4, 12, 2, 10, 6, 14)


def feed_kernel(starts, chunk, where_ref, *refs):
    mixed_ref, embedded_ref, lines_ref, b_up_ref = refs[:4]
    up_parts, down_parts, cotangents = refs[4:8], refs[8:10], refs[10:13]
    finals = refs[13:16]
    up_keep, up_give, down_keep, down_give, g_bias_ref = refs[16:21]
    branch_ref, g_mixed_ref, sums_ref = refs[21:24]
    middle, normed, grads, act, grad_up, total, back = refs[24:31]
    w_up, w_down, w_out, g_up, g_down, g_out = refs[31:37]
    up_in, down_in, out_in, up_out, down_out, out_out, one, ends = refs[37:]
    step, steps = pl.program_id(0), pl.num_programs(0)
    rows = middle.shape[0]
    me, other = where_ref[0], where_ref[1]
    slot = lax.rem(step, 2)
    tile = w_up.shape[2]
    up_rows, down_rows = up_keep.shape[2], w_down.shape[1] // 4
    count = 16

    def at(index, size):
        return pl.ds(pl.multiple_of(index * size, size), size)

    def load_up(s, half):
        t = lax.bitwise_xor(s, me // 4)
        return [
            pltpu.make_async_copy(
                up_parts[2 * (d % 2) + half].at[ORDER.index(d - d % 2), :, at(lax.rem(t, 2), tile)],
                w_up.at[lax.rem(s, 2), at(lax.bitwise_xor(me, d), up_rows), :],
                up_in.at[lax.rem(s, 2), d],
            )
            for d in range(count)
        ]

    def load_down(s):
        copies = []
        for j in range(4):
            place_ = s // 2 + 2 * lax.rem(s, 2) + 4 * (j // 2)
            copies.append(
                pltpu.make_async_copy(
                    down_parts[j % 2].at[place_, pl.ds(0, down_rows), :],
                    w_down.at[lax.rem(s, 2), at(lax.bitwise_xor(lax.rem(me, 4), j), down_rows), :],
                    down_in.at[lax.rem(s, 2), j],
                )
            )
        return copies

    def load(s):
        t = lax.bitwise_xor(s, me // 4)
        side = lax.bitwise_xor(t // 2, other)
        for half in range(2):

            @pl.when(side == half)
            def _():
                for copy in load_up(s, half):
                    copy.start()

        for copy in load_down(s):
            copy.start()

    def load_out():
        return [
            pltpu.make_async_copy(
                down_parts[d % 2].at[ORDER.index(d - d % 2), pl.ds(down_rows, up_rows), :],
                w_out.at[at(lax.bitwise_xor(me, d), up_rows), :],
                out_in.at[d],
            )
            for d in range(count)
        ]

    def store(s):
        t = lax.bitwise_xor(s, me // 4)
        side = lax.bitwise_xor(t // 2, other)
        copies = []
        for d in range(count):
            copies.append(
                pltpu.make_async_copy(
                    g_up.at[lax.rem(s, 2), at(lax.bitwise_xor(me, d), up_rows), :],
                    (up_keep, up_give)[d % 2].at[side, d // 2, :, at(lax.rem(t, 2), tile)],
                    up_out.at[lax.rem(s, 2), d],
                )
            )
        for j in range(4):
            copies.append(
                pltpu.make_async_copy(
                    g_down.at[lax.rem(s, 2), at(lax.bitwise_xor(lax.rem(me, 4), j), down_rows), :],
                    (down_keep, down_give)[j % 2].at[2 * s + j // 2, pl.ds(0, down_rows), :],
                    down_out.at[lax.rem(s, 2), j],
                )
            )
        return copies

    def store_out():
        return [
            pltpu.make_async_copy(
                g_out.at[at(lax.bitwise_xor(me, d), up_rows), :],
                (down_keep, down_give)[d % 2].at[d // 2, pl.ds(down_rows, up_rows), :],
                out_out.at[d],
            )
            for d in range(count)
        ]

    @pl.when(step == 0)
    def _():
        copy = pltpu.make_async_copy(embedded_ref, middle, one.at[0])
        copy.start()
        for first in load_out():
            first.start()
        load(0)
        for i, ref in enumerate(cotangents):
            grads[starts[i] : starts[i + 1], :] = ref[0]
        copy.wait()
        for first in load_out():
            first.wait()
        for first, size in chunks(rows, 416):
            part = slice(first, first + size)
            value = middle[part, :] + dot(mixed_ref[part, :], w_out[...]) + lines_ref[5:6, :]
            middle[part, :] = value
            unit_rows, _ = unit(value)
            normed[part, :] = (unit_rows * lines_ref[6:7, :] + lines_ref[7:8, :]).astype(BF16)
            total[part, :] = value + lines_ref[8:9, :]
            back[part, :] = jnp.zeros((size, back.shape[1]), F32)

    @pl.when(step + 1 < steps)
    def _():
        load(step + 1)

    for copy in load_up(step, 0) + load_down(step):
        copy.wait()

    column = jnp.zeros((1, tile), F32)
    for first, size in chunks(rows, chunk):
        part = slice(first, first + size)
        up = dot(normed[part, :], w_up[slot]) + b_up_ref[...]
        value, slope = gelu_pair(up)
        value = value.astype(BF16)
        act[part, :] = value
        grad = (slope * outer_t(grads[part, :], w_down[slot])).astype(BF16)
        grad_up[part, :] = grad
        column += jnp.sum(grad.astype(F32), axis=0, keepdims=True)
        total[part, :] += dot(value, w_down[slot])
        back[part, :] += outer_t(grad, w_up[slot])
    g_bias_ref[...] = column

    @pl.when(step >= 2)
    def _():
        for copy in store(step - 2):
            copy.wait()

    g_down[slot] = inner_t(act[...], grads[...]).astype(BF16)
    g_up[slot] = inner_t(normed[...], grad_up[...]).astype(BF16)
    for copy in store(step):
        copy.start()

    @pl.when(step == steps - 1)
    def _():
        done = []

        def leave(source, target):
            done.append(pltpu.make_async_copy(source, target, ends.at[len(done)]))
            done[-1].start()

        for i, ref in enumerate(finals):
            part = pl.ds(starts[i], starts[i + 1] - starts[i])
            act[part, :] = total[part, :].astype(BF16)
            leave(act.at[part, :], ref.at[0])
        width = middle.shape[1]
        sums = [jnp.zeros((1, width), F32)] * 4
        for first, size in chunks(rows, 416):
            part = pl.ds(first, size)
            unit_rows, inverse = unit(middle[part, :])
            out = back[part, :]
            down = grads[part, :].astype(F32)
            grad, gain, bias = norm_backward(out, unit_rows, inverse, lines_ref[6:7, :])
            low = (grad + down).astype(BF16)
            normed[part, :] = low
            leave(normed.at[part, :], branch_ref.at[part, :])
            grad_up[part, :] = outer_t(low, w_out[...]).astype(BF16)
            leave(grad_up.at[part, :], g_mixed_ref.at[part, :])
            found = (
                gain[None],
                bias[None],
                jnp.sum(down, axis=0, keepdims=True),
                jnp.sum(low.astype(F32), axis=0, keepdims=True),
            )
            sums = [a + b for a, b in zip(sums, found)]
        g_out[...] = inner_t(mixed_ref[...], normed[...]).astype(BF16)
        for last in store_out():
            last.start()
        sums_ref[...] = jnp.concatenate(sums + [jnp.zeros((4, width), F32)])
        for last in store_out() + store(step - 1) + store(step) + done:
            last.wait()


def feed_all(where, mixed, embedded, lines, b_up, up_parts, down_parts, cotangents, starts, chunk=624):
    rows, width = mixed.shape
    tile = up_parts[0].shape[2] // 2
    hidden = 4 * tile
    up_rows = up_parts[0].shape[1]
    down_rows = down_parts[0].shape[1]
    fixed = lambda *shape: pl.BlockSpec(
        shape, lambda s, w: (0,) * len(shape), pipeline_mode=pl.Buffered(1)
    )
    whole = lambda *shape: pl.BlockSpec(shape, lambda s, w: (0,) * len(shape))
    mine = pl.BlockSpec((1, tile), lambda s, w: (0, lax.bitwise_xor(s, w[0] // 4)))
    anywhere = pl.BlockSpec(memory_space=pl.ANY)
    like = lambda shape, kind: jax.ShapeDtypeStruct(shape, kind)
    return pl.pallas_call(
        functools.partial(feed_kernel, starts, chunk),
        grid_spec=pltpu.PrefetchScalarGridSpec(
            num_scalar_prefetch=1,
            grid=(4,),
            in_specs=[fixed(rows, width), anywhere, fixed(16, width), mine]
            + [anywhere] * 6
            + [fixed(*c.shape) for c in cotangents],
            out_specs=[anywhere] * 7 + [mine, anywhere, anywhere, whole(8, width)],
            scratch_shapes=[
                pltpu.VMEM((rows, width), F32),
                pltpu.VMEM((rows, width), BF16),
                pltpu.VMEM((rows, width), BF16),
                pltpu.VMEM((rows, tile), BF16),
                pltpu.VMEM((rows, tile), BF16),
                pltpu.VMEM((rows, width), F32),
                pltpu.VMEM((rows, width), F32),
                pltpu.VMEM((2, width, tile), BF16),
                pltpu.VMEM((2, tile, width), BF16),
                pltpu.VMEM((width, width), BF16),
                pltpu.VMEM((2, width, tile), BF16),
                pltpu.VMEM((2, tile, width), BF16),
                pltpu.VMEM((width, width), BF16),
                pltpu.SemaphoreType.DMA((2, 16)),
                pltpu.SemaphoreType.DMA((2, 4)),
                pltpu.SemaphoreType.DMA((16,)),
                pltpu.SemaphoreType.DMA((2, 16)),
                pltpu.SemaphoreType.DMA((2, 4)),
                pltpu.SemaphoreType.DMA((16,)),
                pltpu.SemaphoreType.DMA((1,)),
                pltpu.SemaphoreType.DMA((3 + 2 * len(chunks(rows, 416)),)),
            ],
        ),
        out_shape=[like(c.shape, BF16) for c in cotangents]
        + [like((2, 8, up_rows, hidden // 2), BF16)] * 2
        + [like((8, down_rows, width), BF16)] * 2
        + [
            like((1, hidden), F32),
            like((rows, width), BF16),
            like((rows, width), BF16),
            like((8, width), F32),
        ],
        compiler_params=pltpu.CompilerParams(vmem_limit_bytes=56 * 2**20),
        cost_estimate=BRIEF,
    )(where, mixed, embedded, lines, b_up, *up_parts, *down_parts, *cotangents)


def spread_copies(source, segments, where_ref, sems, first=0):
    me, other = where_ref[0], where_ref[1]
    copies = []
    for start, columns, targets, half, there in segments:
        for d in range(16):
            rows = source.shape[0] // 16
            row = pl.ds(pl.multiple_of(lax.bitwise_xor(me, d) * rows, rows), rows)
            target = targets[d % 2]
            if half is not None:
                target = target.at[lax.bitwise_xor(other, half)]
            copies.append(
                pltpu.make_async_copy(
                    source.at[row, pl.ds(start, columns)],
                    target.at[d // 2, :, pl.ds(there, columns)],
                    sems.at[first + len(copies)],
                )
            )
    return copies


def leave_kernel(pieces, starts, bounds, spots, low_columns, chunk, where_ref, *refs):
    grads, units, branch, lines_ref, given_ref, bias_ref, inverse_ref, map_ref = refs[:8]
    patches, parts, refs = refs[8:11], refs[11 : 11 + len(pieces)], refs[11 + len(pieces) :]
    low_ref, low_outs, high_outs, refs = refs[0], refs[1:3], refs[3:5], refs[5:]
    normed, weight, embed_out, qkv_out, sums, weight_sems, out_sems = refs
    rows, width = low_ref.shape
    weights = place_copies(pieces, parts, weight, where_ref, weight_sems)
    half = embed_out.shape[1] // 2
    quarter = half // 2
    low = low_columns - half
    rest = (3 * width - low) // 2
    segments = [
        (qkv_out, (0, low, low_outs, None, half)),
        (qkv_out, (low, rest, high_outs, 0, quarter)),
        (qkv_out, (low + rest, rest, high_outs, 1, quarter)),
        (embed_out, (0, half, low_outs, None, 0)),
        (embed_out, (half, quarter, high_outs, 0, 0)),
        (embed_out, (half + quarter, quarter, high_outs, 1, 0)),
    ]
    copies = []
    for source, segment in segments:
        copies += spread_copies(source, [segment], where_ref, out_sems, len(copies))
    for copy in weights:
        copy.start()
    normed[...] = (units[...].astype(F32) * lines_ref[1:2, :] + lines_ref[2:3, :]).astype(BF16)
    for i in range(3):
        columns = slice(i * width, (i + 1) * width)
        qkv_out[:, columns] = inner_t(normed[...], grads[i]).astype(BF16)
        for copy in copies[16 * i - 16 : 16 * i] if i < 2 else copies[16:48]:
            copy.start()
    sums[...] = jnp.zeros_like(sums)
    sums[5:6, :] = given_ref[3:4, :]
    sums[6:9, :] = given_ref[:3, :]
    for copy in weights:
        copy.wait()
    totals = [jnp.zeros((1, width), F32)] * 4
    for first, size in chunks(rows, chunk):
        part = slice(first, first + size)
        found = sum(
            outer_t(grads[i, part, :], weight[:, i * width : (i + 1) * width]) for i in range(3)
        )
        grad, gain, bias = norm_backward(
            found, units[part, :].astype(F32), inverse_ref[part, :], lines_ref[1:2, :]
        )
        low_ref[part, :] = (grad + branch[part, :].astype(F32)).astype(BF16)
        found = [gain[None], bias[None]] + [
            jnp.sum(grads[i, part, :].astype(F32), axis=0, keepdims=True) for i in (0, 2)
        ]
        totals = [a + b for a, b in zip(totals, found)]
    for i, value in enumerate(totals):
        sums[i + 1 : i + 2, :] = value
    row = lax.broadcasted_iota(jnp.int32, (16, 128), 0)
    lane = lax.broadcasted_iota(jnp.int32, (16, 128), 1)
    smalls = inner_t(sums[...].astype(BF16), ((lane == row + spots) & (row < 9)).astype(BF16))
    rise = bias_ref.shape[1]
    smalls += dot(bias_ref[...], ((lane == row + spots + 9)[:rise]).astype(BF16))
    started = 48
    for i, patch_ref in enumerate(patches):
        part = slice(starts[i], starts[i + 1])
        size = bounds[i + 1] - bounds[i]
        above, below = two_terms(map_ref[part, :])
        found = inner_t(low_ref[part, :], jnp.concatenate([patch_ref[...], above, below], axis=1))
        embed_out[:, bounds[i] : bounds[i + 1]] = found[:, :size].astype(BF16)
        smalls += found[:, size : size + 128] + found[:, size + 128 :]
        if bounds[i + 1] >= half and started == 48:
            started = 64
            for copy in copies[48:64]:
                copy.start()
    embed_out[:, bounds[3] :] = smalls.astype(BF16)
    for copy in copies[started:]:
        copy.start()
    for copy in copies:
        copy.wait()


def leave_all(
    qkv_parts,
    grad_qkv,
    units,
    branch,
    lines,
    given,
    bias,
    inverse,
    maps,
    patches,
    starts,
    bounds,
    spots,
    low_columns,
    chunk=416,
):
    _, rows, width = grad_qkv.shape
    whole = pl.BlockSpec(memory_space=pltpu.VMEM)
    anywhere = pl.BlockSpec(memory_space=pl.ANY)
    parts = qkv_parts.parts
    columns = bounds[3] + 128
    block = width // 16
    high_columns = (3 * width + columns - low_columns) // 2
    return pl.pallas_call(
        functools.partial(
            leave_kernel, qkv_parts.pieces, starts, bounds, spots, low_columns, chunk
        ),
        out_shape=[jax.ShapeDtypeStruct((rows, width), BF16)]
        + [jax.ShapeDtypeStruct((8, block, low_columns), BF16)] * 2
        + [jax.ShapeDtypeStruct((2, 8, block, high_columns), BF16)] * 2,
        in_specs=[pl.BlockSpec(memory_space=pltpu.SMEM)]
        + [whole] * 11
        + [anywhere] * len(parts),
        out_specs=[whole] + [anywhere] * 4,
        scratch_shapes=[
            pltpu.VMEM((rows, width), BF16),
            pltpu.VMEM((width, 3 * width), BF16),
            pltpu.VMEM((width, columns), BF16),
            pltpu.VMEM((width, 3 * width), BF16),
            pltpu.VMEM((16, width), F32),
            pltpu.SemaphoreType.DMA((copies_of(qkv_parts.pieces),)),
            pltpu.SemaphoreType.DMA((96,)),
        ],
        compiler_params=pltpu.CompilerParams(vmem_limit_bytes=44 * 2**20),
        cost_estimate=BRIEF,
    )(
        qkv_parts.where,
        grad_qkv,
        units,
        branch,
        lines,
        given,
        bias,
        inverse,
        maps,
        *patches,
        *parts,
    )


def dot(first, second):
    return jnp.dot(first, second, preferred_element_type=F32)


def inner_t(first, second):
    return lax.dot_general(first, second, (((0,), (0,)), ((), ())), preferred_element_type=F32)


def body(count, pixels, resizes, posmaps, weights, cotangents):
    base_kernel, patch_bias, posemb = weights[:3]
    ln1_gain, ln1_bias, qkv_weight, qv_bias, out_weight, out_bias = weights[3:9]
    ln2_gain, ln2_bias, up_weight, up_bias, down_weight, down_bias = weights[9:]
    channels, base_pixels, share = base_kernel.shape
    width = share * count
    spots = posemb.shape[0]
    where = jnp.stack([lax.axis_index("fsdp"), lax.axis_index("rep")]).astype(jnp.int32)
    tokens = [c.shape[1] for c in cotangents]
    starts = [sum(tokens[:i]) for i in range(4)]
    bits = [2**i for i in range(1, count.bit_length() - 1)]
    inward = [(bit,) for bit in bits]
    outward = inward[::-1]
    turned = inward[:1] + outward[:-1]
    short = inward[:-2] + [(bits[-2], bits[-1], bits[-2] + bits[-1])]

    up_per = up_bias.shape[0] // share
    used = spots + 9 + up_per
    bounds = [0]
    for side in SIDES:
        bounds.append(bounds[-1] + up_to(3 * side * SLOT, 128))
    columns = bounds[3] + 128
    vectors = [
        v.reshape(1, -1)
        for v in (
            patch_bias,
            ln1_gain,
            ln1_bias,
            qv_bias[0],
            qv_bias[1],
            out_bias,
            ln2_gain,
            ln2_bias,
            down_bias,
            up_bias,
        )
    ]
    maps = jnp.concatenate(posmaps)
    maps = jnp.concatenate(
        [maps, jnp.ones((maps.shape[0], 1), F32), jnp.zeros((maps.shape[0], 127 - spots), F32)],
        axis=1,
    )

    base_turned = base_kernel.swapaxes(1, 2)
    down_rows = (down_weight.shape[0], out_weight.shape[0])
    down_block = jnp.concatenate([down_weight, out_weight])
    qkv_shards = Gather(qkv_weight, where, count, outward, split=True).send()
    up_shards = Gather(up_weight, where, count, outward, split=True).send()
    shards = resize_all(resizes, base_turned, posemb.T, vectors, bounds, columns)
    embed_low = Gather(shards[0], where, count, outward).send()
    embed_high = Gather(shards[1], where, count, outward).send()
    held = go_on((pixels, maps, *shards), qkv_shards, embed_low, qkv_shards, embed_high, up_shards)
    pixels, maps, *_ = go_on(held, embed_low, qkv_shards)
    patches = patch_all(pixels)
    patches = finish(patches, embed_high, up_shards)
    embed_high.send()
    patches, down_block = after(patches, down_block)
    down_shards = Gather(down_block, where, count, outward).send()
    patches = go_on(patches, embed_low, qkv_shards, embed_high, down_shards)
    up_shards.send()
    patches, maps = complete((patches, maps), embed_low, qkv_shards, embed_high)
    w_qkv = Parts([qkv_shards], where, count)
    w_embed = Parts([embed_low, embed_high], where, count)
    embedded, units, qkv, lines, inverse, columns_small = enter_all(
        w_embed, w_qkv, patches, maps, starts, bounds, spots
    )
    qkv = together(qkv, up_shards, down_shards)
    mixed, totals = attend_forward(qkv, starts)
    mixed = together(mixed, up_shards, down_shards)
    mixed = complete(mixed, up_shards, down_shards)
    w_up = Parts([up_shards], where, count)
    w_down = Parts([down_shards], where, count, down_rows)
    b_up = columns_small[:, spots + 9 : used].astype(F32)
    b_up = b_up.reshape(count, share, up_per).swapaxes(1, 2).reshape(1, -1)
    (
        *results,
        up_keep,
        up_give,
        down_keep,
        down_give,
        grad_b_up,
        branch,
        grad_mixed,
        sums,
    ) = feed_all(
        w_up.where, mixed, embedded, lines, b_up, w_up.pairs(2), w_down.pairs(1), cotangents, starts
    )
    rows16 = (down_rows[0] * count // 16, down_rows[1] * count // 16)
    down_sums = Scatter(
        *ordered(down_keep, down_give, where, count, rows16), where, count, inward
    ).send()
    up_sums = Scatter(
        *ordered(up_keep, up_give, where, count, split=True), where, count, inward, split=True
    ).send()
    grad_qkv = attend_backward(qkv, mixed, totals, grad_mixed, starts[:3])
    grad_qkv = together(grad_qkv, down_sums, up_sums)
    grad_qkv = attend_backward(qkv, mixed, totals, grad_mixed, starts[2:], (grad_qkv,))
    grad_qkv = together(grad_qkv, down_sums, up_sums)
    half = columns // 2
    low_columns = half + 5 * width // 3
    grad_low, *shares = leave_all(
        w_qkv,
        grad_qkv,
        units,
        branch,
        lines,
        sums,
        grad_b_up.reshape(width, up_per).astype(BF16),
        inverse,
        maps,
        patches,
        starts,
        bounds,
        spots,
        low_columns,
    )
    grad_low, *shares = together((grad_low, *shares), down_sums, up_sums)
    low_sums = Scatter(*ordered(*shares[:2], where, count), where, count, short).send()
    high_sums = Scatter(
        *ordered(*shares[2:], where, count, split=True), where, count, short, split=True
    ).send()
    grad_low = go_on(grad_low, low_sums, high_sums)
    pixel_grads = unpatch_all(grad_low, w_embed, starts, bounds, [p.shape[2] for p in pixels])
    pixel_grads = complete(pixel_grads, low_sums, high_sums, down_sums, up_sums)

    low, high = low_sums.result, high_sums.result
    quarter = half // 2
    embed_sum = jnp.concatenate([low[:, :half]] + [h[:, :quarter] for h in high], axis=1)
    qkv_sum = jnp.concatenate([low[:, half:]] + [h[:, quarter:] for h in high], axis=1).astype(F32)
    down_sum = down_sums.result.astype(F32)
    up_sum = jnp.concatenate(up_sums.result, axis=1).astype(F32)
    base_grad = base_gradient(resizes, embed_sum, base_turned.shape, bounds).swapaxes(1, 2)
    small_sum = embed_sum[:, bounds[3] : bounds[3] + used].astype(F32)
    vectors = small_sum[:, spots : spots + 9].T
    return (
        *results,
        *pixel_grads,
        base_grad,
        vectors[0],
        small_sum[:, :spots].T,
        vectors[1],
        vectors[2],
        qkv_sum,
        vectors[3:5],
        down_sum[down_rows[0] :],
        vectors[5],
        vectors[6],
        vectors[7],
        up_sum,
        small_sum[:, spots + 9 :].reshape(-1),
        down_sum[: down_rows[0]],
        vectors[8],
    )


def solution(mesh):
    count = mesh.shape["fsdp"]

    def run(*args):
        return body(count, args[:3], args[3:6], args[6:9], args[9:24], args[24:])

    images = ("rep", "fsdp")
    weight_specs = (
        P(None, None, "fsdp"),
        P("fsdp"),
        P(None, "fsdp"),
        P("fsdp"),
        P("fsdp"),
        P("fsdp", None),
        P(None, "fsdp"),
        P("fsdp", None),
        P("fsdp"),
        P("fsdp"),
        P("fsdp"),
        P("fsdp", None),
        P("fsdp"),
        P("fsdp", None),
        P("fsdp"),
    )
    return jax.shard_map(
        run,
        mesh=mesh,
        in_specs=(P(images, None, None, None),) * 3
        + (P(),) * 6
        + weight_specs
        + (P(images, None, None),) * 3,
        out_specs=(P(images, None, None),) * 3
        + (P(images, None, None, None),) * 3
        + weight_specs,
        check_vma=False,
    )
```

```python
import functools
import math

import jax
import jax.numpy as jnp
from jax import lax
from jax.experimental import pallas as pl
from jax.experimental.pallas import tpu as pltpu
from jax.sharding import PartitionSpec as P

HEADS = 12
HEAD = 64
SIDES = (10, 12, 16)
SLOT = 16
F32 = jnp.float32
BF16 = jnp.bfloat16
BRIEF = pl.CostEstimate(flops=1, bytes_accessed=1, transcendentals=0)


def swap(value, axis, size, bit):
    return lax.ppermute(value, axis, [(i, i ^ bit) for i in range(size)])


def after(first, *rest):
    return lax.optimization_barrier((first, *rest))


class Gather:
    def __init__(self, shard, where, count, steps, split=False, joined=True):
        self.count, self.split, self.columns, self.joined = count, split, shard.shape[1], joined
        if split:
            width = shard.shape[1] // 2
            shard = lax.dynamic_slice_in_dim(shard, where[1] * width, width, 1)
        self.held = [(shard[None], [0])]
        self.steps = list(steps) + (["rep"] if split else []) + ["core"]
        self.step = None
        self.pieces = []
        self.ready = [shard[None]]

    def prepare(self):
        if not self.steps:
            self.ready = []
            return
        last = self.steps[0] in ("rep", "core")
        if len(self.held) > 1 and len(self.held[0]) == 2 and (self.joined or not last):
            offsets = [o for _, offsets in self.held for o in offsets]
            self.held = [(join([blocks for blocks, _ in self.held]), offsets)]
        self.ready = [blocks for blocks, *_ in self.held]

    def renew(self, ready):
        if ready:
            self.held = [(blocks, *h[1:]) for blocks, h in zip(ready, self.held)]
        self.ready = ready

    def send(self):
        self.step, self.steps = self.steps[0], self.steps[1:]
        if self.step in ("rep", "core"):
            axis, size = ("rep", 2) if self.step == "rep" else ("fsdp", self.count)
            self.sent = [swap(blocks, axis, size, 1) for blocks in self.ready]
        else:
            self.sent = [swap(self.ready[0], "fsdp", self.count, offset) for offset in self.step]
        return self

    def take(self, arrived):
        if self.step == "rep":
            self.held = [(*h, 0) for h in self.held] + [
                (blocks, h[1], 1) for blocks, h in zip(arrived, self.held)
            ]
        elif self.step == "core":
            held = [h if len(h) == 3 else (*h, None) for h in self.held]
            self.held = held + [
                (blocks, [o ^ 1 for o in h[1]], h[2]) for blocks, h in zip(arrived, held)
            ]
        else:
            offsets = self.held[0][1]
            self.held = self.held + [
                (blocks, [o ^ offset for o in offsets])
                for blocks, offset in zip(arrived, self.step)
            ]


def finish(anchor, *chains):
    sizes = [len(chain.sent) for chain in chains]
    anchor, *flat = after(anchor, *[part for chain in chains for part in chain.sent])
    for chain, size in zip(chains, sizes):
        chain.take(flat[:size])
        chain.prepare()
        flat = flat[size:]
        chain.sent = []
    sizes = [len(chain.ready) for chain in chains]
    anchor, *flat = after(anchor, *[part for chain in chains for part in chain.ready])
    for chain, size in zip(chains, sizes):
        chain.renew(flat[:size])
        flat = flat[size:]
    return anchor


def together(anchor, *chains):
    anchor = finish(anchor, *chains)
    for chain in chains:
        if chain.steps:
            chain.send()
    return anchor


def go_on(anchor, *chains):
    for chain in chains:
        anchor = together(anchor, chain)
    return anchor


def complete(anchor, *chains):
    chains = [chain for chain in chains if chain.sent]
    while chains:
        left = [chain for chain in chains if chain.steps]
        anchor = go_on(anchor, *chains)
        chains = left
    return anchor


def place_copies(pieces, parts, whole, where_ref, sems):
    me, other = where_ref[0], where_ref[1]
    copies = []
    for part, (offsets, half, first, columns) in zip(parts, pieces):
        rows = part.shape[1]
        for k, offset in enumerate(offsets):
            row = pl.ds(pl.multiple_of(lax.bitwise_xor(me, offset) * rows, rows), rows)
            if half is None:
                target = whole.at[row, pl.ds(first, columns)]
            else:
                width = columns // 2
                start = pl.multiple_of(first + lax.bitwise_xor(other, half) * width, 128)
                target = whole.at[row, pl.ds(start, width)]
            copies.append(pltpu.make_async_copy(part.at[k], target, sems.at[len(copies)]))
    return copies


def copies_of(pieces):
    return sum(len(offsets) for offsets, *_ in pieces)


def place_kernel(pieces, me_ref, *refs):
    parts, whole, sems = refs[: len(pieces)], refs[len(pieces)], refs[len(pieces) + 1]
    me, other = me_ref[0], me_ref[1]
    copies = []
    for part, (offsets, half, first, columns) in zip(parts, pieces):
        for k, offset in enumerate(offsets):
            row = lax.bitwise_xor(me, offset)
            if half is None:
                target = whole.at[row, :, pl.ds(first, columns)]
            else:
                width = columns // 2
                start = pl.multiple_of(first + lax.bitwise_xor(other, half) * width, 128)
                target = whole.at[row, :, pl.ds(start, width)]
            copies.append(pltpu.make_async_copy(part.at[k], target, sems.at[len(copies)]))
    for copy in copies:
        copy.start()
    for copy in copies:
        copy.wait()


def place(gathers, where, count):
    parts, pieces = parts_of(gathers)
    rows, kind = parts[0].shape[1], parts[0].dtype
    columns = sum(g.columns for g in gathers)
    whole = pl.pallas_call(
        functools.partial(place_kernel, pieces),
        out_shape=jax.ShapeDtypeStruct((count, rows, columns), kind),
        in_specs=[pl.BlockSpec(memory_space=pltpu.SMEM)]
        + [pl.BlockSpec(memory_space=pl.ANY)] * len(pieces),
        out_specs=pl.BlockSpec(memory_space=pltpu.VMEM),
        scratch_shapes=[pltpu.SemaphoreType.DMA((copies_of(pieces),))],
        compiler_params=pltpu.CompilerParams(vmem_limit_bytes=16 * 2**20),
        cost_estimate=BRIEF,
    )(where, *parts)
    return whole.reshape(count * rows, columns)


def parts_of(gathers):
    parts, pieces, first = [], [], 0
    for g in gathers:
        for blocks, offsets, half in g.held:
            parts.append(blocks)
            pieces.append((tuple(offsets), half, first, g.columns))
        first += g.columns
    return parts, pieces


def regroup(blocks, rows, count):
    parts, first = [], 0
    for size in rows:
        part = blocks[:, first : first + size]
        parts.append(part.reshape(count, -1, blocks.shape[2]))
        first += size
    return jnp.concatenate(parts, axis=1)


class Parts:
    def __init__(self, gathers, where, count, rows=None):
        self.columns = sum(g.columns for g in gathers)
        self.where = where
        if count == 16:
            self.parts, self.pieces = parts_of(gathers)
        else:
            whole = place(gathers, where, count).reshape(count, -1, self.columns)
            rows = rows or (whole.shape[1],)
            self.parts = [regroup(whole, rows, 16)]
            self.pieces = [(tuple(range(16)), None, 0, self.columns)]
            self.where = jnp.zeros_like(where)

    def quarters(self, halves):
        if len(self.parts) > 1:
            assert len(self.parts) == 4 * halves
            assert self.pieces[0][0] + self.pieces[1][0] == ORDER
            return self.parts
        size = self.columns // halves
        return [
            jnp.stack([self.parts[0][o + core, :, h * size : (h + 1) * size] for o in quarter])
            for core in range(2)
            for h in range(halves)
            for quarter in (ORDER[:4], ORDER[4:])
        ]


def ordered(keep, give, where, count, rows=None, split=False):
    if count == 16:
        return keep, give
    if not split:
        keep, give = keep[None], give[None]
    whole = jnp.stack([keep, give], axis=2)
    halves, blocks, _, size, columns = whole.shape
    whole = whole.reshape(halves, 2 * blocks, size, columns)
    whole = jnp.concatenate([whole[h] for h in range(halves)], axis=2)
    columns = whole.shape[2]
    whole = regroup(whole, rows or (size,), count).reshape(-1, columns)
    found = take([whole], [(0, 0, columns)], where, count, split)
    if split:
        return jnp.stack(found[:2]), jnp.stack(found[2:])
    return found


def take_kernel(count, split, segments, me_ref, *refs):
    inputs = max(which for which, *_ in segments) + 1
    wholes, outs, sems = refs[:inputs], refs[inputs:-1], refs[-1]
    me, other = me_ref[0], me_ref[1]
    half = outs[0].shape[2]

    def copies(switch):
        found = []
        for which, start, columns, first in segments:
            for d in range(count):
                source = wholes[which].at[lax.bitwise_xor(me, d), :, pl.ds(start, columns)]
                side = (first // half) ^ switch
                target = outs[2 * (d % 2) + side] if split else outs[d % 2]
                target = target.at[d // 2, :, pl.ds(first % half, columns)]
                found.append(pltpu.make_async_copy(source, target, sems.at[len(found)]))
        return found

    def run(switch):
        found = copies(switch)
        for copy in found:
            copy.start()
        for copy in found:
            copy.wait()

    if split:
        for switch in range(2):
            pl.when(other == switch)(functools.partial(run, switch))
    else:
        run(0)


def take(wholes, segments, where, count, split):
    rows = wholes[0].shape[0] // count
    blocks = [w.reshape(count, rows, w.shape[1]) for w in wholes]
    columns = sum(segment[2] for segment in segments)
    half = columns // 2 if split else columns
    ends, first = [], 0
    for which, start, size in segments:
        while size:
            room = min(size, half - first % half)
            ends.append((which, start, room, first))
            first, start, size = first + room, start + room, size - room
    shape = jax.ShapeDtypeStruct((count // 2, rows, half), wholes[0].dtype)
    outs = 4 if split else 2
    return pl.pallas_call(
        functools.partial(take_kernel, count, split, ends),
        out_shape=(shape,) * outs,
        in_specs=[pl.BlockSpec(memory_space=pltpu.SMEM)]
        + [pl.BlockSpec(memory_space=pltpu.VMEM)] * len(blocks),
        out_specs=[pl.BlockSpec(memory_space=pl.ANY)] * outs,
        scratch_shapes=[pltpu.SemaphoreType.DMA((count * len(ends),))],
        compiler_params=pltpu.CompilerParams(vmem_limit_bytes=16 * 2**20),
        cost_estimate=BRIEF,
    )(where, *blocks)


def add(*values):
    return sum(value.astype(F32) for value in values).astype(BF16)


def join_kernel(*refs):
    *parts, whole = refs
    first = 0
    for part in parts:
        whole[first : first + part.shape[0]] = part[...]
        first += part.shape[0]


def join(parts):
    blocks = sum(part.shape[0] for part in parts)
    whole = pl.BlockSpec(memory_space=pltpu.VMEM)
    return pl.pallas_call(
        join_kernel,
        out_shape=jax.ShapeDtypeStruct((blocks, *parts[0].shape[1:]), parts[0].dtype),
        in_specs=[whole] * len(parts),
        out_specs=whole,
        compiler_params=pltpu.CompilerParams(vmem_limit_bytes=16 * 2**20),
        cost_estimate=BRIEF,
    )(*parts)


def merge_kernel(groups, parts, *refs):
    outs = refs[parts:]
    for group, out in zip(groups, outs):
        for j, index in enumerate(group):
            out[j] = sum(ref[index].astype(F32) for ref in refs[:parts]).astype(BF16)


def merge(parts, groups):
    rest = parts[0].shape[-2:]
    whole = pl.BlockSpec(memory_space=pltpu.VMEM)
    return pl.pallas_call(
        functools.partial(merge_kernel, groups, len(parts)),
        out_shape=[jax.ShapeDtypeStruct((len(group), *rest), BF16) for group in groups],
        in_specs=[whole] * len(parts),
        out_specs=[whole] * len(groups),
        compiler_params=pltpu.CompilerParams(vmem_limit_bytes=24 * 2**20),
        cost_estimate=BRIEF,
    )(*parts)


class Scatter:
    def __init__(self, keep, give, where, count, steps, split=False):
        self.where, self.count, self.split = where, count, split
        self.keep, self.give = keep, give
        self.steps = ["core"] + (["half"] if split else []) + list(steps) + ["rep"]
        self.offsets = list(range(0, count, 2))
        self.step = None

        self.ready = [give]

    def prepare(self):
        pass

    def renew(self, ready):
        self.ready = ready

    def send(self):
        self.step, self.steps = self.steps[0], self.steps[1:]
        if self.step in ("half", "rep"):
            self.sent = [swap(self.ready[0], "rep", 2, 1)]
        else:
            offsets = [1] if self.step == "core" else self.step
            self.sent = [
                swap(part, "fsdp", self.count, offset)
                for part, offset in zip(self.ready, offsets)
            ]
        return self

    def share_out(self, parts):
        step = self.steps[0]
        if step == "rep":
            self.held = merge(parts, [[0]])[0][0]
            self.ready = [self.held]
            return
        mask = 0
        for offset in step:
            mask |= offset
        stay = [o for o in self.offsets if o & mask == 0]
        groups = [[self.offsets.index(o | offset) for o in stay] for offset in (0, *step)]
        self.staying, *self.ready = merge(parts, groups)
        self.offsets = stay

    def take(self, arrived):
        if self.step == "core" and self.split:
            blocks = len(self.offsets)
            flat = [a.reshape(2 * blocks, *a.shape[2:]) for a in (self.keep, *arrived)]
            away, self.staying = merge(
                flat, [list(range(blocks, 2 * blocks)), list(range(blocks))]
            )
            self.ready = [away]
        elif self.step == "core":
            self.share_out([self.keep, *arrived])
        elif self.step == "rep":
            if self.split:
                low = self.where[1] == 0
                self.result = [
                    jnp.where(low, self.held, arrived[0]),
                    jnp.where(low, arrived[0], self.held),
                ]
            else:
                self.result = add(self.held, arrived[0])
            self.ready = []
        else:
            self.share_out([self.staying, *arrived])


def up_to(value, unit):
    return -(-value // unit) * unit

def swap_chunks(lines):
    chunk = lax.broadcasted_iota(jnp.int32, lines[0].shape, 1) // SLOT
    for step in (1, 2, 4):
        stays = (chunk & step) == 0
        for i in range(8):
            if i & step == 0:
                low, high = lines[i], lines[i + step]
                lines[i] = jnp.where(stays, low, pltpu.roll(high, step * SLOT, 1))
                lines[i + step] = jnp.where(stays, pltpu.roll(low, 128 - step * SLOT, 1), high)
    return lines

def spread(side, grid, columns):
    pixel = lax.broadcasted_iota(jnp.int32, (grid * side, columns), 0)
    column = lax.broadcasted_iota(jnp.int32, (grid * side, columns), 1)
    place = column % SLOT
    return ((pixel == column // SLOT * side + place) & (place < side)).astype(BF16)

def patch_kernel(*refs):
    pixels, outs, rows_ref, flat_ref = refs[:3], refs[3:6], refs[6], refs[7]
    for side, pixel_ref, out in zip(SIDES, pixels, outs):
        high = pixel_ref.shape[2]
        grid = high // side
        columns = up_to(grid * SLOT, 128)
        table = None if side == SLOT else spread(side, grid, columns)
        for c in range(3):
            picture = pixel_ref[0, c]
            if table is None:
                wide = picture.astype(F32)
            else:
                wide = jnp.dot(picture, table, preferred_element_type=F32)
            for block in range(columns // 128):
                rows_ref[3 * c + block, :high, :] = wide[:, 128 * block:128 * block + 128]
        slots = 3 * side
        for group in range(out.shape[1] // 128):
            for block in range(columns // 128):
                lines = []
                for q in range(8 * group, 8 * group + 8):
                    if q < slots:
                        lines.append(rows_ref[q // side * 3 + block, pl.ds(q % side, grid, stride=side), :])
                    else:
                        lines.append(jnp.zeros((grid, 128), F32))
                lines = swap_chunks(lines)
                for g in range(8):
                    if 8 * block + g < grid:
                        flat_ref[group, pl.ds(8 * block + g, grid, stride=grid), :] = lines[g]
        for group in range(out.shape[1] // 128):
            out[:, 128 * group:128 * group + 128] = flat_ref[group, :grid * grid, :].astype(BF16)

def patch_all(pixels):
    shapes = []
    for picture, side in zip(pixels, SIDES):
        grid = picture.shape[2] // side
        shapes.append(jax.ShapeDtypeStruct((grid * grid, up_to(3 * side * SLOT, 128)), BF16))
    high = max(p.shape[2] for p in pixels)
    return pl.pallas_call(
        patch_kernel,
        out_shape=shapes,
        in_specs=[pl.BlockSpec(memory_space=pltpu.VMEM)] * 3,
        out_specs=[pl.BlockSpec(memory_space=pltpu.VMEM)] * 3,
        scratch_shapes=[pltpu.VMEM((9, high, 128), F32), pltpu.VMEM((max(s.shape[1] for s in shapes) // 128, max(s.shape[0] for s in shapes), 128), F32)],
        compiler_params=pltpu.CompilerParams(vmem_limit_bytes=40 * 2**20),
        cost_estimate=BRIEF,
    )(*pixels)

def unpatch_kernel(pieces, starts, bounds, where_ref, grad_ref, *refs):
    parts, refs = refs[: len(pieces)], refs[len(pieces) :]
    outs, flat_ref, rows_ref, kernel_ref, sems = refs[:3], *refs[3:]
    copies = place_copies(pieces, parts, kernel_ref, where_ref, sems)
    for copy in copies:
        copy.start()
    for copy in copies:
        copy.wait()
    for i, side in enumerate(SIDES):
        out = outs[i]
        high = out.shape[2]
        grid = high // side
        columns = up_to(grid * SLOT, 128)
        width = bounds[i + 1] - bounds[i]
        grads = grad_ref[starts[i]:starts[i + 1], :]
        flat = jnp.dot(grads, kernel_ref[:, bounds[i]:bounds[i + 1]], preferred_element_type=F32)
        for group in range(width // 128):
            flat_ref[group, :grid * grid, :] = flat[:, 128 * group:128 * group + 128]
        slots = 3 * side
        for group in range(width // 128):
            for block in range(columns // 128):
                lines = []
                for g in range(8):
                    if 8 * block + g < grid:
                        lines.append(flat_ref[group, pl.ds(8 * block + g, grid, stride=grid), :])
                    else:
                        lines.append(jnp.zeros((grid, 128), F32))
                lines = swap_chunks(lines)
                for q in range(8 * group, min(8 * group + 8, slots)):
                    rows_ref[q // side * 3 + block, pl.ds(q % side, grid, stride=side), :] = lines[q % 8]
        table = None if side == SLOT else spread(side, grid, columns)
        for c in range(3):
            picture = jnp.concatenate([rows_ref[3 * c + block, :high, :] for block in range(columns // 128)], axis=1).astype(BF16)
            if table is not None:
                picture = lax.dot_general(picture, table, (((1,), (1,)), ((), ())), preferred_element_type=F32).astype(BF16)
            out[0, c] = picture

def unpatch_all(grads, embed_parts, starts, bounds, sides):
    high = max(sides)
    whole = pl.BlockSpec(memory_space=pltpu.VMEM)
    parts = embed_parts.parts
    return pl.pallas_call(
        functools.partial(unpatch_kernel, embed_parts.pieces, starts, bounds),
        out_shape=[jax.ShapeDtypeStruct((1, 3, s, s), BF16) for s in sides],
        in_specs=[pl.BlockSpec(memory_space=pltpu.SMEM), whole]
        + [pl.BlockSpec(memory_space=pltpu.HBM)] * len(parts),
        out_specs=[whole] * 3,
        scratch_shapes=[
            pltpu.VMEM(
                (
                    max(e - s for s, e in zip(bounds, bounds[1:])) // 128,
                    max(e - s for s, e in zip(starts, starts[1:])),
                    128,
                ),
                F32,
            ),
            pltpu.VMEM((9, high, 128), F32),
            pltpu.VMEM((grads.shape[1], embed_parts.columns), BF16),
            pltpu.SemaphoreType.DMA((copies_of(embed_parts.pieces),)),
        ],
        compiler_params=pltpu.CompilerParams(vmem_limit_bytes=32 * 2**20),
        cost_estimate=BRIEF,
    )(embed_parts.where, grads, *parts)


def unit(values):
    mean_row = jnp.mean(values, axis=-1, keepdims=True)
    centred = values - mean_row
    inverse = lax.rsqrt(jnp.mean(centred * centred, axis=-1, keepdims=True) + 1e-06)
    return centred * inverse, inverse


def norm_backward(grad_out, unit_rows, inverse, gain):
    grad_unit = grad_out * gain
    inner = jnp.mean(grad_unit * unit_rows, axis=-1, keepdims=True)
    grad_in = inverse * (
        grad_unit - jnp.mean(grad_unit, axis=-1, keepdims=True) - unit_rows * inner
    )
    return grad_in, jnp.sum(grad_out * unit_rows, axis=0), jnp.sum(grad_out, axis=0)


def chunks(total, most):
    pieces = -(-total // most)
    size = -(-total // pieces)
    size = -(-size // 16) * 16
    return [(s, min(size, total - s)) for s in range(0, total, size)]

def outer_t(first, second):
    return lax.dot_general(first, second, (((1,), (1,)), ((), ())), preferred_element_type=F32)

def attend_kernel(starts, chunk, q_ref, k_ref, v_ref, *refs):
    pair = pl.program_id(0)
    mixed_ref, total_ref = refs[-2:]
    if len(refs) > 2:
        mixed_ref[: starts[0], :] = refs[0][: starts[0], :]

    @pl.when(pair == 0)
    def _():
        total_ref[...] = refs[1][...] if len(refs) > 2 else jnp.zeros_like(total_ref)

    for begin, end in zip(starts, starts[1:]):
        keys, values = k_ref[begin:end, :], v_ref[begin:end, :]
        for offset, size in chunks(end - begin, chunk):
            rows = slice(begin + offset, begin + offset + size)
            queries = q_ref[rows, :] * (HEAD ** -0.5)
            lane = lax.broadcasted_iota(jnp.int32, (size, 128), 1)
            mixed, totals = [], []
            for head in range(2):
                own = (lane < HEAD) if head == 0 else (lane >= HEAD)
                scores = outer_t(jnp.where(own, queries, jnp.zeros_like(queries)), keys)
                top = jnp.max(scores, axis=1, keepdims=True)
                expo = jnp.exp(scores - top)
                total = jnp.sum(expo, axis=1, keepdims=True)
                out = jnp.dot(expo.astype(BF16), values, preferred_element_type=F32)
                mixed.append(out / total)
                totals.append(top + jnp.log(total))
            mixed_ref[rows, :] = jnp.where(lane < HEAD, mixed[0], mixed[1]).astype(BF16)
            held = total_ref[rows, :]
            held = jnp.where(lane == 2 * pair, totals[0], held)
            total_ref[rows, :] = jnp.where(lane == 2 * pair + 1, totals[1], held)

def attend_forward(qkv, starts, done=(), chunk=576):
    rows, width = qkv.shape[0], qkv.shape[1] // 3
    pairs = width // 128
    block = lambda first: pl.BlockSpec((rows, 128), lambda j: (0, first * pairs + j))
    return pl.pallas_call(
        functools.partial(attend_kernel, starts, chunk),
        grid=(pairs,),
        out_shape=(jax.ShapeDtypeStruct((rows, width), BF16), jax.ShapeDtypeStruct((rows, 128), F32)),
        in_specs=[block(0), block(1), block(2)]
        + [block(0), pl.BlockSpec((rows, 128), lambda j: (0, 0))][: len(done)],
        out_specs=[pl.BlockSpec((rows, 128), lambda j: (0, j)), pl.BlockSpec((rows, 128), lambda j: (0, 0))],
        compiler_params=pltpu.CompilerParams(vmem_limit_bytes=24 * 2**20),
        cost_estimate=BRIEF,
    )(qkv, qkv, qkv, *done)

def terms(value):
    first = value.astype(BF16)
    rest = value - first.astype(F32)
    second = rest.astype(BF16)
    return first, second, (rest - second.astype(F32)).astype(BF16)

def attend_back_kernel(starts, chunk, q_ref, k_ref, v_ref, mixed_ref, grad_ref, total_ref, *refs):
    pair = pl.program_id(0)
    *done, out_ref, left, right, acc = refs
    if done:
        out_ref[:, : starts[0], :] = done[0][...]
    scale = HEAD ** -0.5
    zero = jnp.zeros((), BF16)
    for begin, end in zip(starts, starts[1:]):
        size = end - begin
        for offset, part in chunks(size, chunk):
            rows = slice(begin + offset, begin + offset + part)
            lane = lax.broadcasted_iota(jnp.int32, (part, 128), 1)
            queries, grads = q_ref[rows, :] * scale, grad_ref[rows, :]
            product = grads.astype(F32) * mixed_ref[rows, :].astype(F32)
            total_all = total_ref[rows, :]
            for head in range(2):
                own = (lane < HEAD) if head == 0 else (lane >= HEAD)
                free = HEAD * (1 - head)
                inner = jnp.sum(jnp.where(own, product, 0.0), axis=1, keepdims=True)
                total = jnp.sum(jnp.where(lane == 2 * pair + head, total_all, 0.0), axis=1, keepdims=True)
                for target, value, line in ((left, queries, total), (right, grads, inner)):
                    wide = jnp.where(own, value, zero)
                    for i, term in enumerate(terms(line)):
                        wide = jnp.where(lane == free + i, term, wide)
                    target[head, offset:offset + part, :] = wide
        queries, grads = q_ref[begin:end, :], grad_ref[begin:end, :]
        acc[...] = jnp.zeros_like(acc)
        for offset, part in chunks(size, chunk):
            rows = slice(begin + offset, begin + offset + part)
            lane = lax.broadcasted_iota(jnp.int32, (part, 128), 1)
            keys, values = k_ref[rows, :], v_ref[rows, :]
            grad_key, grad_value = [], []
            for head in range(2):
                own = (lane < HEAD) if head == 0 else (lane >= HEAD)
                free = HEAD * (1 - head)
                minus = jnp.where((lane >= free) & (lane < free + 3), -jnp.ones((), BF16), zero)
                scores = outer_t(jnp.where(own, keys, minus), left[head, :size, :])
                probs = jnp.exp(scores)
                grad_scores = outer_t(jnp.where(own, values, minus), right[head, :size, :])
                grad_scores = (probs * grad_scores).astype(BF16)
                grad_value.append(jnp.dot(probs.astype(BF16), grads, preferred_element_type=F32))
                grad_key.append(jnp.dot(grad_scores, queries, preferred_element_type=F32))
                acc[head, :size, :] += lax.dot_general(grad_scores, keys, (((0,), (0,)), ((), ())), preferred_element_type=F32)
            out_ref[1, rows, :] = (jnp.where(lane < HEAD, *grad_key) * scale).astype(BF16)
            out_ref[2, rows, :] = jnp.where(lane < HEAD, *grad_value).astype(BF16)
        lane = lax.broadcasted_iota(jnp.int32, (size, 128), 1)
        out_ref[0, begin:end, :] = (jnp.where(lane < HEAD, acc[0, :size, :], acc[1, :size, :]) * scale).astype(BF16)

def attend_backward(qkv, mixed, totals, grad_mixed, starts, done=(), chunk=400):
    rows, width = starts[-1], mixed.shape[1]
    pairs = width // 128
    longest = max(e - s for s, e in zip(starts, starts[1:]))
    block = lambda first: pl.BlockSpec((rows, 128), lambda j: (0, first * pairs + j))
    return pl.pallas_call(
        functools.partial(attend_back_kernel, starts, chunk),
        grid=(pairs,),
        out_shape=jax.ShapeDtypeStruct((3, rows, width), BF16),
        in_specs=[block(0), block(1), block(2), block(0), block(0)]
        + [pl.BlockSpec((rows, 128), lambda j: (0, 0))]
        + [pl.BlockSpec((3, starts[0], 128), lambda j: (0, 0, j))][: len(done)],
        out_specs=pl.BlockSpec((3, rows, 128), lambda j: (0, 0, j)),
        scratch_shapes=[
            pltpu.VMEM((2, longest, 128), BF16),
            pltpu.VMEM((2, longest, 128), BF16),
            pltpu.VMEM((2, longest, 128), F32),
        ],
        compiler_params=pltpu.CompilerParams(vmem_limit_bytes=24 * 2**20),
        cost_estimate=BRIEF,
    )(qkv, qkv, qkv, mixed, grad_mixed, totals, *done)


def slot_table(side, size, c):
    pixel = lax.broadcasted_iota(jnp.int32, (side * side, size), 0)
    column = lax.broadcasted_iota(jnp.int32, (side * side, size), 1)
    row, spot = column // SLOT - c * side, column % SLOT
    table = (row >= 0) & (row < side) & (spot < side) & (pixel == row * side + spot)
    return table.astype(BF16)


def two_terms(value):
    first = value.astype(BF16)
    return first, (value - first.astype(F32)).astype(BF16)


def resize_kernel(starts, inputs, *refs):
    sources, base_ref, pos_ref, vectors = refs[:3], refs[3], refs[4], refs[5 : 5 + inputs]
    low_ref, high_ref, *resizes, sems, out_ref, small = refs[5 + inputs :]
    copies = [
        pltpu.make_async_copy(source, target, sems.at[i])
        for i, (source, target) in enumerate(zip(sources, resizes))
    ]
    for copy in copies:
        copy.start()
    share = base_ref.shape[1]
    base = jnp.concatenate([base_ref[c] for c in range(3)])
    for start, side, resize_ref, copy in zip(starts, SIDES, resizes, copies):
        copy.wait()
        size = up_to(3 * side * SLOT, 128)
        own = sum(outer_t(base, term) for term in two_terms(resize_ref[...])[::-1]).astype(BF16)
        if side == SLOT:
            for c in range(3):
                first = start + c * side * SLOT
                out_ref[:, first : first + side * SLOT] = own[c * share : (c + 1) * share]
        else:
            out_ref[:, start : start + size] = sum(
                dot(own[c * share : (c + 1) * share], slot_table(side, size, c)) for c in range(3)
            ).astype(BF16)
    spots, width = pos_ref.shape[1], out_ref.shape[1] - starts[3]
    rise = vectors[-1].shape[1] // share
    for i, ref in enumerate(vectors):
        rows = [ref[:, k * share : (k + 1) * share] for k in range(ref.shape[1] // share)]
        for k, row in enumerate(rows):
            small[i + k : i + k + 1, :] = row.astype(F32)
    count = len(vectors) - 1 + rise

    def shift(rows, by):
        row = lax.broadcasted_iota(jnp.int32, (rows, width), 0)
        column = lax.broadcasted_iota(jnp.int32, (rows, width), 1)
        return ((row + by == column) & (row < count + 64 * (by == 0))).astype(BF16)

    small[count:, :] = jnp.zeros((16 - count, share), F32)
    out_ref[:, starts[3] :] = (
        dot(pos_ref[...], shift(spots, 0)) + inner_t(small[...].astype(BF16), shift(16, spots))
    ).astype(BF16)
    low_ref[...] = out_ref[:, : low_ref.shape[1]]
    high_ref[...] = out_ref[:, low_ref.shape[1] :]


def resize_all(resizes, base_kernel, posemb, vectors, starts, columns):
    whole = pl.BlockSpec(memory_space=pltpu.VMEM)
    share = base_kernel.shape[1]
    half = jax.ShapeDtypeStruct((share, columns // 2), BF16)
    return pl.pallas_call(
        functools.partial(resize_kernel, starts, len(vectors)),
        out_shape=(half, half),
        in_specs=[pl.BlockSpec(memory_space=pl.ANY)] * 3 + [whole] * (2 + len(vectors)),
        out_specs=(whole, whole),
        scratch_shapes=[pltpu.VMEM(r.shape, F32) for r in resizes]
        + [
            pltpu.SemaphoreType.DMA((3,)),
            pltpu.VMEM((share, columns), BF16),
            pltpu.VMEM((16, share), F32),
        ],
        compiler_params=pltpu.CompilerParams(vmem_limit_bytes=60 * 2**20),
        cost_estimate=BRIEF,
    )(*resizes, base_kernel, posemb, *vectors)


def enter_kernel(embed_pieces, qkv_pieces, starts, bounds, spots, where_ref, *refs):
    patches, map_ref, refs = refs[:3], refs[3], refs[4:]
    embed_parts, refs = refs[: len(embed_pieces)], refs[len(embed_pieces) :]
    qkv_parts, refs = refs[: len(qkv_pieces)], refs[len(qkv_pieces) :]
    embedded, units, qkv, lines_ref, inverse_ref, small_ref = refs[:6]
    normed, table, weight, embed_sems, qkv_sems = refs[6:]
    width = embedded.shape[1]
    embed_copies = place_copies(embed_pieces, embed_parts, table, where_ref, embed_sems)
    qkv_copies = place_copies(qkv_pieces, qkv_parts, weight, where_ref, qkv_sems)
    for copy in embed_copies + qkv_copies:
        copy.start()
    for copy in embed_copies:
        copy.wait()
    smalls = table[:, bounds[3] :]
    small_ref[...] = smalls
    row = lax.broadcasted_iota(jnp.int32, (16, 128), 0)
    lane = lax.broadcasted_iota(jnp.int32, (16, 128), 1)
    lines = outer_t(((lane == row + spots) & (row < 9)).astype(BF16), smalls)
    lines_ref[...] = lines
    for i, patch_ref in enumerate(patches):
        rows = slice(starts[i], starts[i + 1])
        value = outer_t(patch_ref[...], table[:, bounds[i] : bounds[i + 1]])
        for part in reversed(terms(map_ref[rows, :])):
            value = value + outer_t(part, smalls)
        embedded[rows, :] = value
        unit_rows, inverse = unit(value)
        inverse_ref[rows, :] = inverse
        units[rows, :] = unit_rows.astype(BF16)
        normed[rows, :] = (unit_rows * lines[1:2] + lines[2:3]).astype(BF16)
    for copy in qkv_copies:
        copy.wait()
    for i in range(3):
        columns = slice(i * width, (i + 1) * width)
        value = dot(normed[...], weight[:, columns])
        if i != 1:
            value = value + lines[3 + i // 2 : 4 + i // 2]
        qkv[:, columns] = value.astype(BF16)


def enter_all(embed_parts, qkv_parts, patches, maps, starts, bounds, spots):
    whole = pl.BlockSpec(memory_space=pltpu.VMEM)
    anywhere = pl.BlockSpec(memory_space=pl.ANY)
    parts = [*embed_parts.parts, *qkv_parts.parts]
    rows, width = maps.shape[0], 16 * parts[0].shape[1]
    return pl.pallas_call(
        functools.partial(
            enter_kernel, embed_parts.pieces, qkv_parts.pieces, starts, bounds, spots
        ),
        out_shape=(
            jax.ShapeDtypeStruct((rows, width), F32),
            jax.ShapeDtypeStruct((rows, width), BF16),
            jax.ShapeDtypeStruct((rows, 3 * width), BF16),
            jax.ShapeDtypeStruct((16, width), F32),
            jax.ShapeDtypeStruct((rows, 1), F32),
            jax.ShapeDtypeStruct((width, embed_parts.columns - bounds[3]), BF16),
        ),
        in_specs=[pl.BlockSpec(memory_space=pltpu.SMEM)]
        + [whole] * 4
        + [pl.BlockSpec(memory_space=pltpu.HBM)] * len(parts),
        out_specs=[whole] * 6,
        scratch_shapes=[
            pltpu.VMEM((rows, width), BF16),
            pltpu.VMEM((width, embed_parts.columns), BF16),
            pltpu.VMEM((width, 3 * width), BF16),
            pltpu.SemaphoreType.DMA((copies_of(embed_parts.pieces),)),
            pltpu.SemaphoreType.DMA((copies_of(qkv_parts.pieces),)),
        ],
        compiler_params=pltpu.CompilerParams(vmem_limit_bytes=40 * 2**20),
        cost_estimate=BRIEF,
    )(embed_parts.where, *patches, maps, *parts)


def base_gradient_kernel(starts, *refs):
    resizes, sum_ref, out_ref = refs[:3], refs[3], refs[4]
    share = sum_ref.shape[0]
    total = None
    for start, side, resize_ref in zip(starts, SIDES, resizes):
        size = up_to(3 * side * SLOT, 128)
        given = sum_ref[:, start : start + size]
        if side == SLOT:
            own = [given[:, c * side * SLOT : (c + 1) * side * SLOT] for c in range(3)]
        else:
            own = [outer_t(given, slot_table(side, size, c)).astype(BF16) for c in range(3)]
        own = jnp.concatenate(own)
        for term in two_terms(resize_ref[...])[::-1]:
            value = dot(own, term)
            total = value if total is None else total + value
    for c in range(3):
        out_ref[c] = total[c * share : (c + 1) * share]


def base_gradient(resizes, embed_sum, shape, starts):
    whole = pl.BlockSpec(memory_space=pltpu.VMEM)
    return pl.pallas_call(
        functools.partial(base_gradient_kernel, starts),
        out_shape=jax.ShapeDtypeStruct(shape, F32),
        in_specs=[whole] * 4,
        out_specs=whole,
        compiler_params=pltpu.CompilerParams(vmem_limit_bytes=24 * 2**20),
        cost_estimate=BRIEF,
    )(*resizes, embed_sum)


def gelu_pair(value):
    slope = math.sqrt(2 / math.pi)
    square = value * value
    curve = jnp.tanh(value * (slope + (slope * 0.044715) * square))
    half = 0.5 * value
    rise = 0.5 + 0.5 * curve
    bend = (half - half * (curve * curve)) * (slope + (3 * slope * 0.044715) * square)
    return value * rise, rise + bend


ORDER = (0, 8, 4, 12, 2, 10, 6, 14)


def feed_kernel(starts, chunk, where_ref, *refs):
    mixed_ref, embedded_ref, lines_ref, b_up_ref = refs[:4]
    up_parts, down_parts, cotangents, refs = refs[4:12], refs[12:16], refs[16:19], refs[19:]
    finals = refs[:3]
    up_keep, up_give, down_keep, down_give, g_bias_ref = refs[3:8]
    branch_ref, g_mixed_ref, sums_ref = refs[8:11]
    middle, normed, grads, act, grad_up, total, back = refs[11:18]
    w_up, w_down, w_out, g_up, g_down, g_out = refs[18:24]
    up_in, down_in, out_in, up_out, down_out, out_out, one, ends = refs[24:]
    step, steps = pl.program_id(0), pl.num_programs(0)
    rows = middle.shape[0]
    me, other = where_ref[0], where_ref[1]
    slot = lax.rem(step, 2)
    tile = w_up.shape[2]
    up_rows, down_rows = up_keep.shape[2], w_down.shape[1] // 4
    count = 16

    def at(index, size):
        return pl.ds(pl.multiple_of(index * size, size), size)

    def load_up(s, half):
        t = lax.bitwise_xor(s, me // 4)
        return [
            pltpu.make_async_copy(
                up_parts[4 * (d % 2) + 2 * half + ORDER.index(d - d % 2) // 4].at[
                    ORDER.index(d - d % 2) % 4, :, at(lax.rem(t, 2), tile)
                ],
                w_up.at[lax.rem(s, 2), at(lax.bitwise_xor(me, d), up_rows), :],
                up_in.at[lax.rem(s, 2), d],
            )
            for d in range(count)
        ]

    def load_down(s):
        copies = []
        for j in range(4):
            place_ = s // 2 + 2 * lax.rem(s, 2)
            copies.append(
                pltpu.make_async_copy(
                    down_parts[2 * (j % 2) + j // 2].at[place_, pl.ds(0, down_rows), :],
                    w_down.at[lax.rem(s, 2), at(lax.bitwise_xor(lax.rem(me, 4), j), down_rows), :],
                    down_in.at[lax.rem(s, 2), j],
                )
            )
        return copies

    def load(s):
        t = lax.bitwise_xor(s, me // 4)
        side = lax.bitwise_xor(t // 2, other)
        for half in range(2):

            @pl.when(side == half)
            def _():
                for copy in load_up(s, half):
                    copy.start()

        for copy in load_down(s):
            copy.start()

    def load_out():
        return [
            pltpu.make_async_copy(
                down_parts[2 * (d % 2) + ORDER.index(d - d % 2) // 4].at[
                    ORDER.index(d - d % 2) % 4, pl.ds(down_rows, up_rows), :
                ],
                w_out.at[at(lax.bitwise_xor(me, d), up_rows), :],
                out_in.at[d],
            )
            for d in range(count)
        ]

    def store(s):
        t = lax.bitwise_xor(s, me // 4)
        side = lax.bitwise_xor(t // 2, other)
        copies = []
        for d in range(count):
            copies.append(
                pltpu.make_async_copy(
                    g_up.at[lax.rem(s, 2), at(lax.bitwise_xor(me, d), up_rows), :],
                    (up_keep, up_give)[d % 2].at[side, d // 2, :, at(lax.rem(t, 2), tile)],
                    up_out.at[lax.rem(s, 2), d],
                )
            )
        for j in range(4):
            copies.append(
                pltpu.make_async_copy(
                    g_down.at[lax.rem(s, 2), at(lax.bitwise_xor(lax.rem(me, 4), j), down_rows), :],
                    (down_keep, down_give)[j % 2].at[2 * s + j // 2, pl.ds(0, down_rows), :],
                    down_out.at[lax.rem(s, 2), j],
                )
            )
        return copies

    def store_out():
        return [
            pltpu.make_async_copy(
                g_out.at[at(lax.bitwise_xor(me, d), up_rows), :],
                (down_keep, down_give)[d % 2].at[d // 2, pl.ds(down_rows, up_rows), :],
                out_out.at[d],
            )
            for d in range(count)
        ]

    @pl.when(step == 0)
    def _():
        copy = pltpu.make_async_copy(embedded_ref, middle, one.at[0])
        copy.start()
        for first in load_out():
            first.start()
        load(0)
        for i, ref in enumerate(cotangents):
            grads[starts[i] : starts[i + 1], :] = ref[0]
        copy.wait()
        for first in load_out():
            first.wait()
        for first, size in chunks(rows, 416):
            part = slice(first, first + size)
            value = middle[part, :] + dot(mixed_ref[part, :], w_out[...]) + lines_ref[5:6, :]
            middle[part, :] = value
            unit_rows, _ = unit(value)
            normed[part, :] = (unit_rows * lines_ref[6:7, :] + lines_ref[7:8, :]).astype(BF16)
            total[part, :] = value + lines_ref[8:9, :]
            back[part, :] = jnp.zeros((size, back.shape[1]), F32)

    @pl.when(step + 1 < steps)
    def _():
        load(step + 1)

    for copy in load_up(step, 0) + load_down(step):
        copy.wait()

    column = jnp.zeros((1, tile), F32)
    for first, size in chunks(rows, chunk):
        part = slice(first, first + size)
        up = dot(normed[part, :], w_up[slot]) + b_up_ref[...]
        value, slope = gelu_pair(up)
        value = value.astype(BF16)
        act[part, :] = value
        grad = (slope * outer_t(grads[part, :], w_down[slot])).astype(BF16)
        grad_up[part, :] = grad
        column += jnp.sum(grad.astype(F32), axis=0, keepdims=True)
        total[part, :] += dot(value, w_down[slot])
        back[part, :] += outer_t(grad, w_up[slot])
    g_bias_ref[...] = column

    @pl.when(step >= 2)
    def _():
        for copy in store(step - 2):
            copy.wait()

    g_down[slot] = inner_t(act[...], grads[...]).astype(BF16)
    g_up[slot] = inner_t(normed[...], grad_up[...]).astype(BF16)
    for copy in store(step):
        copy.start()

    @pl.when(step == steps - 1)
    def _():
        done = []

        def leave(source, target):
            done.append(pltpu.make_async_copy(source, target, ends.at[len(done)]))
            done[-1].start()

        for i, ref in enumerate(finals):
            part = pl.ds(starts[i], starts[i + 1] - starts[i])
            act[part, :] = total[part, :].astype(BF16)
            leave(act.at[part, :], ref.at[0])
        width = middle.shape[1]
        sums = [jnp.zeros((1, width), F32)] * 4
        for first, size in chunks(rows, 416):
            part = pl.ds(first, size)
            unit_rows, inverse = unit(middle[part, :])
            out = back[part, :]
            down = grads[part, :].astype(F32)
            grad, gain, bias = norm_backward(out, unit_rows, inverse, lines_ref[6:7, :])
            low = (grad + down).astype(BF16)
            normed[part, :] = low
            leave(normed.at[part, :], branch_ref.at[part, :])
            grad_up[part, :] = outer_t(low, w_out[...]).astype(BF16)
            leave(grad_up.at[part, :], g_mixed_ref.at[part, :])
            found = (
                gain[None],
                bias[None],
                jnp.sum(down, axis=0, keepdims=True),
                jnp.sum(low.astype(F32), axis=0, keepdims=True),
            )
            sums = [a + b for a, b in zip(sums, found)]
        g_out[...] = inner_t(mixed_ref[...], normed[...]).astype(BF16)
        for last in store_out():
            last.start()
        sums_ref[...] = jnp.concatenate(sums + [jnp.zeros((4, width), F32)])
        for last in store_out() + store(step - 1) + store(step) + done:
            last.wait()


def feed_all(where, mixed, embedded, lines, b_up, up_parts, down_parts, cotangents, starts, chunk=624):
    rows, width = mixed.shape
    tile = up_parts[0].shape[2] // 2
    hidden = 4 * tile
    up_rows = up_parts[0].shape[1]
    down_rows = down_parts[0].shape[1]
    fixed = lambda *shape: pl.BlockSpec(
        shape, lambda s, w: (0,) * len(shape), pipeline_mode=pl.Buffered(1)
    )
    whole = lambda *shape: pl.BlockSpec(shape, lambda s, w: (0,) * len(shape))
    mine = pl.BlockSpec((1, tile), lambda s, w: (0, lax.bitwise_xor(s, w[0] // 4)))
    anywhere = pl.BlockSpec(memory_space=pl.ANY)
    like = lambda shape, kind: jax.ShapeDtypeStruct(shape, kind)
    return pl.pallas_call(
        functools.partial(feed_kernel, starts, chunk),
        grid_spec=pltpu.PrefetchScalarGridSpec(
            num_scalar_prefetch=1,
            grid=(4,),
            in_specs=[fixed(rows, width), anywhere, fixed(16, width), mine]
            + [pl.BlockSpec(memory_space=pltpu.HBM)] * 12
            + [fixed(*c.shape) for c in cotangents],
            out_specs=[anywhere] * 7 + [mine, anywhere, anywhere, whole(8, width)],
            scratch_shapes=[
                pltpu.VMEM((rows, width), F32),
                pltpu.VMEM((rows, width), BF16),
                pltpu.VMEM((rows, width), BF16),
                pltpu.VMEM((rows, tile), BF16),
                pltpu.VMEM((rows, tile), BF16),
                pltpu.VMEM((rows, width), F32),
                pltpu.VMEM((rows, width), F32),
                pltpu.VMEM((2, width, tile), BF16),
                pltpu.VMEM((2, tile, width), BF16),
                pltpu.VMEM((width, width), BF16),
                pltpu.VMEM((2, width, tile), BF16),
                pltpu.VMEM((2, tile, width), BF16),
                pltpu.VMEM((width, width), BF16),
                pltpu.SemaphoreType.DMA((2, 16)),
                pltpu.SemaphoreType.DMA((2, 4)),
                pltpu.SemaphoreType.DMA((16,)),
                pltpu.SemaphoreType.DMA((2, 16)),
                pltpu.SemaphoreType.DMA((2, 4)),
                pltpu.SemaphoreType.DMA((16,)),
                pltpu.SemaphoreType.DMA((1,)),
                pltpu.SemaphoreType.DMA((3 + 2 * len(chunks(rows, 416)),)),
            ],
        ),
        out_shape=[like(c.shape, BF16) for c in cotangents]
        + [like((2, 8, up_rows, hidden // 2), BF16)] * 2
        + [like((8, down_rows, width), BF16)] * 2
        + [
            like((1, hidden), F32),
            like((rows, width), BF16),
            like((rows, width), BF16),
            like((8, width), F32),
        ],
        compiler_params=pltpu.CompilerParams(vmem_limit_bytes=56 * 2**20),
        cost_estimate=BRIEF,
    )(where, mixed, embedded, lines, b_up, *up_parts, *down_parts, *cotangents)


def spread_copies(source, segments, where_ref, sems, first=0):
    me, other = where_ref[0], where_ref[1]
    copies = []
    for start, columns, targets, half, there in segments:
        for d in range(16):
            rows = source.shape[0] // 16
            row = pl.ds(pl.multiple_of(lax.bitwise_xor(me, d) * rows, rows), rows)
            target = targets[d % 2]
            if half is not None:
                target = target.at[lax.bitwise_xor(other, half)]
            copies.append(
                pltpu.make_async_copy(
                    source.at[row, pl.ds(start, columns)],
                    target.at[d // 2, :, pl.ds(there, columns)],
                    sems.at[first + len(copies)],
                )
            )
    return copies


def leave_kernel(pieces, starts, bounds, spots, low_columns, chunk, where_ref, *refs):
    grads, units, branch, lines_ref, given_ref, bias_ref, inverse_ref, map_ref = refs[:8]
    patches, parts, refs = refs[8:11], refs[11 : 11 + len(pieces)], refs[11 + len(pieces) :]
    low_ref, low_outs, high_outs, refs = refs[0], refs[1:3], refs[3:5], refs[5:]
    normed, weight, embed_out, qkv_out, sums, weight_sems, out_sems = refs
    rows, width = low_ref.shape
    weights = place_copies(pieces, parts, weight, where_ref, weight_sems)
    half = embed_out.shape[1] // 2
    quarter = half // 2
    low = low_columns - half
    rest = (3 * width - low) // 2
    segments = [
        (qkv_out, (0, low, low_outs, None, half)),
        (qkv_out, (low, rest, high_outs, 0, quarter)),
        (qkv_out, (low + rest, rest, high_outs, 1, quarter)),
        (embed_out, (0, half, low_outs, None, 0)),
        (embed_out, (half, quarter, high_outs, 0, 0)),
        (embed_out, (half + quarter, quarter, high_outs, 1, 0)),
    ]
    copies = []
    for source, segment in segments:
        copies += spread_copies(source, [segment], where_ref, out_sems, len(copies))
    for copy in weights:
        copy.start()
    normed[...] = (units[...].astype(F32) * lines_ref[1:2, :] + lines_ref[2:3, :]).astype(BF16)
    for i in range(3):
        columns = slice(i * width, (i + 1) * width)
        qkv_out[:, columns] = inner_t(normed[...], grads[i]).astype(BF16)
        for copy in copies[16 * i - 16 : 16 * i] if i < 2 else copies[16:48]:
            copy.start()
    sums[...] = jnp.zeros_like(sums)
    sums[5:6, :] = given_ref[3:4, :]
    sums[6:9, :] = given_ref[:3, :]
    for copy in weights:
        copy.wait()
    totals = [jnp.zeros((1, width), F32)] * 4
    for first, size in chunks(rows, chunk):
        part = slice(first, first + size)
        found = sum(
            outer_t(grads[i, part, :], weight[:, i * width : (i + 1) * width]) for i in range(3)
        )
        grad, gain, bias = norm_backward(
            found, units[part, :].astype(F32), inverse_ref[part, :], lines_ref[1:2, :]
        )
        low_ref[part, :] = (grad + branch[part, :].astype(F32)).astype(BF16)
        found = [gain[None], bias[None]] + [
            jnp.sum(grads[i, part, :].astype(F32), axis=0, keepdims=True) for i in (0, 2)
        ]
        totals = [a + b for a, b in zip(totals, found)]
    for i, value in enumerate(totals):
        sums[i + 1 : i + 2, :] = value
    row = lax.broadcasted_iota(jnp.int32, (16, 128), 0)
    lane = lax.broadcasted_iota(jnp.int32, (16, 128), 1)
    smalls = inner_t(sums[...].astype(BF16), ((lane == row + spots) & (row < 9)).astype(BF16))
    rise = bias_ref.shape[1]
    smalls += dot(bias_ref[...], ((lane == row + spots + 9)[:rise]).astype(BF16))
    started = 48
    for i, patch_ref in enumerate(patches):
        part = slice(starts[i], starts[i + 1])
        size = bounds[i + 1] - bounds[i]
        above, below = two_terms(map_ref[part, :])
        found = inner_t(low_ref[part, :], jnp.concatenate([patch_ref[...], above, below], axis=1))
        embed_out[:, bounds[i] : bounds[i + 1]] = found[:, :size].astype(BF16)
        smalls += found[:, size : size + 128] + found[:, size + 128 :]
        if bounds[i + 1] >= half and started == 48:
            started = 64
            for copy in copies[48:64]:
                copy.start()
    embed_out[:, bounds[3] :] = smalls.astype(BF16)
    for copy in copies[started:]:
        copy.start()
    for copy in copies:
        copy.wait()


def leave_all(
    qkv_parts,
    grad_qkv,
    units,
    branch,
    lines,
    given,
    bias,
    inverse,
    maps,
    patches,
    starts,
    bounds,
    spots,
    low_columns,
    chunk=416,
):
    _, rows, width = grad_qkv.shape
    whole = pl.BlockSpec(memory_space=pltpu.VMEM)
    anywhere = pl.BlockSpec(memory_space=pl.ANY)
    parts = qkv_parts.parts
    columns = bounds[3] + 128
    block = width // 16
    high_columns = (3 * width + columns - low_columns) // 2
    return pl.pallas_call(
        functools.partial(
            leave_kernel, qkv_parts.pieces, starts, bounds, spots, low_columns, chunk
        ),
        out_shape=[jax.ShapeDtypeStruct((rows, width), BF16)]
        + [jax.ShapeDtypeStruct((8, block, low_columns), BF16)] * 2
        + [jax.ShapeDtypeStruct((2, 8, block, high_columns), BF16)] * 2,
        in_specs=[pl.BlockSpec(memory_space=pltpu.SMEM)]
        + [whole] * 11
        + [pl.BlockSpec(memory_space=pltpu.HBM)] * len(parts),
        out_specs=[whole] + [anywhere] * 4,
        scratch_shapes=[
            pltpu.VMEM((rows, width), BF16),
            pltpu.VMEM((width, 3 * width), BF16),
            pltpu.VMEM((width, columns), BF16),
            pltpu.VMEM((width, 3 * width), BF16),
            pltpu.VMEM((16, width), F32),
            pltpu.SemaphoreType.DMA((copies_of(qkv_parts.pieces),)),
            pltpu.SemaphoreType.DMA((96,)),
        ],
        compiler_params=pltpu.CompilerParams(vmem_limit_bytes=44 * 2**20),
        cost_estimate=BRIEF,
    )(
        qkv_parts.where,
        grad_qkv,
        units,
        branch,
        lines,
        given,
        bias,
        inverse,
        maps,
        *patches,
        *parts,
    )


def dot(first, second):
    return jnp.dot(first, second, preferred_element_type=F32)


def inner_t(first, second):
    return lax.dot_general(first, second, (((0,), (0,)), ((), ())), preferred_element_type=F32)


def body(count, pixels, resizes, posmaps, weights, cotangents):
    base_kernel, patch_bias, posemb = weights[:3]
    ln1_gain, ln1_bias, qkv_weight, qv_bias, out_weight, out_bias = weights[3:9]
    ln2_gain, ln2_bias, up_weight, up_bias, down_weight, down_bias = weights[9:]
    channels, base_pixels, share = base_kernel.shape
    width = share * count
    spots = posemb.shape[0]
    where = jnp.stack([lax.axis_index("fsdp"), lax.axis_index("rep")]).astype(jnp.int32)
    tokens = [c.shape[1] for c in cotangents]
    starts = [sum(tokens[:i]) for i in range(4)]
    bits = [2**i for i in range(1, count.bit_length() - 1)]
    inward = [(bit,) for bit in bits]
    outward = inward[::-1]
    turned = inward[:1] + outward[:-1]

    up_per = up_bias.shape[0] // share
    used = spots + 9 + up_per
    bounds = [0]
    for side in SIDES:
        bounds.append(bounds[-1] + up_to(3 * side * SLOT, 128))
    columns = bounds[3] + 128
    vectors = [
        v.reshape(1, -1)
        for v in (
            patch_bias,
            ln1_gain,
            ln1_bias,
            qv_bias[0],
            qv_bias[1],
            out_bias,
            ln2_gain,
            ln2_bias,
            down_bias,
            up_bias,
        )
    ]
    maps = jnp.concatenate(posmaps)
    maps = jnp.concatenate(
        [maps, jnp.ones((maps.shape[0], 1), F32), jnp.zeros((maps.shape[0], 127 - spots), F32)],
        axis=1,
    )

    base_turned = base_kernel.swapaxes(1, 2)
    down_rows = (down_weight.shape[0], out_weight.shape[0])
    down_block = jnp.concatenate([down_weight, out_weight])
    qkv_shards = Gather(qkv_weight, where, count, outward, split=True).send()
    up_shards = Gather(up_weight, where, count, outward, split=True, joined=False).send()
    shards = resize_all(resizes, base_turned, posemb.T, vectors, bounds, columns)
    embed_low = Gather(shards[0], where, count, outward).send()
    embed_high = Gather(shards[1], where, count, outward).send()
    held = go_on((pixels, maps, *shards), qkv_shards, embed_low, qkv_shards, embed_high, up_shards)
    held = go_on(held, embed_low, qkv_shards)
    held, down_block = after(held, down_block)
    down_shards = Gather(down_block, where, count, outward, joined=False).send()
    held = finish(held, embed_high, up_shards)
    embed_high.send()
    pixels, maps, *_ = held
    patches = patch_all(pixels)
    patches, maps = together((patches, maps), embed_low, embed_high, qkv_shards, down_shards)
    patches, maps = complete((patches, maps), embed_low, qkv_shards, embed_high)
    up_shards.send()
    w_qkv = Parts([qkv_shards], where, count)
    w_embed = Parts([embed_low, embed_high], where, count)
    embedded, units, qkv, lines, inverse, columns_small = enter_all(
        w_embed, w_qkv, patches, maps, starts, bounds, spots
    )
    qkv = together(qkv, up_shards, down_shards)
    mixed, totals = attend_forward(qkv, starts)
    mixed = together(mixed, up_shards, down_shards)
    mixed = complete(mixed, up_shards, down_shards)
    w_up = Parts([up_shards], where, count)
    w_down = Parts([down_shards], where, count, down_rows)
    b_up = columns_small[:, spots + 9 : used].astype(F32)
    b_up = b_up.reshape(count, share, up_per).swapaxes(1, 2).reshape(1, -1)
    (
        *results,
        up_keep,
        up_give,
        down_keep,
        down_give,
        grad_b_up,
        branch,
        grad_mixed,
        sums,
    ) = feed_all(
        w_up.where, mixed, embedded, lines, b_up, w_up.quarters(2), w_down.quarters(1), cotangents, starts
    )
    rows16 = (down_rows[0] * count // 16, down_rows[1] * count // 16)
    down_sums = Scatter(
        *ordered(down_keep, down_give, where, count, rows16), where, count, inward
    ).send()
    up_sums = Scatter(
        *ordered(up_keep, up_give, where, count, split=True), where, count, inward, split=True
    ).send()
    grad_qkv = attend_backward(qkv, mixed, totals, grad_mixed, starts[:2])
    grad_qkv = together(grad_qkv, down_sums, up_sums)
    grad_qkv = attend_backward(qkv, mixed, totals, grad_mixed, starts[1:], (grad_qkv,))
    grad_qkv = together(grad_qkv, down_sums, up_sums)
    half = columns // 2
    low_columns = half + 5 * width // 3
    grad_low, *shares = leave_all(
        w_qkv,
        grad_qkv,
        units,
        branch,
        lines,
        sums,
        grad_b_up.reshape(width, up_per).astype(BF16),
        inverse,
        maps,
        patches,
        starts,
        bounds,
        spots,
        low_columns,
    )
    grad_low, *arrived = after((grad_low, *shares), *down_sums.sent, *up_sums.sent)
    grad_low, *shares = grad_low
    low_sums = Scatter(*ordered(*shares[:2], where, count), where, count, inward).send()
    high_sums = Scatter(
        *ordered(*shares[2:], where, count, split=True), where, count, inward, split=True
    ).send()
    for chain in (down_sums, up_sums):
        chain.sent, arrived = arrived[: len(chain.sent)], arrived[len(chain.sent) :]
    grad_low = together(grad_low, down_sums, up_sums)
    grad_low = together(grad_low, low_sums)
    grad_low = together(grad_low, high_sums)
    pixel_grads = unpatch_all(grad_low, w_embed, starts, bounds, [p.shape[2] for p in pixels])
    pixel_grads = together(pixel_grads, down_sums, up_sums)
    pixel_grads = go_on(pixel_grads, high_sums, low_sums, high_sums, low_sums, high_sums)
    pixel_grads = go_on(pixel_grads, up_sums, low_sums)
    pixel_grads = complete(pixel_grads, down_sums, high_sums, up_sums, low_sums)

    low, high = low_sums.result, high_sums.result
    quarter = half // 2
    embed_sum = jnp.concatenate([low[:, :half]] + [h[:, :quarter] for h in high], axis=1)
    qkv_sum = jnp.concatenate([low[:, half:]] + [h[:, quarter:] for h in high], axis=1).astype(F32)
    down_sum = down_sums.result.astype(F32)
    up_sum = jnp.concatenate(up_sums.result, axis=1).astype(F32)
    base_grad = base_gradient(resizes, embed_sum, base_turned.shape, bounds).swapaxes(1, 2)
    small_sum = embed_sum[:, bounds[3] : bounds[3] + used].astype(F32)
    vectors = small_sum[:, spots : spots + 9].T
    return (
        *results,
        *pixel_grads,
        base_grad,
        vectors[0],
        small_sum[:, :spots].T,
        vectors[1],
        vectors[2],
        qkv_sum,
        vectors[3:5],
        down_sum[down_rows[0] :],
        vectors[5],
        vectors[6],
        vectors[7],
        up_sum,
        small_sum[:, spots + 9 :].reshape(-1),
        down_sum[: down_rows[0]],
        vectors[8],
    )


def solution(mesh):
    count = mesh.shape["fsdp"]

    def run(*args):
        return body(count, args[:3], args[3:6], args[6:9], args[9:24], args[24:])

    images = ("rep", "fsdp")
    weight_specs = (
        P(None, None, "fsdp"),
        P("fsdp"),
        P(None, "fsdp"),
        P("fsdp"),
        P("fsdp"),
        P("fsdp", None),
        P(None, "fsdp"),
        P("fsdp", None),
        P("fsdp"),
        P("fsdp"),
        P("fsdp"),
        P("fsdp", None),
        P("fsdp"),
        P("fsdp", None),
        P("fsdp"),
    )
    return jax.shard_map(
        run,
        mesh=mesh,
        in_specs=(P(images, None, None, None),) * 3
        + (P(),) * 6
        + weight_specs
        + (P(images, None, None),) * 3,
        out_specs=(P(images, None, None),) * 3
        + (P(images, None, None, None),) * 3
        + weight_specs,
        check_vma=False,
    )
```

```python
import functools
import math

import jax
import jax.numpy as jnp
from jax import lax
from jax.experimental import pallas as pl
from jax.experimental.pallas import tpu as pltpu
from jax.sharding import PartitionSpec as P

HEADS = 12
HEAD = 64
SIDES = (10, 12, 16)
SLOT = 16
F32 = jnp.float32
BF16 = jnp.bfloat16
BRIEF = pl.CostEstimate(flops=1, bytes_accessed=1, transcendentals=0)


def swap(value, axis, size, bit):
    return lax.ppermute(value, axis, [(i, i ^ bit) for i in range(size)])


def after(first, *rest):
    return lax.optimization_barrier((first, *rest))


class Gather:
    def __init__(self, shard, where, count, steps, split=False, joined=True):
        self.count, self.split, self.columns, self.joined = count, split, shard.shape[1], joined
        if split:
            width = shard.shape[1] // 2
            shard = lax.dynamic_slice_in_dim(shard, where[1] * width, width, 1)
        self.held = [(shard[None], [0])]
        self.steps = list(steps) + (["rep"] if split else []) + ["core"]
        self.step = None
        self.pieces = []
        self.ready = [shard[None]]

    def prepare(self):
        if not self.steps:
            self.ready = []
            return
        if self.steps[0] == "core":
            if self.joined:
                size = len(self.held) // (2 if self.split else 1)
                self.held = [
                    self.join(self.held[i : i + size]) for i in range(0, len(self.held), size)
                ]
        elif self.steps[0] != "rep" and len(self.held) > 1:
            self.held = [self.join(self.held)]
        self.ready = [blocks for blocks, *_ in self.held]
        if self.steps[0] == "rep":
            self.ready = self.ready[1:2]

    def join(self, held):
        offsets = [o for h in held for o in h[1]]
        return (join([h[0] for h in held]) if len(held) > 1 else held[0][0], offsets, *held[0][2:])

    def renew(self, ready):
        if self.steps and self.steps[0] == "rep":
            self.held = [self.held[0], (ready[0], *self.held[1][1:]), *self.held[2:]]
        elif ready:
            self.held = [(blocks, *h[1:]) for blocks, h in zip(ready, self.held)]
        self.ready = ready

    def send(self):
        self.step, self.steps = self.steps[0], self.steps[1:]
        if self.step in ("rep", "core"):
            axis, size = ("rep", 2) if self.step == "rep" else ("fsdp", self.count)
            self.sent = [swap(blocks, axis, size, 1) for blocks in self.ready]
        else:
            self.sent = [swap(self.ready[0], "fsdp", self.count, offset) for offset in self.step]
            if self.steps[0] == "rep":
                self.sent.append(swap(self.ready[0], "rep", 2, 1))
        return self

    def take(self, arrived):
        if self.step == "rep":
            own, given, early = self.held
            self.held = [
                (*own, 0),
                (*given, 0),
                (early[0], own[1], 1),
                (arrived[0], given[1], 1),
            ]
        elif self.step == "core":
            held = [h if len(h) == 3 else (*h, None) for h in self.held]
            self.held = held + [
                (blocks, [o ^ 1 for o in h[1]], h[2]) for blocks, h in zip(arrived, held)
            ]
        else:
            offsets = self.held[0][1]
            self.held = self.held + [
                (blocks, [o ^ offset for o in offsets])
                for blocks, offset in zip(arrived, self.step)
            ]
            if self.steps[0] == "rep":
                self.held.append((arrived[-1], offsets))


def finish(anchor, *chains):
    sizes = [len(chain.sent) for chain in chains]
    anchor, *flat = after(anchor, *[part for chain in chains for part in chain.sent])
    for chain, size in zip(chains, sizes):
        chain.take(flat[:size])
        chain.prepare()
        flat = flat[size:]
        chain.sent = []
    sizes = [len(chain.ready) for chain in chains]
    anchor, *flat = after(anchor, *[part for chain in chains for part in chain.ready])
    for chain, size in zip(chains, sizes):
        chain.renew(flat[:size])
        flat = flat[size:]
    return anchor


def together(anchor, *chains):
    anchor = finish(anchor, *chains)
    for chain in chains:
        if chain.steps:
            chain.send()
    return anchor


def go_on(anchor, *chains):
    for chain in chains:
        anchor = together(anchor, chain)
    return anchor


def complete(anchor, *chains):
    chains = [chain for chain in chains if chain.sent]
    while chains:
        left = [chain for chain in chains if chain.steps]
        anchor = go_on(anchor, *chains)
        chains = left
    return anchor


def place_copies(pieces, parts, whole, where_ref, sems):
    me, other = where_ref[0], where_ref[1]
    copies = []
    for part, (offsets, half, first, columns) in zip(parts, pieces):
        rows = part.shape[1]
        for k, offset in enumerate(offsets):
            row = pl.ds(pl.multiple_of(lax.bitwise_xor(me, offset) * rows, rows), rows)
            if half is None:
                target = whole.at[row, pl.ds(first, columns)]
            else:
                width = columns // 2
                start = pl.multiple_of(first + lax.bitwise_xor(other, half) * width, 128)
                target = whole.at[row, pl.ds(start, width)]
            copies.append(pltpu.make_async_copy(part.at[k], target, sems.at[len(copies)]))
    return copies


def copies_of(pieces):
    return sum(len(offsets) for offsets, *_ in pieces)


def place_kernel(pieces, me_ref, *refs):
    parts, whole, sems = refs[: len(pieces)], refs[len(pieces)], refs[len(pieces) + 1]
    me, other = me_ref[0], me_ref[1]
    copies = []
    for part, (offsets, half, first, columns) in zip(parts, pieces):
        for k, offset in enumerate(offsets):
            row = lax.bitwise_xor(me, offset)
            if half is None:
                target = whole.at[row, :, pl.ds(first, columns)]
            else:
                width = columns // 2
                start = pl.multiple_of(first + lax.bitwise_xor(other, half) * width, 128)
                target = whole.at[row, :, pl.ds(start, width)]
            copies.append(pltpu.make_async_copy(part.at[k], target, sems.at[len(copies)]))
    for copy in copies:
        copy.start()
    for copy in copies:
        copy.wait()


def place(gathers, where, count):
    parts, pieces = parts_of(gathers)
    rows, kind = parts[0].shape[1], parts[0].dtype
    columns = sum(g.columns for g in gathers)
    whole = pl.pallas_call(
        functools.partial(place_kernel, pieces),
        out_shape=jax.ShapeDtypeStruct((count, rows, columns), kind),
        in_specs=[pl.BlockSpec(memory_space=pltpu.SMEM)]
        + [pl.BlockSpec(memory_space=pl.ANY)] * len(pieces),
        out_specs=pl.BlockSpec(memory_space=pltpu.VMEM),
        scratch_shapes=[pltpu.SemaphoreType.DMA((copies_of(pieces),))],
        compiler_params=pltpu.CompilerParams(vmem_limit_bytes=16 * 2**20),
        cost_estimate=BRIEF,
    )(where, *parts)
    return whole.reshape(count * rows, columns)


def parts_of(gathers):
    parts, pieces, first = [], [], 0
    for g in gathers:
        for blocks, offsets, half in g.held:
            parts.append(blocks)
            pieces.append((tuple(offsets), half, first, g.columns))
        first += g.columns
    return parts, pieces


def regroup(blocks, rows, count):
    parts, first = [], 0
    for size in rows:
        part = blocks[:, first : first + size]
        parts.append(part.reshape(count, -1, blocks.shape[2]))
        first += size
    return jnp.concatenate(parts, axis=1)


class Parts:
    def __init__(self, gathers, where, count, rows=None):
        self.columns = sum(g.columns for g in gathers)
        self.where = where
        if count == 16:
            self.parts, self.pieces = parts_of(gathers)
        else:
            whole = place(gathers, where, count).reshape(count, -1, self.columns)
            rows = rows or (whole.shape[1],)
            self.parts = [regroup(whole, rows, 16)]
            self.pieces = [(tuple(range(16)), None, 0, self.columns)]
            self.where = jnp.zeros_like(where)

    def quarters(self, halves):
        if len(self.parts) > 1:
            assert len(self.parts) == 4 * halves
            assert self.pieces[0][0] + self.pieces[1][0] == ORDER
            return self.parts
        size = self.columns // halves
        return [
            jnp.stack([self.parts[0][o + core, :, h * size : (h + 1) * size] for o in quarter])
            for core in range(2)
            for h in range(halves)
            for quarter in (ORDER[:4], ORDER[4:])
        ]


def ordered(keep, give, where, count, rows=None, split=False):
    if count == 16:
        return keep, give
    if not split:
        keep, give = keep[None], give[None]
    whole = jnp.stack([keep, give], axis=2)
    halves, blocks, _, size, columns = whole.shape
    whole = whole.reshape(halves, 2 * blocks, size, columns)
    whole = jnp.concatenate([whole[h] for h in range(halves)], axis=2)
    columns = whole.shape[2]
    whole = regroup(whole, rows or (size,), count).reshape(-1, columns)
    found = take([whole], [(0, 0, columns)], where, count, split)
    if split:
        return jnp.stack(found[:2]), jnp.stack(found[2:])
    return found


def take_kernel(count, split, segments, me_ref, *refs):
    inputs = max(which for which, *_ in segments) + 1
    wholes, outs, sems = refs[:inputs], refs[inputs:-1], refs[-1]
    me, other = me_ref[0], me_ref[1]
    half = outs[0].shape[2]

    def copies(switch):
        found = []
        for which, start, columns, first in segments:
            for d in range(count):
                source = wholes[which].at[lax.bitwise_xor(me, d), :, pl.ds(start, columns)]
                side = (first // half) ^ switch
                target = outs[2 * (d % 2) + side] if split else outs[d % 2]
                target = target.at[d // 2, :, pl.ds(first % half, columns)]
                found.append(pltpu.make_async_copy(source, target, sems.at[len(found)]))
        return found

    def run(switch):
        found = copies(switch)
        for copy in found:
            copy.start()
        for copy in found:
            copy.wait()

    if split:
        for switch in range(2):
            pl.when(other == switch)(functools.partial(run, switch))
    else:
        run(0)


def take(wholes, segments, where, count, split):
    rows = wholes[0].shape[0] // count
    blocks = [w.reshape(count, rows, w.shape[1]) for w in wholes]
    columns = sum(segment[2] for segment in segments)
    half = columns // 2 if split else columns
    ends, first = [], 0
    for which, start, size in segments:
        while size:
            room = min(size, half - first % half)
            ends.append((which, start, room, first))
            first, start, size = first + room, start + room, size - room
    shape = jax.ShapeDtypeStruct((count // 2, rows, half), wholes[0].dtype)
    outs = 4 if split else 2
    return pl.pallas_call(
        functools.partial(take_kernel, count, split, ends),
        out_shape=(shape,) * outs,
        in_specs=[pl.BlockSpec(memory_space=pltpu.SMEM)]
        + [pl.BlockSpec(memory_space=pltpu.VMEM)] * len(blocks),
        out_specs=[pl.BlockSpec(memory_space=pl.ANY)] * outs,
        scratch_shapes=[pltpu.SemaphoreType.DMA((count * len(ends),))],
        compiler_params=pltpu.CompilerParams(vmem_limit_bytes=16 * 2**20),
        cost_estimate=BRIEF,
    )(where, *blocks)


def add(*values):
    return sum(value.astype(F32) for value in values).astype(BF16)


def join_kernel(*refs):
    *parts, whole = refs
    first = 0
    for part in parts:
        whole[first : first + part.shape[0]] = part[...]
        first += part.shape[0]


def join(parts):
    blocks = sum(part.shape[0] for part in parts)
    whole = pl.BlockSpec(memory_space=pltpu.VMEM)
    return pl.pallas_call(
        join_kernel,
        out_shape=jax.ShapeDtypeStruct((blocks, *parts[0].shape[1:]), parts[0].dtype),
        in_specs=[whole] * len(parts),
        out_specs=whole,
        compiler_params=pltpu.CompilerParams(vmem_limit_bytes=16 * 2**20),
        cost_estimate=BRIEF,
    )(*parts)


def merge_kernel(groups, parts, *refs):
    outs = refs[parts:]
    for group, out in zip(groups, outs):
        for j, index in enumerate(group):
            out[j] = sum(ref[index].astype(F32) for ref in refs[:parts]).astype(BF16)


def merge(parts, groups):
    rest = parts[0].shape[-2:]
    whole = pl.BlockSpec(memory_space=pltpu.VMEM)
    return pl.pallas_call(
        functools.partial(merge_kernel, groups, len(parts)),
        out_shape=[jax.ShapeDtypeStruct((len(group), *rest), BF16) for group in groups],
        in_specs=[whole] * len(parts),
        out_specs=[whole] * len(groups),
        compiler_params=pltpu.CompilerParams(vmem_limit_bytes=24 * 2**20),
        cost_estimate=BRIEF,
    )(*parts)


class Scatter:
    def __init__(self, keep, give, where, count, steps, split=False):
        self.where, self.count, self.split = where, count, split
        self.keep, self.give = keep, give
        self.steps = ["core"] + (["half"] if split else []) + list(steps) + ["rep"]
        self.offsets = list(range(0, count, 2))
        self.step = None

        self.ready = [give]

    def prepare(self):
        pass

    def renew(self, ready):
        self.ready = ready

    def send(self):
        self.step, self.steps = self.steps[0], self.steps[1:]
        if self.step in ("half", "rep"):
            self.sent = [swap(self.ready[0], "rep", 2, 1)]
        else:
            offsets = [1] if self.step == "core" else self.step
            self.sent = [
                swap(part, "fsdp", self.count, offset)
                for part, offset in zip(self.ready, offsets)
            ]
        return self

    def share_out(self, parts):
        step = self.steps[0]
        if step == "rep":
            self.held = merge(parts, [[0]])[0][0]
            self.ready = [self.held]
            return
        mask = 0
        for offset in step:
            mask |= offset
        stay = [o for o in self.offsets if o & mask == 0]
        groups = [[self.offsets.index(o | offset) for o in stay] for offset in (0, *step)]
        self.staying, *self.ready = merge(parts, groups)
        self.offsets = stay

    def take(self, arrived):
        if self.step == "core" and self.split:
            blocks = len(self.offsets)
            flat = [a.reshape(2 * blocks, *a.shape[2:]) for a in (self.keep, *arrived)]
            away, self.staying = merge(
                flat, [list(range(blocks, 2 * blocks)), list(range(blocks))]
            )
            self.ready = [away]
        elif self.step == "core":
            self.share_out([self.keep, *arrived])
        elif self.step == "rep":
            if self.split:
                low = self.where[1] == 0
                self.result = [
                    jnp.where(low, self.held, arrived[0]),
                    jnp.where(low, arrived[0], self.held),
                ]
            else:
                self.result = add(self.held, arrived[0])
            self.ready = []
        else:
            self.share_out([self.staying, *arrived])


def up_to(value, unit):
    return -(-value // unit) * unit

def swap_chunks(lines):
    chunk = lax.broadcasted_iota(jnp.int32, lines[0].shape, 1) // SLOT
    for step in (1, 2, 4):
        stays = (chunk & step) == 0
        for i in range(8):
            if i & step == 0:
                low, high = lines[i], lines[i + step]
                lines[i] = jnp.where(stays, low, pltpu.roll(high, step * SLOT, 1))
                lines[i + step] = jnp.where(stays, pltpu.roll(low, 128 - step * SLOT, 1), high)
    return lines

def spread(side, grid, columns):
    pixel = lax.broadcasted_iota(jnp.int32, (grid * side, columns), 0)
    column = lax.broadcasted_iota(jnp.int32, (grid * side, columns), 1)
    place = column % SLOT
    return ((pixel == column // SLOT * side + place) & (place < side)).astype(BF16)

def patch_kernel(*refs):
    pixels, outs, rows_ref, flat_ref = refs[:3], refs[3:6], refs[6], refs[7]
    for side, pixel_ref, out in zip(SIDES, pixels, outs):
        high = pixel_ref.shape[2]
        grid = high // side
        columns = up_to(grid * SLOT, 128)
        table = None if side == SLOT else spread(side, grid, columns)
        for c in range(3):
            picture = pixel_ref[0, c]
            if table is None:
                wide = picture.astype(F32)
            else:
                wide = jnp.dot(picture, table, preferred_element_type=F32)
            for block in range(columns // 128):
                rows_ref[3 * c + block, :high, :] = wide[:, 128 * block:128 * block + 128]
        slots = 3 * side
        for group in range(out.shape[1] // 128):
            for block in range(columns // 128):
                lines = []
                for q in range(8 * group, 8 * group + 8):
                    if q < slots:
                        lines.append(rows_ref[q // side * 3 + block, pl.ds(q % side, grid, stride=side), :])
                    else:
                        lines.append(jnp.zeros((grid, 128), F32))
                lines = swap_chunks(lines)
                for g in range(8):
                    if 8 * block + g < grid:
                        flat_ref[group, pl.ds(8 * block + g, grid, stride=grid), :] = lines[g]
        for group in range(out.shape[1] // 128):
            out[:, 128 * group:128 * group + 128] = flat_ref[group, :grid * grid, :].astype(BF16)

def patch_all(pixels):
    shapes = []
    for picture, side in zip(pixels, SIDES):
        grid = picture.shape[2] // side
        shapes.append(jax.ShapeDtypeStruct((grid * grid, up_to(3 * side * SLOT, 128)), BF16))
    high = max(p.shape[2] for p in pixels)
    return pl.pallas_call(
        patch_kernel,
        out_shape=shapes,
        in_specs=[pl.BlockSpec(memory_space=pltpu.VMEM)] * 3,
        out_specs=[pl.BlockSpec(memory_space=pltpu.VMEM)] * 3,
        scratch_shapes=[pltpu.VMEM((9, high, 128), F32), pltpu.VMEM((max(s.shape[1] for s in shapes) // 128, max(s.shape[0] for s in shapes), 128), F32)],
        compiler_params=pltpu.CompilerParams(vmem_limit_bytes=40 * 2**20),
        cost_estimate=BRIEF,
    )(*pixels)

def unpatch_kernel(pieces, starts, bounds, where_ref, grad_ref, *refs):
    parts, refs = refs[: len(pieces)], refs[len(pieces) :]
    outs, flat_ref, rows_ref, kernel_ref, sems = refs[:3], *refs[3:]
    copies = place_copies(pieces, parts, kernel_ref, where_ref, sems)
    for copy in copies:
        copy.start()
    for copy in copies:
        copy.wait()
    for i, side in enumerate(SIDES):
        out = outs[i]
        high = out.shape[2]
        grid = high // side
        columns = up_to(grid * SLOT, 128)
        width = bounds[i + 1] - bounds[i]
        grads = grad_ref[starts[i]:starts[i + 1], :]
        flat = jnp.dot(grads, kernel_ref[:, bounds[i]:bounds[i + 1]], preferred_element_type=F32)
        for group in range(width // 128):
            flat_ref[group, :grid * grid, :] = flat[:, 128 * group:128 * group + 128]
        slots = 3 * side
        for group in range(width // 128):
            for block in range(columns // 128):
                lines = []
                for g in range(8):
                    if 8 * block + g < grid:
                        lines.append(flat_ref[group, pl.ds(8 * block + g, grid, stride=grid), :])
                    else:
                        lines.append(jnp.zeros((grid, 128), F32))
                lines = swap_chunks(lines)
                for q in range(8 * group, min(8 * group + 8, slots)):
                    rows_ref[q // side * 3 + block, pl.ds(q % side, grid, stride=side), :] = lines[q % 8]
        table = None if side == SLOT else spread(side, grid, columns)
        for c in range(3):
            picture = jnp.concatenate([rows_ref[3 * c + block, :high, :] for block in range(columns // 128)], axis=1).astype(BF16)
            if table is not None:
                picture = lax.dot_general(picture, table, (((1,), (1,)), ((), ())), preferred_element_type=F32).astype(BF16)
            out[0, c] = picture

def unpatch_all(grads, embed_parts, starts, bounds, sides):
    high = max(sides)
    whole = pl.BlockSpec(memory_space=pltpu.VMEM)
    parts = embed_parts.parts
    return pl.pallas_call(
        functools.partial(unpatch_kernel, embed_parts.pieces, starts, bounds),
        out_shape=[jax.ShapeDtypeStruct((1, 3, s, s), BF16) for s in sides],
        in_specs=[pl.BlockSpec(memory_space=pltpu.SMEM), whole]
        + [pl.BlockSpec(memory_space=pltpu.HBM)] * len(parts),
        out_specs=[whole] * 3,
        scratch_shapes=[
            pltpu.VMEM(
                (
                    max(e - s for s, e in zip(bounds, bounds[1:])) // 128,
                    max(e - s for s, e in zip(starts, starts[1:])),
                    128,
                ),
                F32,
            ),
            pltpu.VMEM((9, high, 128), F32),
            pltpu.VMEM((grads.shape[1], embed_parts.columns), BF16),
            pltpu.SemaphoreType.DMA((copies_of(embed_parts.pieces),)),
        ],
        compiler_params=pltpu.CompilerParams(vmem_limit_bytes=32 * 2**20),
        cost_estimate=BRIEF,
    )(embed_parts.where, grads, *parts)


def unit(values):
    mean_row = jnp.mean(values, axis=-1, keepdims=True)
    centred = values - mean_row
    inverse = lax.rsqrt(jnp.mean(centred * centred, axis=-1, keepdims=True) + 1e-06)
    return centred * inverse, inverse


def norm_backward(grad_out, unit_rows, inverse, gain):
    grad_unit = grad_out * gain
    inner = jnp.mean(grad_unit * unit_rows, axis=-1, keepdims=True)
    grad_in = inverse * (
        grad_unit - jnp.mean(grad_unit, axis=-1, keepdims=True) - unit_rows * inner
    )
    return grad_in, jnp.sum(grad_out * unit_rows, axis=0), jnp.sum(grad_out, axis=0)


def chunks(total, most):
    pieces = -(-total // most)
    size = -(-total // pieces)
    size = -(-size // 16) * 16
    return [(s, min(size, total - s)) for s in range(0, total, size)]

def outer_t(first, second):
    return lax.dot_general(first, second, (((1,), (1,)), ((), ())), preferred_element_type=F32)

def attend_kernel(starts, chunk, q_ref, k_ref, v_ref, *refs):
    pair = pl.program_id(0)
    mixed_ref, total_ref = refs[-2:]
    if len(refs) > 2:
        mixed_ref[: starts[0], :] = refs[0][: starts[0], :]

    @pl.when(pair == 0)
    def _():
        total_ref[...] = refs[1][...] if len(refs) > 2 else jnp.zeros_like(total_ref)

    for begin, end in zip(starts, starts[1:]):
        keys, values = k_ref[begin:end, :], v_ref[begin:end, :]
        for offset, size in chunks(end - begin, chunk):
            rows = slice(begin + offset, begin + offset + size)
            queries = q_ref[rows, :] * (HEAD ** -0.5)
            lane = lax.broadcasted_iota(jnp.int32, (size, 128), 1)
            mixed, totals = [], []
            for head in range(2):
                own = (lane < HEAD) if head == 0 else (lane >= HEAD)
                scores = outer_t(jnp.where(own, queries, jnp.zeros_like(queries)), keys)
                top = jnp.max(scores, axis=1, keepdims=True)
                expo = jnp.exp(scores - top)
                total = jnp.sum(expo, axis=1, keepdims=True)
                out = jnp.dot(expo.astype(BF16), values, preferred_element_type=F32)
                mixed.append(out / total)
                totals.append(top + jnp.log(total))
            mixed_ref[rows, :] = jnp.where(lane < HEAD, mixed[0], mixed[1]).astype(BF16)
            held = total_ref[rows, :]
            held = jnp.where(lane == 2 * pair, totals[0], held)
            total_ref[rows, :] = jnp.where(lane == 2 * pair + 1, totals[1], held)

def attend_forward(qkv, starts, done=(), chunk=576):
    rows, width = qkv.shape[0], qkv.shape[1] // 3
    pairs = width // 128
    block = lambda first: pl.BlockSpec((rows, 128), lambda j: (0, first * pairs + j))
    return pl.pallas_call(
        functools.partial(attend_kernel, starts, chunk),
        grid=(pairs,),
        out_shape=(jax.ShapeDtypeStruct((rows, width), BF16), jax.ShapeDtypeStruct((rows, 128), F32)),
        in_specs=[block(0), block(1), block(2)]
        + [block(0), pl.BlockSpec((rows, 128), lambda j: (0, 0))][: len(done)],
        out_specs=[pl.BlockSpec((rows, 128), lambda j: (0, j)), pl.BlockSpec((rows, 128), lambda j: (0, 0))],
        compiler_params=pltpu.CompilerParams(vmem_limit_bytes=60 * 2**20),
        cost_estimate=BRIEF,
    )(qkv, qkv, qkv, *done)

def terms(value):
    first = value.astype(BF16)
    rest = value - first.astype(F32)
    second = rest.astype(BF16)
    return first, second, (rest - second.astype(F32)).astype(BF16)

def attend_back_kernel(starts, chunk, q_ref, k_ref, v_ref, mixed_ref, grad_ref, total_ref, *refs):
    pair = pl.program_id(0)
    *done, out_ref, left, right, acc = refs
    if done:
        out_ref[:, : starts[0], :] = done[0][...]
    scale = HEAD ** -0.5
    zero = jnp.zeros((), BF16)
    for begin, end in zip(starts, starts[1:]):
        size = end - begin
        for offset, part in chunks(size, chunk):
            rows = slice(begin + offset, begin + offset + part)
            lane = lax.broadcasted_iota(jnp.int32, (part, 128), 1)
            queries, grads = q_ref[rows, :] * scale, grad_ref[rows, :]
            product = grads.astype(F32) * mixed_ref[rows, :].astype(F32)
            total_all = total_ref[rows, :]
            for head in range(2):
                own = (lane < HEAD) if head == 0 else (lane >= HEAD)
                free = HEAD * (1 - head)
                inner = jnp.sum(jnp.where(own, product, 0.0), axis=1, keepdims=True)
                total = jnp.sum(jnp.where(lane == 2 * pair + head, total_all, 0.0), axis=1, keepdims=True)
                for target, value, line in ((left, queries, total), (right, grads, inner)):
                    wide = jnp.where(own, value, zero)
                    for i, term in enumerate(terms(line)):
                        wide = jnp.where(lane == free + i, term, wide)
                    target[head, offset:offset + part, :] = wide
        queries, grads = q_ref[begin:end, :], grad_ref[begin:end, :]
        acc[...] = jnp.zeros_like(acc)
        for offset, part in chunks(size, chunk):
            rows = slice(begin + offset, begin + offset + part)
            lane = lax.broadcasted_iota(jnp.int32, (part, 128), 1)
            keys, values = k_ref[rows, :], v_ref[rows, :]
            grad_key, grad_value = [], []
            for head in range(2):
                own = (lane < HEAD) if head == 0 else (lane >= HEAD)
                free = HEAD * (1 - head)
                minus = jnp.where((lane >= free) & (lane < free + 3), -jnp.ones((), BF16), zero)
                scores = outer_t(jnp.where(own, keys, minus), left[head, :size, :])
                probs = jnp.exp(scores)
                grad_scores = outer_t(jnp.where(own, values, minus), right[head, :size, :])
                grad_scores = (probs * grad_scores).astype(BF16)
                grad_value.append(jnp.dot(probs.astype(BF16), grads, preferred_element_type=F32))
                grad_key.append(jnp.dot(grad_scores, queries, preferred_element_type=F32))
                acc[head, :size, :] += lax.dot_general(grad_scores, keys, (((0,), (0,)), ((), ())), preferred_element_type=F32)
            out_ref[1, rows, :] = (jnp.where(lane < HEAD, *grad_key) * scale).astype(BF16)
            out_ref[2, rows, :] = jnp.where(lane < HEAD, *grad_value).astype(BF16)
        lane = lax.broadcasted_iota(jnp.int32, (size, 128), 1)
        out_ref[0, begin:end, :] = (jnp.where(lane < HEAD, acc[0, :size, :], acc[1, :size, :]) * scale).astype(BF16)

def attend_backward(qkv, mixed, totals, grad_mixed, starts, done=(), chunk=400):
    rows, width = starts[-1], mixed.shape[1]
    pairs = width // 128
    longest = max(e - s for s, e in zip(starts, starts[1:]))
    block = lambda first: pl.BlockSpec((rows, 128), lambda j: (0, first * pairs + j))
    return pl.pallas_call(
        functools.partial(attend_back_kernel, starts, chunk),
        grid=(pairs,),
        out_shape=jax.ShapeDtypeStruct((3, rows, width), BF16),
        in_specs=[block(0), block(1), block(2), block(0), block(0)]
        + [pl.BlockSpec((rows, 128), lambda j: (0, 0))]
        + [pl.BlockSpec((3, starts[0], 128), lambda j: (0, 0, j))][: len(done)],
        out_specs=pl.BlockSpec((3, rows, 128), lambda j: (0, 0, j)),
        scratch_shapes=[
            pltpu.VMEM((2, longest, 128), BF16),
            pltpu.VMEM((2, longest, 128), BF16),
            pltpu.VMEM((2, longest, 128), F32),
        ],
        compiler_params=pltpu.CompilerParams(vmem_limit_bytes=24 * 2**20),
        cost_estimate=BRIEF,
    )(qkv, qkv, qkv, mixed, grad_mixed, totals, *done)


def slot_table(side, size, c):
    pixel = lax.broadcasted_iota(jnp.int32, (side * side, size), 0)
    column = lax.broadcasted_iota(jnp.int32, (side * side, size), 1)
    row, spot = column // SLOT - c * side, column % SLOT
    table = (row >= 0) & (row < side) & (spot < side) & (pixel == row * side + spot)
    return table.astype(BF16)


def two_terms(value):
    first = value.astype(BF16)
    return first, (value - first.astype(F32)).astype(BF16)


def resize_kernel(starts, inputs, *refs):
    sources, base_ref, pos_ref, vectors = refs[:3], refs[3], refs[4], refs[5 : 5 + inputs]
    low_ref, high_ref, *resizes, sems, out_ref, small = refs[5 + inputs :]
    copies = [
        pltpu.make_async_copy(source, target, sems.at[i])
        for i, (source, target) in enumerate(zip(sources, resizes))
    ]
    for copy in copies:
        copy.start()
    share = base_ref.shape[1]
    base = jnp.concatenate([base_ref[c] for c in range(3)])
    for start, side, resize_ref, copy in zip(starts, SIDES, resizes, copies):
        copy.wait()
        size = up_to(3 * side * SLOT, 128)
        own = sum(outer_t(base, term) for term in two_terms(resize_ref[...])[::-1]).astype(BF16)
        if side == SLOT:
            for c in range(3):
                first = start + c * side * SLOT
                out_ref[:, first : first + side * SLOT] = own[c * share : (c + 1) * share]
        else:
            out_ref[:, start : start + size] = sum(
                dot(own[c * share : (c + 1) * share], slot_table(side, size, c)) for c in range(3)
            ).astype(BF16)
    spots, width = pos_ref.shape[1], out_ref.shape[1] - starts[3]
    rise = vectors[-1].shape[1] // share
    for i, ref in enumerate(vectors):
        rows = [ref[:, k * share : (k + 1) * share] for k in range(ref.shape[1] // share)]
        for k, row in enumerate(rows):
            small[i + k : i + k + 1, :] = row.astype(F32)
    count = len(vectors) - 1 + rise

    def shift(rows, by):
        row = lax.broadcasted_iota(jnp.int32, (rows, width), 0)
        column = lax.broadcasted_iota(jnp.int32, (rows, width), 1)
        return ((row + by == column) & (row < count + 64 * (by == 0))).astype(BF16)

    small[count:, :] = jnp.zeros((16 - count, share), F32)
    out_ref[:, starts[3] :] = (
        dot(pos_ref[...], shift(spots, 0)) + inner_t(small[...].astype(BF16), shift(16, spots))
    ).astype(BF16)
    low_ref[...] = out_ref[:, : low_ref.shape[1]]
    high_ref[...] = out_ref[:, low_ref.shape[1] :]


def resize_all(resizes, base_kernel, posemb, vectors, starts, columns):
    whole = pl.BlockSpec(memory_space=pltpu.VMEM)
    share = base_kernel.shape[1]
    half = jax.ShapeDtypeStruct((share, columns // 2), BF16)
    return pl.pallas_call(
        functools.partial(resize_kernel, starts, len(vectors)),
        out_shape=(half, half),
        in_specs=[pl.BlockSpec(memory_space=pl.ANY)] * 3 + [whole] * (2 + len(vectors)),
        out_specs=(whole, whole),
        scratch_shapes=[pltpu.VMEM(r.shape, F32) for r in resizes]
        + [
            pltpu.SemaphoreType.DMA((3,)),
            pltpu.VMEM((share, columns), BF16),
            pltpu.VMEM((16, share), F32),
        ],
        compiler_params=pltpu.CompilerParams(vmem_limit_bytes=60 * 2**20),
        cost_estimate=BRIEF,
    )(*resizes, base_kernel, posemb, *vectors)


def enter_kernel(embed_pieces, qkv_pieces, starts, bounds, spots, where_ref, *refs):
    patches, map_ref, refs = refs[:3], refs[3], refs[4:]
    embed_parts, refs = refs[: len(embed_pieces)], refs[len(embed_pieces) :]
    qkv_parts, refs = refs[: len(qkv_pieces)], refs[len(qkv_pieces) :]
    embedded, units, qkv, lines_ref, inverse_ref, small_ref = refs[:6]
    normed, table, weight, embed_sems, qkv_sems = refs[6:]
    width = embedded.shape[1]
    embed_copies = place_copies(embed_pieces, embed_parts, table, where_ref, embed_sems)
    qkv_copies = place_copies(qkv_pieces, qkv_parts, weight, where_ref, qkv_sems)
    for copy in embed_copies + qkv_copies:
        copy.start()
    for copy in embed_copies:
        copy.wait()
    smalls = table[:, bounds[3] :]
    small_ref[...] = smalls
    row = lax.broadcasted_iota(jnp.int32, (16, 128), 0)
    lane = lax.broadcasted_iota(jnp.int32, (16, 128), 1)
    lines = outer_t(((lane == row + spots) & (row < 9)).astype(BF16), smalls)
    lines_ref[...] = lines
    for i, patch_ref in enumerate(patches):
        rows = slice(starts[i], starts[i + 1])
        value = outer_t(patch_ref[...], table[:, bounds[i] : bounds[i + 1]])
        for part in reversed(terms(map_ref[rows, :])):
            value = value + outer_t(part, smalls)
        embedded[rows, :] = value
        unit_rows, inverse = unit(value)
        inverse_ref[rows, :] = inverse
        units[rows, :] = unit_rows.astype(BF16)
        normed[rows, :] = (unit_rows * lines[1:2] + lines[2:3]).astype(BF16)
    for copy in qkv_copies:
        copy.wait()
    for i in range(3):
        columns = slice(i * width, (i + 1) * width)
        value = dot(normed[...], weight[:, columns])
        if i != 1:
            value = value + lines[3 + i // 2 : 4 + i // 2]
        qkv[:, columns] = value.astype(BF16)


def enter_all(embed_parts, qkv_parts, patches, maps, starts, bounds, spots):
    whole = pl.BlockSpec(memory_space=pltpu.VMEM)
    anywhere = pl.BlockSpec(memory_space=pl.ANY)
    parts = [*embed_parts.parts, *qkv_parts.parts]
    rows, width = maps.shape[0], 16 * parts[0].shape[1]
    return pl.pallas_call(
        functools.partial(
            enter_kernel, embed_parts.pieces, qkv_parts.pieces, starts, bounds, spots
        ),
        out_shape=(
            jax.ShapeDtypeStruct((rows, width), F32),
            jax.ShapeDtypeStruct((rows, width), BF16),
            jax.ShapeDtypeStruct((rows, 3 * width), BF16),
            jax.ShapeDtypeStruct((16, width), F32),
            jax.ShapeDtypeStruct((rows, 1), F32),
            jax.ShapeDtypeStruct((width, embed_parts.columns - bounds[3]), BF16),
        ),
        in_specs=[pl.BlockSpec(memory_space=pltpu.SMEM)]
        + [whole] * 4
        + [pl.BlockSpec(memory_space=pltpu.HBM)] * len(parts),
        out_specs=[whole] * 6,
        scratch_shapes=[
            pltpu.VMEM((rows, width), BF16),
            pltpu.VMEM((width, embed_parts.columns), BF16),
            pltpu.VMEM((width, 3 * width), BF16),
            pltpu.SemaphoreType.DMA((copies_of(embed_parts.pieces),)),
            pltpu.SemaphoreType.DMA((copies_of(qkv_parts.pieces),)),
        ],
        compiler_params=pltpu.CompilerParams(vmem_limit_bytes=58 * 2**20),
        cost_estimate=BRIEF,
    )(embed_parts.where, *patches, maps, *parts)


def base_gradient_kernel(starts, *refs):
    resizes, sum_ref, out_ref = refs[:3], refs[3], refs[4]
    share = sum_ref.shape[0]
    total = None
    for start, side, resize_ref in zip(starts, SIDES, resizes):
        size = up_to(3 * side * SLOT, 128)
        given = sum_ref[:, start : start + size]
        if side == SLOT:
            own = [given[:, c * side * SLOT : (c + 1) * side * SLOT] for c in range(3)]
        else:
            own = [outer_t(given, slot_table(side, size, c)).astype(BF16) for c in range(3)]
        own = jnp.concatenate(own)
        for term in two_terms(resize_ref[...])[::-1]:
            value = dot(own, term)
            total = value if total is None else total + value
    for c in range(3):
        out_ref[c] = total[c * share : (c + 1) * share]


def base_gradient(resizes, embed_sum, shape, starts):
    whole = pl.BlockSpec(memory_space=pltpu.VMEM)
    return pl.pallas_call(
        functools.partial(base_gradient_kernel, starts),
        out_shape=jax.ShapeDtypeStruct(shape, F32),
        in_specs=[whole] * 4,
        out_specs=whole,
        compiler_params=pltpu.CompilerParams(vmem_limit_bytes=24 * 2**20),
        cost_estimate=BRIEF,
    )(*resizes, embed_sum)


def gelu_pair(value):
    slope = math.sqrt(2 / math.pi)
    square = value * value
    curve = jnp.tanh(value * (slope + (slope * 0.044715) * square))
    half = 0.5 * value
    rise = 0.5 + 0.5 * curve
    bend = (half - half * (curve * curve)) * (slope + (3 * slope * 0.044715) * square)
    return value * rise, rise + bend


ORDER = (0, 8, 4, 12, 2, 10, 6, 14)


def feed_kernel(starts, chunk, where_ref, *refs):
    mixed_ref, embedded_ref, lines_ref, b_up_ref = refs[:4]
    up_parts, down_parts, cotangents, refs = refs[4:12], refs[12:16], refs[16:19], refs[19:]
    finals = refs[:3]
    up_keep, up_give, down_keep, down_give, g_bias_ref = refs[3:8]
    branch_ref, g_mixed_ref, sums_ref = refs[8:11]
    middle, normed, grads, act, grad_up, total, back = refs[11:18]
    w_up, w_down, w_out, g_up, g_down, g_out = refs[18:24]
    up_in, down_in, out_in, up_out, down_out, out_out, one, ends = refs[24:]
    step, steps = pl.program_id(0), pl.num_programs(0)
    rows = middle.shape[0]
    me, other = where_ref[0], where_ref[1]
    slot = lax.rem(step, 2)
    tile = w_up.shape[2]
    up_rows, down_rows = up_keep.shape[2], w_down.shape[1] // 4
    out_columns = up_parts[0].shape[2] - 2 * tile
    count = 16

    def at(index, size):
        return pl.ds(pl.multiple_of(index * size, size), size)

    def load_up(s, half):
        t = lax.bitwise_xor(s, me // 4)
        return [
            pltpu.make_async_copy(
                up_parts[4 * (d % 2) + 2 * half + ORDER.index(d - d % 2) // 4].at[
                    ORDER.index(d - d % 2) % 4, :, at(lax.rem(t, 2), tile)
                ],
                w_up.at[lax.rem(s, 2), at(lax.bitwise_xor(me, d), up_rows), :],
                up_in.at[lax.rem(s, 2), d],
            )
            for d in range(count)
        ]

    def load_down(s):
        copies = []
        for j in range(4):
            place_ = s // 2 + 2 * lax.rem(s, 2)
            copies.append(
                pltpu.make_async_copy(
                    down_parts[2 * (j % 2) + j // 2].at[place_],
                    w_down.at[lax.rem(s, 2), at(lax.bitwise_xor(lax.rem(me, 4), j), down_rows), :],
                    down_in.at[lax.rem(s, 2), j],
                )
            )
        return copies

    def load(s):
        t = lax.bitwise_xor(s, me // 4)
        side = lax.bitwise_xor(t // 2, other)
        for half in range(2):

            @pl.when(side == half)
            def _():
                for copy in load_up(s, half):
                    copy.start()

        for copy in load_down(s):
            copy.start()

    def load_out():
        return [
            pltpu.make_async_copy(
                up_parts[4 * (d % 2) + 2 * half + ORDER.index(d - d % 2) // 4].at[
                    ORDER.index(d - d % 2) % 4, :, pl.ds(2 * tile, out_columns)
                ],
                w_out.at[
                    at(lax.bitwise_xor(me, d), up_rows), at(lax.bitwise_xor(other, half), out_columns)
                ],
                out_in.at[half, d],
            )
            for half in range(2)
            for d in range(count)
        ]

    def store(s):
        t = lax.bitwise_xor(s, me // 4)
        side = lax.bitwise_xor(t // 2, other)
        copies = []
        for d in range(count):
            copies.append(
                pltpu.make_async_copy(
                    g_up.at[lax.rem(s, 2), at(lax.bitwise_xor(me, d), up_rows), :],
                    (up_keep, up_give)[d % 2].at[side, d // 2, :, at(lax.rem(t, 2), tile)],
                    up_out.at[lax.rem(s, 2), d],
                )
            )
        for j in range(4):
            copies.append(
                pltpu.make_async_copy(
                    g_down.at[lax.rem(s, 2), at(lax.bitwise_xor(lax.rem(me, 4), j), down_rows), :],
                    (down_keep, down_give)[j % 2].at[2 * s + j // 2, pl.ds(0, down_rows), :],
                    down_out.at[lax.rem(s, 2), j],
                )
            )
        return copies

    def store_out():
        return [
            pltpu.make_async_copy(
                g_out.at[at(lax.bitwise_xor(me, d), up_rows), :],
                (down_keep, down_give)[d % 2].at[d // 2, pl.ds(down_rows, up_rows), :],
                out_out.at[d],
            )
            for d in range(count)
        ]

    @pl.when(step == 0)
    def _():
        copy = pltpu.make_async_copy(embedded_ref, middle, one.at[0])
        copy.start()
        for first in load_out():
            first.start()
        load(0)
        for i, ref in enumerate(cotangents):
            grads[starts[i] : starts[i + 1], :] = ref[0]
        copy.wait()
        for first in load_out():
            first.wait()
        for first, size in chunks(rows, 416):
            part = slice(first, first + size)
            value = middle[part, :] + dot(mixed_ref[part, :], w_out[...]) + lines_ref[5:6, :]
            middle[part, :] = value
            unit_rows, _ = unit(value)
            normed[part, :] = (unit_rows * lines_ref[6:7, :] + lines_ref[7:8, :]).astype(BF16)
            total[part, :] = value + lines_ref[8:9, :]
            back[part, :] = jnp.zeros((size, back.shape[1]), F32)

    @pl.when(step + 1 < steps)
    def _():
        load(step + 1)

    for copy in load_up(step, 0) + load_down(step):
        copy.wait()

    column = jnp.zeros((1, tile), F32)
    for first, size in chunks(rows, chunk):
        part = slice(first, first + size)
        up = dot(normed[part, :], w_up[slot]) + b_up_ref[...]
        value, slope = gelu_pair(up)
        value = value.astype(BF16)
        act[part, :] = value
        grad = (slope * outer_t(grads[part, :], w_down[slot])).astype(BF16)
        grad_up[part, :] = grad
        column += jnp.sum(grad.astype(F32), axis=0, keepdims=True)
        total[part, :] += dot(value, w_down[slot])
        back[part, :] += outer_t(grad, w_up[slot])
    g_bias_ref[...] = column

    @pl.when(step >= 2)
    def _():
        for copy in store(step - 2):
            copy.wait()

    g_down[slot] = inner_t(act[...], grads[...]).astype(BF16)
    g_up[slot] = inner_t(normed[...], grad_up[...]).astype(BF16)
    for copy in store(step):
        copy.start()

    @pl.when(step == steps - 1)
    def _():
        done = []

        def leave(source, target):
            done.append(pltpu.make_async_copy(source, target, ends.at[len(done)]))
            done[-1].start()

        for i, ref in enumerate(finals):
            part = pl.ds(starts[i], starts[i + 1] - starts[i])
            act[part, :] = total[part, :].astype(BF16)
            leave(act.at[part, :], ref.at[0])
        width = middle.shape[1]
        sums = [jnp.zeros((1, width), F32)] * 4
        for first, size in chunks(rows, 416):
            part = pl.ds(first, size)
            unit_rows, inverse = unit(middle[part, :])
            out = back[part, :]
            down = grads[part, :].astype(F32)
            grad, gain, bias = norm_backward(out, unit_rows, inverse, lines_ref[6:7, :])
            low = (grad + down).astype(BF16)
            normed[part, :] = low
            leave(normed.at[part, :], branch_ref.at[part, :])
            grad_up[part, :] = outer_t(low, w_out[...]).astype(BF16)
            leave(grad_up.at[part, :], g_mixed_ref.at[part, :])
            found = (
                gain[None],
                bias[None],
                jnp.sum(down, axis=0, keepdims=True),
                jnp.sum(low.astype(F32), axis=0, keepdims=True),
            )
            sums = [a + b for a, b in zip(sums, found)]
        g_out[...] = inner_t(mixed_ref[...], normed[...]).astype(BF16)
        for last in store_out():
            last.start()
        sums_ref[...] = jnp.concatenate(sums + [jnp.zeros((4, width), F32)])
        for last in store_out() + store(step - 1) + store(step) + done:
            last.wait()


def feed_all(where, mixed, embedded, lines, b_up, up_parts, down_parts, cotangents, starts, chunk=624):
    rows, width = mixed.shape
    tile = (up_parts[0].shape[2] - width // 2) // 2
    hidden = 4 * tile
    up_rows = up_parts[0].shape[1]
    down_rows = down_parts[0].shape[1]
    fixed = lambda *shape: pl.BlockSpec(
        shape, lambda s, w: (0,) * len(shape), pipeline_mode=pl.Buffered(1)
    )
    whole = lambda *shape: pl.BlockSpec(shape, lambda s, w: (0,) * len(shape))
    mine = pl.BlockSpec((1, tile), lambda s, w: (0, lax.bitwise_xor(s, w[0] // 4)))
    anywhere = pl.BlockSpec(memory_space=pl.ANY)
    like = lambda shape, kind: jax.ShapeDtypeStruct(shape, kind)
    return pl.pallas_call(
        functools.partial(feed_kernel, starts, chunk),
        grid_spec=pltpu.PrefetchScalarGridSpec(
            num_scalar_prefetch=1,
            grid=(4,),
            in_specs=[fixed(rows, width), anywhere, fixed(16, width), mine]
            + [pl.BlockSpec(memory_space=pltpu.HBM)] * 12
            + [fixed(*c.shape) for c in cotangents],
            out_specs=[anywhere] * 7 + [mine, anywhere, anywhere, whole(8, width)],
            scratch_shapes=[
                pltpu.VMEM((rows, width), F32),
                pltpu.VMEM((rows, width), BF16),
                pltpu.VMEM((rows, width), BF16),
                pltpu.VMEM((rows, tile), BF16),
                pltpu.VMEM((rows, tile), BF16),
                pltpu.VMEM((rows, width), F32),
                pltpu.VMEM((rows, width), F32),
                pltpu.VMEM((2, width, tile), BF16),
                pltpu.VMEM((2, tile, width), BF16),
                pltpu.VMEM((width, width), BF16),
                pltpu.VMEM((2, width, tile), BF16),
                pltpu.VMEM((2, tile, width), BF16),
                pltpu.VMEM((width, width), BF16),
                pltpu.SemaphoreType.DMA((2, 16)),
                pltpu.SemaphoreType.DMA((2, 4)),
                pltpu.SemaphoreType.DMA((2, 16)),
                pltpu.SemaphoreType.DMA((2, 16)),
                pltpu.SemaphoreType.DMA((2, 4)),
                pltpu.SemaphoreType.DMA((16,)),
                pltpu.SemaphoreType.DMA((1,)),
                pltpu.SemaphoreType.DMA((3 + 2 * len(chunks(rows, 416)),)),
            ],
        ),
        out_shape=[like(c.shape, BF16) for c in cotangents]
        + [like((2, 8, up_rows, hidden // 2), BF16)] * 2
        + [like((8, down_rows + up_rows, width), BF16)] * 2
        + [
            like((1, hidden), F32),
            like((rows, width), BF16),
            like((rows, width), BF16),
            like((8, width), F32),
        ],
        compiler_params=pltpu.CompilerParams(vmem_limit_bytes=56 * 2**20),
        cost_estimate=BRIEF,
    )(where, mixed, embedded, lines, b_up, *up_parts, *down_parts, *cotangents)


def spread_copies(source, segments, where_ref, sems, first=0):
    me, other = where_ref[0], where_ref[1]
    copies = []
    for start, columns, targets, half, there in segments:
        for d in range(16):
            rows = source.shape[0] // 16
            row = pl.ds(pl.multiple_of(lax.bitwise_xor(me, d) * rows, rows), rows)
            target = targets[d % 2]
            if half is not None:
                target = target.at[lax.bitwise_xor(other, half)]
            copies.append(
                pltpu.make_async_copy(
                    source.at[row, pl.ds(start, columns)],
                    target.at[d // 2, :, pl.ds(there, columns)],
                    sems.at[first + len(copies)],
                )
            )
    return copies


def leave_kernel(pieces, starts, bounds, spots, low_columns, chunk, where_ref, *refs):
    grads, units, branch, lines_ref, given_ref, bias_ref, inverse_ref, map_ref = refs[:8]
    patches, parts, refs = refs[8:11], refs[11 : 11 + len(pieces)], refs[11 + len(pieces) :]
    low_ref, low_outs, high_outs, refs = refs[0], refs[1:3], refs[3:5], refs[5:]
    normed, weight, embed_out, qkv_out, sums, weight_sems, out_sems = refs
    rows, width = low_ref.shape
    weights = place_copies(pieces, parts, weight, where_ref, weight_sems)
    half = embed_out.shape[1] // 2
    quarter = half // 2
    low = low_columns - half
    rest = (3 * width - low) // 2
    segments = [
        (qkv_out, (0, low, low_outs, None, half)),
        (qkv_out, (low, rest, high_outs, 0, quarter)),
        (qkv_out, (low + rest, rest, high_outs, 1, quarter)),
        (embed_out, (0, half, low_outs, None, 0)),
        (embed_out, (half, quarter, high_outs, 0, 0)),
        (embed_out, (half + quarter, quarter, high_outs, 1, 0)),
    ]
    copies = []
    for source, segment in segments:
        copies += spread_copies(source, [segment], where_ref, out_sems, len(copies))
    for copy in weights:
        copy.start()
    normed[...] = (units[...].astype(F32) * lines_ref[1:2, :] + lines_ref[2:3, :]).astype(BF16)
    for i in range(3):
        columns = slice(i * width, (i + 1) * width)
        qkv_out[:, columns] = inner_t(normed[...], grads[i]).astype(BF16)
        for copy in copies[16 * i - 16 : 16 * i] if i < 2 else copies[16:48]:
            copy.start()
    sums[...] = jnp.zeros_like(sums)
    sums[5:6, :] = given_ref[3:4, :]
    sums[6:9, :] = given_ref[:3, :]
    for copy in weights:
        copy.wait()
    totals = [jnp.zeros((1, width), F32)] * 4
    for first, size in chunks(rows, chunk):
        part = slice(first, first + size)
        found = sum(
            outer_t(grads[i, part, :], weight[:, i * width : (i + 1) * width]) for i in range(3)
        )
        grad, gain, bias = norm_backward(
            found, units[part, :].astype(F32), inverse_ref[part, :], lines_ref[1:2, :]
        )
        low_ref[part, :] = (grad + branch[part, :].astype(F32)).astype(BF16)
        found = [gain[None], bias[None]] + [
            jnp.sum(grads[i, part, :].astype(F32), axis=0, keepdims=True) for i in (0, 2)
        ]
        totals = [a + b for a, b in zip(totals, found)]
    for i, value in enumerate(totals):
        sums[i + 1 : i + 2, :] = value
    row = lax.broadcasted_iota(jnp.int32, (16, 128), 0)
    lane = lax.broadcasted_iota(jnp.int32, (16, 128), 1)
    smalls = inner_t(sums[...].astype(BF16), ((lane == row + spots) & (row < 9)).astype(BF16))
    rise = bias_ref.shape[1]
    smalls += dot(bias_ref[...], ((lane == row + spots + 9)[:rise]).astype(BF16))
    started = 48
    for i, patch_ref in enumerate(patches):
        part = slice(starts[i], starts[i + 1])
        size = bounds[i + 1] - bounds[i]
        above, below = two_terms(map_ref[part, :])
        found = inner_t(low_ref[part, :], jnp.concatenate([patch_ref[...], above, below], axis=1))
        embed_out[:, bounds[i] : bounds[i + 1]] = found[:, :size].astype(BF16)
        smalls += found[:, size : size + 128] + found[:, size + 128 :]
        if bounds[i + 1] >= half and started == 48:
            started = 64
            for copy in copies[48:64]:
                copy.start()
    embed_out[:, bounds[3] :] = smalls.astype(BF16)
    for copy in copies[started:]:
        copy.start()
    for copy in copies:
        copy.wait()


def leave_all(
    qkv_parts,
    grad_qkv,
    units,
    branch,
    lines,
    given,
    bias,
    inverse,
    maps,
    patches,
    starts,
    bounds,
    spots,
    low_columns,
    chunk=416,
):
    _, rows, width = grad_qkv.shape
    whole = pl.BlockSpec(memory_space=pltpu.VMEM)
    anywhere = pl.BlockSpec(memory_space=pl.ANY)
    parts = qkv_parts.parts
    columns = bounds[3] + 128
    block = width // 16
    high_columns = (3 * width + columns - low_columns) // 2
    return pl.pallas_call(
        functools.partial(
            leave_kernel, qkv_parts.pieces, starts, bounds, spots, low_columns, chunk
        ),
        out_shape=[jax.ShapeDtypeStruct((rows, width), BF16)]
        + [jax.ShapeDtypeStruct((8, block, low_columns), BF16)] * 2
        + [jax.ShapeDtypeStruct((2, 8, block, high_columns), BF16)] * 2,
        in_specs=[pl.BlockSpec(memory_space=pltpu.SMEM)]
        + [whole] * 11
        + [pl.BlockSpec(memory_space=pltpu.HBM)] * len(parts),
        out_specs=[whole] + [anywhere] * 4,
        scratch_shapes=[
            pltpu.VMEM((rows, width), BF16),
            pltpu.VMEM((width, 3 * width), BF16),
            pltpu.VMEM((width, columns), BF16),
            pltpu.VMEM((width, 3 * width), BF16),
            pltpu.VMEM((16, width), F32),
            pltpu.SemaphoreType.DMA((copies_of(qkv_parts.pieces),)),
            pltpu.SemaphoreType.DMA((96,)),
        ],
        compiler_params=pltpu.CompilerParams(vmem_limit_bytes=44 * 2**20),
        cost_estimate=BRIEF,
    )(
        qkv_parts.where,
        grad_qkv,
        units,
        branch,
        lines,
        given,
        bias,
        inverse,
        maps,
        *patches,
        *parts,
    )


def dot(first, second):
    return jnp.dot(first, second, preferred_element_type=F32)


def inner_t(first, second):
    return lax.dot_general(first, second, (((0,), (0,)), ((), ())), preferred_element_type=F32)


def body(count, pixels, resizes, posmaps, weights, cotangents):
    base_kernel, patch_bias, posemb = weights[:3]
    ln1_gain, ln1_bias, qkv_weight, qv_bias, out_weight, out_bias = weights[3:9]
    ln2_gain, ln2_bias, up_weight, up_bias, down_weight, down_bias = weights[9:]
    channels, base_pixels, share = base_kernel.shape
    width = share * count
    spots = posemb.shape[0]
    where = jnp.stack([lax.axis_index("fsdp"), lax.axis_index("rep")]).astype(jnp.int32)
    tokens = [c.shape[1] for c in cotangents]
    starts = [sum(tokens[:i]) for i in range(4)]
    bits = [2**i for i in range(1, count.bit_length() - 1)]
    inward = [(bit,) for bit in bits]
    outward = inward[::-1]
    turned = inward[:1] + outward[:-1]

    up_per = up_bias.shape[0] // share
    used = spots + 9 + up_per
    bounds = [0]
    for side in SIDES:
        bounds.append(bounds[-1] + up_to(3 * side * SLOT, 128))
    columns = bounds[3] + 128
    vectors = [
        v.reshape(1, -1)
        for v in (
            patch_bias,
            ln1_gain,
            ln1_bias,
            qv_bias[0],
            qv_bias[1],
            out_bias,
            ln2_gain,
            ln2_bias,
            down_bias,
            up_bias,
        )
    ]
    maps = jnp.concatenate(posmaps)
    maps = jnp.concatenate(
        [maps, jnp.ones((maps.shape[0], 1), F32), jnp.zeros((maps.shape[0], 127 - spots), F32)],
        axis=1,
    )

    base_turned = base_kernel.swapaxes(1, 2)
    down_rows = (down_weight.shape[0], out_weight.shape[0])
    up_half, out_half = up_weight.shape[1] // 2, width // 2
    up_block = jnp.concatenate(
        [
            up_weight[:, :up_half],
            out_weight[:, :out_half],
            up_weight[:, up_half:],
            out_weight[:, out_half:],
        ],
        axis=1,
    )
    qkv_shards = Gather(qkv_weight, where, count, outward, split=True).send()
    up_shards = Gather(up_block, where, count, outward, split=True, joined=False).send()
    shards = resize_all(resizes, base_turned, posemb.T, vectors, bounds, columns)
    embed_low = Gather(shards[0], where, count, outward).send()
    embed_high = Gather(shards[1], where, count, outward).send()
    held = go_on((pixels, maps, *shards), qkv_shards)
    held = together(held, embed_low, embed_high)
    held = go_on(held, qkv_shards)
    held = together(held, embed_low, embed_high)
    held, down_weight = after(held, down_weight)
    down_shards = Gather(down_weight, where, count, outward, joined=False).send()
    held = together(held, qkv_shards, up_shards)
    pixels, maps, *_ = held
    patches = patch_all(pixels)
    patches, maps = finish(
        (patches, maps), embed_low, embed_high, qkv_shards, down_shards, up_shards
    )
    for chain in (embed_low, embed_high, qkv_shards, down_shards):
        chain.send()
    patches, maps = complete((patches, maps), embed_low, embed_high, qkv_shards)
    up_shards.send()
    w_qkv = Parts([qkv_shards], where, count)
    w_embed = Parts([embed_low, embed_high], where, count)
    embedded, units, qkv, lines, inverse, columns_small = enter_all(
        w_embed, w_qkv, patches, maps, starts, bounds, spots
    )
    qkv = together(qkv, up_shards, down_shards)
    mixed, totals = attend_forward(qkv, starts)
    mixed = together(mixed, up_shards, down_shards)
    mixed = complete(mixed, up_shards, down_shards)
    w_up = Parts([up_shards], where, count)
    w_down = Parts([down_shards], where, count)
    b_up = columns_small[:, spots + 9 : used].astype(F32)
    b_up = b_up.reshape(count, share, up_per).swapaxes(1, 2).reshape(1, -1)
    (
        *results,
        up_keep,
        up_give,
        down_keep,
        down_give,
        grad_b_up,
        branch,
        grad_mixed,
        sums,
    ) = feed_all(
        w_up.where, mixed, embedded, lines, b_up, w_up.quarters(2), w_down.quarters(1), cotangents, starts
    )
    rows16 = (down_rows[0] * count // 16, down_rows[1] * count // 16)
    down_sums = Scatter(
        *ordered(down_keep, down_give, where, count, rows16), where, count, inward
    ).send()
    up_sums = Scatter(
        *ordered(up_keep, up_give, where, count, split=True), where, count, inward, split=True
    ).send()
    grad_qkv = attend_backward(qkv, mixed, totals, grad_mixed, starts[:2])
    grad_qkv = together(grad_qkv, down_sums, up_sums)
    grad_qkv = attend_backward(qkv, mixed, totals, grad_mixed, starts[1:], (grad_qkv,))
    grad_qkv = together(grad_qkv, down_sums, up_sums)
    half = columns // 2
    low_columns = half + 5 * width // 3
    grad_low, *shares = leave_all(
        w_qkv,
        grad_qkv,
        units,
        branch,
        lines,
        sums,
        grad_b_up.reshape(width, up_per).astype(BF16),
        inverse,
        maps,
        patches,
        starts,
        bounds,
        spots,
        low_columns,
    )
    grad_low, *arrived = after((grad_low, *shares), *down_sums.sent, *up_sums.sent)
    grad_low, *shares = grad_low
    low_sums = Scatter(*ordered(*shares[:2], where, count), where, count, inward).send()
    high_sums = Scatter(
        *ordered(*shares[2:], where, count, split=True), where, count, inward, split=True
    ).send()
    for chain in (down_sums, up_sums):
        chain.sent, arrived = arrived[: len(chain.sent)], arrived[len(chain.sent) :]
    grad_low = together(grad_low, down_sums, up_sums)
    grad_low = together(grad_low, low_sums)
    grad_low = together(grad_low, high_sums)
    pixel_grads = unpatch_all(grad_low, w_embed, starts, bounds, [p.shape[2] for p in pixels])
    pixel_grads = together(pixel_grads, down_sums, up_sums)
    pixel_grads = go_on(pixel_grads, high_sums, low_sums, high_sums, low_sums, high_sums)
    pixel_grads = go_on(pixel_grads, up_sums, low_sums)
    pixel_grads = complete(pixel_grads, down_sums, high_sums, up_sums, low_sums)

    low, high = low_sums.result, high_sums.result
    quarter = half // 2
    embed_sum = jnp.concatenate([low[:, :half]] + [h[:, :quarter] for h in high], axis=1)
    qkv_sum = jnp.concatenate([low[:, half:]] + [h[:, quarter:] for h in high], axis=1).astype(F32)
    down_sum = down_sums.result.astype(F32)
    up_sum = jnp.concatenate(up_sums.result, axis=1).astype(F32)
    base_grad = base_gradient(resizes, embed_sum, base_turned.shape, bounds).swapaxes(1, 2)
    small_sum = embed_sum[:, bounds[3] : bounds[3] + used].astype(F32)
    vectors = small_sum[:, spots : spots + 9].T
    return (
        *results,
        *pixel_grads,
        base_grad,
        vectors[0],
        small_sum[:, :spots].T,
        vectors[1],
        vectors[2],
        qkv_sum,
        vectors[3:5],
        down_sum[down_rows[0] :],
        vectors[5],
        vectors[6],
        vectors[7],
        up_sum,
        small_sum[:, spots + 9 :].reshape(-1),
        down_sum[: down_rows[0]],
        vectors[8],
    )


def solution(mesh):
    count = mesh.shape["fsdp"]

    def run(*args):
        return body(count, args[:3], args[3:6], args[6:9], args[9:24], args[24:])

    images = ("rep", "fsdp")
    weight_specs = (
        P(None, None, "fsdp"),
        P("fsdp"),
        P(None, "fsdp"),
        P("fsdp"),
        P("fsdp"),
        P("fsdp", None),
        P(None, "fsdp"),
        P("fsdp", None),
        P("fsdp"),
        P("fsdp"),
        P("fsdp"),
        P("fsdp", None),
        P("fsdp"),
        P("fsdp", None),
        P("fsdp"),
    )
    return jax.shard_map(
        run,
        mesh=mesh,
        in_specs=(P(images, None, None, None),) * 3
        + (P(),) * 6
        + weight_specs
        + (P(images, None, None),) * 3,
        out_specs=(P(images, None, None),) * 3
        + (P(images, None, None, None),) * 3
        + weight_specs,
        check_vma=False,
    )
```

```python
import functools
import math

import jax
import jax.numpy as jnp
from jax import lax
from jax.experimental import pallas as pl
from jax.experimental.pallas import tpu as pltpu
from jax.sharding import PartitionSpec as P

HEADS = 12
HEAD = 64
SIDES = (10, 12, 16)
SLOT = 16
F32 = jnp.float32
BF16 = jnp.bfloat16
BRIEF = pl.CostEstimate(flops=1, bytes_accessed=1, transcendentals=0)


def swap(value, axis, size, bit):
    return lax.ppermute(value, axis, [(i, i ^ bit) for i in range(size)])


def after(first, *rest):
    return lax.optimization_barrier((first, *rest))


class Gather:
    def __init__(self, shard, where, count, steps, split=False, joined=True):
        self.count, self.split, self.columns, self.joined = count, split, shard.shape[1], joined
        if split:
            width = shard.shape[1] // 2
            shard = lax.dynamic_slice_in_dim(shard, where[1] * width, width, 1)
        self.held = [(shard[None], [0])]
        self.steps = list(steps) + (["rep"] if split else []) + ["core"]
        self.step = None
        self.pieces = []
        self.ready = [shard[None]]

    def prepare(self):
        if not self.steps:
            self.ready = []
            return
        if self.steps[0] == "core":
            if self.joined:
                size = len(self.held) // (2 if self.split else 1)
                self.held = [
                    self.join(self.held[i : i + size]) for i in range(0, len(self.held), size)
                ]
        elif self.steps[0] != "rep" and len(self.held) > 1:
            self.held = [self.join(self.held)]
        self.ready = [blocks for blocks, *_ in self.held]
        if self.steps[0] == "rep":
            self.ready = self.ready[1:2]

    def join(self, held):
        offsets = [o for h in held for o in h[1]]
        return (join([h[0] for h in held]) if len(held) > 1 else held[0][0], offsets, *held[0][2:])

    def renew(self, ready):
        if self.steps and self.steps[0] == "rep":
            self.held = [self.held[0], (ready[0], *self.held[1][1:]), *self.held[2:]]
        elif ready:
            self.held = [(blocks, *h[1:]) for blocks, h in zip(ready, self.held)]
        self.ready = ready

    def send(self):
        self.step, self.steps = self.steps[0], self.steps[1:]
        if self.step in ("rep", "core"):
            axis, size = ("rep", 2) if self.step == "rep" else ("fsdp", self.count)
            self.sent = [swap(blocks, axis, size, 1) for blocks in self.ready]
        else:
            self.sent = [swap(self.ready[0], "fsdp", self.count, offset) for offset in self.step]
            if self.steps[0] == "rep":
                self.sent.append(swap(self.ready[0], "rep", 2, 1))
        return self

    def take(self, arrived):
        if self.step == "rep":
            own, given, early = self.held
            self.held = [
                (*own, 0),
                (*given, 0),
                (early[0], own[1], 1),
                (arrived[0], given[1], 1),
            ]
        elif self.step == "core":
            held = [h if len(h) == 3 else (*h, None) for h in self.held]
            self.held = held + [
                (blocks, [o ^ 1 for o in h[1]], h[2]) for blocks, h in zip(arrived, held)
            ]
        else:
            offsets = self.held[0][1]
            self.held = self.held + [
                (blocks, [o ^ offset for o in offsets])
                for blocks, offset in zip(arrived, self.step)
            ]
            if self.steps[0] == "rep":
                self.held.append((arrived[-1], offsets))


def finish(anchor, *chains):
    sizes = [len(chain.sent) for chain in chains]
    anchor, *flat = after(anchor, *[part for chain in chains for part in chain.sent])
    for chain, size in zip(chains, sizes):
        chain.take(flat[:size])
        chain.prepare()
        flat = flat[size:]
        chain.sent = []
    sizes = [len(chain.ready) for chain in chains]
    anchor, *flat = after(anchor, *[part for chain in chains for part in chain.ready])
    for chain, size in zip(chains, sizes):
        chain.renew(flat[:size])
        flat = flat[size:]
    return anchor


def together(anchor, *chains):
    anchor = finish(anchor, *chains)
    for chain in chains:
        if chain.steps:
            chain.send()
    return anchor


def go_on(anchor, *chains):
    for chain in chains:
        anchor = together(anchor, chain)
    return anchor


def complete(anchor, *chains):
    chains = [chain for chain in chains if chain.sent]
    while chains:
        left = [chain for chain in chains if chain.steps]
        anchor = go_on(anchor, *chains)
        chains = left
    return anchor


def place_copies(pieces, parts, whole, where_ref, sems):
    me, other = where_ref[0], where_ref[1]
    copies = []
    for part, (offsets, half, first, columns) in zip(parts, pieces):
        rows = part.shape[1]
        for k, offset in enumerate(offsets):
            row = pl.ds(pl.multiple_of(lax.bitwise_xor(me, offset) * rows, rows), rows)
            if half is None:
                target = whole.at[row, pl.ds(first, columns)]
            else:
                width = columns // 2
                start = pl.multiple_of(first + lax.bitwise_xor(other, half) * width, 128)
                target = whole.at[row, pl.ds(start, width)]
            copies.append(pltpu.make_async_copy(part.at[k], target, sems.at[len(copies)]))
    return copies


def copies_of(pieces):
    return sum(len(offsets) for offsets, *_ in pieces)


def place_kernel(pieces, me_ref, *refs):
    parts, whole, sems = refs[: len(pieces)], refs[len(pieces)], refs[len(pieces) + 1]
    me, other = me_ref[0], me_ref[1]
    copies = []
    for part, (offsets, half, first, columns) in zip(parts, pieces):
        for k, offset in enumerate(offsets):
            row = lax.bitwise_xor(me, offset)
            if half is None:
                target = whole.at[row, :, pl.ds(first, columns)]
            else:
                width = columns // 2
                start = pl.multiple_of(first + lax.bitwise_xor(other, half) * width, 128)
                target = whole.at[row, :, pl.ds(start, width)]
            copies.append(pltpu.make_async_copy(part.at[k], target, sems.at[len(copies)]))
    for copy in copies:
        copy.start()
    for copy in copies:
        copy.wait()


def place(gathers, where, count):
    parts, pieces = parts_of(gathers)
    rows, kind = parts[0].shape[1], parts[0].dtype
    columns = sum(g.columns for g in gathers)
    whole = pl.pallas_call(
        functools.partial(place_kernel, pieces),
        out_shape=jax.ShapeDtypeStruct((count, rows, columns), kind),
        in_specs=[pl.BlockSpec(memory_space=pltpu.SMEM)]
        + [pl.BlockSpec(memory_space=pl.ANY)] * len(pieces),
        out_specs=pl.BlockSpec(memory_space=pltpu.VMEM),
        scratch_shapes=[pltpu.SemaphoreType.DMA((copies_of(pieces),))],
        compiler_params=pltpu.CompilerParams(vmem_limit_bytes=16 * 2**20),
        cost_estimate=BRIEF,
    )(where, *parts)
    return whole.reshape(count * rows, columns)


def parts_of(gathers):
    parts, pieces, first = [], [], 0
    for g in gathers:
        for blocks, offsets, half in g.held:
            parts.append(blocks)
            pieces.append((tuple(offsets), half, first, g.columns))
        first += g.columns
    return parts, pieces


def regroup(blocks, rows, count):
    parts, first = [], 0
    for size in rows:
        part = blocks[:, first : first + size]
        parts.append(part.reshape(count, -1, blocks.shape[2]))
        first += size
    return jnp.concatenate(parts, axis=1)


class Parts:
    def __init__(self, gathers, where, count, rows=None):
        self.columns = sum(g.columns for g in gathers)
        self.where = where
        if count == 16:
            self.parts, self.pieces = parts_of(gathers)
        else:
            whole = place(gathers, where, count).reshape(count, -1, self.columns)
            rows = rows or (whole.shape[1],)
            self.parts = [regroup(whole, rows, 16)]
            self.pieces = [(tuple(range(16)), None, 0, self.columns)]
            self.where = jnp.zeros_like(where)

    def quarters(self, halves):
        if len(self.parts) > 1:
            assert len(self.parts) == 4 * halves
            assert self.pieces[0][0] + self.pieces[1][0] == ORDER
            return self.parts
        size = self.columns // halves
        return [
            jnp.stack([self.parts[0][o + core, :, h * size : (h + 1) * size] for o in quarter])
            for core in range(2)
            for h in range(halves)
            for quarter in (ORDER[:4], ORDER[4:])
        ]


def ordered(keep, give, where, count, rows=None, split=False):
    if count == 16:
        return keep, give
    if not split:
        keep, give = keep[None], give[None]
    whole = jnp.stack([keep, give], axis=2)
    halves, blocks, _, size, columns = whole.shape
    whole = whole.reshape(halves, 2 * blocks, size, columns)
    whole = jnp.concatenate([whole[h] for h in range(halves)], axis=2)
    columns = whole.shape[2]
    whole = regroup(whole, rows or (size,), count).reshape(-1, columns)
    found = take([whole], [(0, 0, columns)], where, count, split)
    if split:
        return jnp.stack(found[:2]), jnp.stack(found[2:])
    return found


def take_kernel(count, split, segments, me_ref, *refs):
    inputs = max(which for which, *_ in segments) + 1
    wholes, outs, sems = refs[:inputs], refs[inputs:-1], refs[-1]
    me, other = me_ref[0], me_ref[1]
    half = outs[0].shape[2]

    def copies(switch):
        found = []
        for which, start, columns, first in segments:
            for d in range(count):
                source = wholes[which].at[lax.bitwise_xor(me, d), :, pl.ds(start, columns)]
                side = (first // half) ^ switch
                target = outs[2 * (d % 2) + side] if split else outs[d % 2]
                target = target.at[d // 2, :, pl.ds(first % half, columns)]
                found.append(pltpu.make_async_copy(source, target, sems.at[len(found)]))
        return found

    def run(switch):
        found = copies(switch)
        for copy in found:
            copy.start()
        for copy in found:
            copy.wait()

    if split:
        for switch in range(2):
            pl.when(other == switch)(functools.partial(run, switch))
    else:
        run(0)


def take(wholes, segments, where, count, split):
    rows = wholes[0].shape[0] // count
    blocks = [w.reshape(count, rows, w.shape[1]) for w in wholes]
    columns = sum(segment[2] for segment in segments)
    half = columns // 2 if split else columns
    ends, first = [], 0
    for which, start, size in segments:
        while size:
            room = min(size, half - first % half)
            ends.append((which, start, room, first))
            first, start, size = first + room, start + room, size - room
    shape = jax.ShapeDtypeStruct((count // 2, rows, half), wholes[0].dtype)
    outs = 4 if split else 2
    return pl.pallas_call(
        functools.partial(take_kernel, count, split, ends),
        out_shape=(shape,) * outs,
        in_specs=[pl.BlockSpec(memory_space=pltpu.SMEM)]
        + [pl.BlockSpec(memory_space=pltpu.VMEM)] * len(blocks),
        out_specs=[pl.BlockSpec(memory_space=pl.ANY)] * outs,
        scratch_shapes=[pltpu.SemaphoreType.DMA((count * len(ends),))],
        compiler_params=pltpu.CompilerParams(vmem_limit_bytes=16 * 2**20),
        cost_estimate=BRIEF,
    )(where, *blocks)


def add(*values):
    return sum(value.astype(F32) for value in values).astype(BF16)


def join_kernel(*refs):
    *parts, whole = refs
    first = 0
    for part in parts:
        whole[first : first + part.shape[0]] = part[...]
        first += part.shape[0]


def join(parts):
    blocks = sum(part.shape[0] for part in parts)
    whole = pl.BlockSpec(memory_space=pltpu.VMEM)
    return pl.pallas_call(
        join_kernel,
        out_shape=jax.ShapeDtypeStruct((blocks, *parts[0].shape[1:]), parts[0].dtype),
        in_specs=[whole] * len(parts),
        out_specs=whole,
        compiler_params=pltpu.CompilerParams(vmem_limit_bytes=16 * 2**20),
        cost_estimate=BRIEF,
    )(*parts)


def merge_kernel(groups, parts, *refs):
    outs = refs[parts:]
    for group, out in zip(groups, outs):
        for j, index in enumerate(group):
            out[j] = sum(ref[index].astype(F32) for ref in refs[:parts]).astype(BF16)


def merge(parts, groups):
    rest = parts[0].shape[-2:]
    whole = pl.BlockSpec(memory_space=pltpu.VMEM)
    return pl.pallas_call(
        functools.partial(merge_kernel, groups, len(parts)),
        out_shape=[jax.ShapeDtypeStruct((len(group), *rest), BF16) for group in groups],
        in_specs=[whole] * len(parts),
        out_specs=[whole] * len(groups),
        compiler_params=pltpu.CompilerParams(vmem_limit_bytes=24 * 2**20),
        cost_estimate=BRIEF,
    )(*parts)


class Scatter:
    def __init__(self, keep, give, where, count, steps, split=False):
        self.where, self.count, self.split = where, count, split
        self.keep, self.give = keep, give
        self.steps = ["core"] + (["half"] if split else []) + list(steps) + ["rep"]
        self.offsets = list(range(0, count, 2))
        self.step = None

        self.ready = [give]

    def prepare(self):
        pass

    def renew(self, ready):
        self.ready = ready

    def send(self):
        self.step, self.steps = self.steps[0], self.steps[1:]
        if self.step in ("half", "rep"):
            self.sent = [swap(self.ready[0], "rep", 2, 1)]
        else:
            offsets = [1] if self.step == "core" else self.step
            self.sent = [
                swap(part, "fsdp", self.count, offset)
                for part, offset in zip(self.ready, offsets)
            ]
        return self

    def share_out(self, parts):
        step = self.steps[0]
        if step == "rep":
            self.held = merge(parts, [[0]])[0][0]
            self.ready = [self.held]
            return
        mask = 0
        for offset in step:
            mask |= offset
        stay = [o for o in self.offsets if o & mask == 0]
        groups = [[self.offsets.index(o | offset) for o in stay] for offset in (0, *step)]
        self.staying, *self.ready = merge(parts, groups)
        self.offsets = stay

    def take(self, arrived):
        if self.step == "core" and self.split:
            blocks = len(self.offsets)
            flat = [a.reshape(2 * blocks, *a.shape[2:]) for a in (self.keep, *arrived)]
            away, self.staying = merge(
                flat, [list(range(blocks, 2 * blocks)), list(range(blocks))]
            )
            self.ready = [away]
        elif self.step == "core":
            self.share_out([self.keep, *arrived])
        elif self.step == "rep":
            if self.split:
                low = self.where[1] == 0
                self.result = [
                    jnp.where(low, self.held, arrived[0]),
                    jnp.where(low, arrived[0], self.held),
                ]
            else:
                self.result = add(self.held, arrived[0])
            self.ready = []
        else:
            self.share_out([self.staying, *arrived])


def up_to(value, unit):
    return -(-value // unit) * unit

def swap_chunks(lines):
    chunk = lax.broadcasted_iota(jnp.int32, lines[0].shape, 1) // SLOT
    for step in (1, 2, 4):
        stays = (chunk & step) == 0
        for i in range(8):
            if i & step == 0:
                low, high = lines[i], lines[i + step]
                lines[i] = jnp.where(stays, low, pltpu.roll(high, step * SLOT, 1))
                lines[i + step] = jnp.where(stays, pltpu.roll(low, 128 - step * SLOT, 1), high)
    return lines

def spread(side, grid, columns):
    pixel = lax.broadcasted_iota(jnp.int32, (grid * side, columns), 0)
    column = lax.broadcasted_iota(jnp.int32, (grid * side, columns), 1)
    place = column % SLOT
    return ((pixel == column // SLOT * side + place) & (place < side)).astype(BF16)

def patch_kernel(*refs):
    pixels, outs, rows_ref, flat_ref = refs[:3], refs[3:6], refs[6], refs[7]
    for side, pixel_ref, out in zip(SIDES, pixels, outs):
        high = pixel_ref.shape[2]
        grid = high // side
        columns = up_to(grid * SLOT, 128)
        table = None if side == SLOT else spread(side, grid, columns)
        for c in range(3):
            picture = pixel_ref[0, c]
            if table is None:
                wide = picture.astype(F32)
            else:
                wide = jnp.dot(picture, table, preferred_element_type=F32)
            for block in range(columns // 128):
                rows_ref[3 * c + block, :high, :] = wide[:, 128 * block:128 * block + 128]
        slots = 3 * side
        for group in range(out.shape[1] // 128):
            for block in range(columns // 128):
                lines = []
                for q in range(8 * group, 8 * group + 8):
                    if q < slots:
                        lines.append(rows_ref[q // side * 3 + block, pl.ds(q % side, grid, stride=side), :])
                    else:
                        lines.append(jnp.zeros((grid, 128), F32))
                lines = swap_chunks(lines)
                for g in range(8):
                    if 8 * block + g < grid:
                        flat_ref[group, pl.ds(8 * block + g, grid, stride=grid), :] = lines[g]
        for group in range(out.shape[1] // 128):
            out[:, 128 * group:128 * group + 128] = flat_ref[group, :grid * grid, :].astype(BF16)

def patch_all(pixels):
    shapes = []
    for picture, side in zip(pixels, SIDES):
        grid = picture.shape[2] // side
        shapes.append(jax.ShapeDtypeStruct((grid * grid, up_to(3 * side * SLOT, 128)), BF16))
    high = max(p.shape[2] for p in pixels)
    return pl.pallas_call(
        patch_kernel,
        out_shape=shapes,
        in_specs=[pl.BlockSpec(memory_space=pltpu.VMEM)] * 3,
        out_specs=[pl.BlockSpec(memory_space=pltpu.VMEM)] * 3,
        scratch_shapes=[pltpu.VMEM((9, high, 128), F32), pltpu.VMEM((max(s.shape[1] for s in shapes) // 128, max(s.shape[0] for s in shapes), 128), F32)],
        compiler_params=pltpu.CompilerParams(vmem_limit_bytes=40 * 2**20),
        cost_estimate=BRIEF,
    )(*pixels)

def unpatch_kernel(pieces, starts, bounds, where_ref, grad_ref, *refs):
    parts, refs = refs[: len(pieces)], refs[len(pieces) :]
    outs, flat_ref, rows_ref, kernel_ref, sems = refs[:3], *refs[3:]
    copies = place_copies(pieces, parts, kernel_ref, where_ref, sems)
    for copy in copies:
        copy.start()
    for copy in copies:
        copy.wait()
    for i, side in enumerate(SIDES):
        out = outs[i]
        high = out.shape[2]
        grid = high // side
        columns = up_to(grid * SLOT, 128)
        width = bounds[i + 1] - bounds[i]
        grads = grad_ref[starts[i]:starts[i + 1], :]
        flat = jnp.dot(grads, kernel_ref[:, bounds[i]:bounds[i + 1]], preferred_element_type=F32)
        for group in range(width // 128):
            flat_ref[group, :grid * grid, :] = flat[:, 128 * group:128 * group + 128]
        slots = 3 * side
        for group in range(width // 128):
            for block in range(columns // 128):
                lines = []
                for g in range(8):
                    if 8 * block + g < grid:
                        lines.append(flat_ref[group, pl.ds(8 * block + g, grid, stride=grid), :])
                    else:
                        lines.append(jnp.zeros((grid, 128), F32))
                lines = swap_chunks(lines)
                for q in range(8 * group, min(8 * group + 8, slots)):
                    rows_ref[q // side * 3 + block, pl.ds(q % side, grid, stride=side), :] = lines[q % 8]
        table = None if side == SLOT else spread(side, grid, columns)
        for c in range(3):
            picture = jnp.concatenate([rows_ref[3 * c + block, :high, :] for block in range(columns // 128)], axis=1).astype(BF16)
            if table is not None:
                picture = lax.dot_general(picture, table, (((1,), (1,)), ((), ())), preferred_element_type=F32).astype(BF16)
            out[0, c] = picture

def unpatch_all(grads, embed_parts, starts, bounds, sides):
    high = max(sides)
    whole = pl.BlockSpec(memory_space=pltpu.VMEM)
    parts = embed_parts.parts
    return pl.pallas_call(
        functools.partial(unpatch_kernel, embed_parts.pieces, starts, bounds),
        out_shape=[jax.ShapeDtypeStruct((1, 3, s, s), BF16) for s in sides],
        in_specs=[pl.BlockSpec(memory_space=pltpu.SMEM), whole]
        + [pl.BlockSpec(memory_space=pltpu.HBM)] * len(parts),
        out_specs=[whole] * 3,
        scratch_shapes=[
            pltpu.VMEM(
                (
                    max(e - s for s, e in zip(bounds, bounds[1:])) // 128,
                    max(e - s for s, e in zip(starts, starts[1:])),
                    128,
                ),
                F32,
            ),
            pltpu.VMEM((9, high, 128), F32),
            pltpu.VMEM((grads.shape[1], embed_parts.columns), BF16),
            pltpu.SemaphoreType.DMA((copies_of(embed_parts.pieces),)),
        ],
        compiler_params=pltpu.CompilerParams(vmem_limit_bytes=32 * 2**20),
        cost_estimate=BRIEF,
    )(embed_parts.where, grads, *parts)


def unit(values):
    mean_row = jnp.mean(values, axis=-1, keepdims=True)
    centred = values - mean_row
    inverse = lax.rsqrt(jnp.mean(centred * centred, axis=-1, keepdims=True) + 1e-06)
    return centred * inverse, inverse


def norm_backward(grad_out, unit_rows, inverse, gain):
    grad_unit = grad_out * gain
    inner = jnp.mean(grad_unit * unit_rows, axis=-1, keepdims=True)
    grad_in = inverse * (
        grad_unit - jnp.mean(grad_unit, axis=-1, keepdims=True) - unit_rows * inner
    )
    return grad_in, jnp.sum(grad_out * unit_rows, axis=0), jnp.sum(grad_out, axis=0)


def chunks(total, most):
    pieces = -(-total // most)
    size = -(-total // pieces)
    size = -(-size // 16) * 16
    return [(s, min(size, total - s)) for s in range(0, total, size)]

def outer_t(first, second):
    return lax.dot_general(first, second, (((1,), (1,)), ((), ())), preferred_element_type=F32)

def attend_kernel(starts, chunk, q_ref, k_ref, v_ref, *refs):
    pair = pl.program_id(0)
    mixed_ref, total_ref = refs[-2:]
    if len(refs) > 2:
        mixed_ref[: starts[0], :] = refs[0][: starts[0], :]

    @pl.when(pair == 0)
    def _():
        total_ref[...] = refs[1][...] if len(refs) > 2 else jnp.zeros_like(total_ref)

    for begin, end in zip(starts, starts[1:]):
        keys, values = k_ref[begin:end, :], v_ref[begin:end, :]
        for offset, size in chunks(end - begin, chunk):
            rows = slice(begin + offset, begin + offset + size)
            queries = q_ref[rows, :] * (HEAD ** -0.5)
            lane = lax.broadcasted_iota(jnp.int32, (size, 128), 1)
            mixed, totals = [], []
            for head in range(2):
                own = (lane < HEAD) if head == 0 else (lane >= HEAD)
                scores = outer_t(jnp.where(own, queries, jnp.zeros_like(queries)), keys)
                top = jnp.max(scores, axis=1, keepdims=True)
                expo = jnp.exp(scores - top)
                total = jnp.sum(expo, axis=1, keepdims=True)
                out = jnp.dot(expo.astype(BF16), values, preferred_element_type=F32)
                mixed.append(out / total)
                totals.append(top + jnp.log(total))
            mixed_ref[rows, :] = jnp.where(lane < HEAD, mixed[0], mixed[1]).astype(BF16)
            held = total_ref[rows, :]
            held = jnp.where(lane == 2 * pair, totals[0], held)
            total_ref[rows, :] = jnp.where(lane == 2 * pair + 1, totals[1], held)

def attend_forward(qkv, starts, done=(), chunk=576):
    rows, width = qkv.shape[0], qkv.shape[1] // 3
    pairs = width // 128
    block = lambda first: pl.BlockSpec((rows, 128), lambda j: (0, first * pairs + j))
    return pl.pallas_call(
        functools.partial(attend_kernel, starts, chunk),
        grid=(pairs,),
        out_shape=(jax.ShapeDtypeStruct((rows, width), BF16), jax.ShapeDtypeStruct((rows, 128), F32)),
        in_specs=[block(0), block(1), block(2)]
        + [block(0), pl.BlockSpec((rows, 128), lambda j: (0, 0))][: len(done)],
        out_specs=[pl.BlockSpec((rows, 128), lambda j: (0, j)), pl.BlockSpec((rows, 128), lambda j: (0, 0))],
        compiler_params=pltpu.CompilerParams(vmem_limit_bytes=60 * 2**20),
        cost_estimate=BRIEF,
    )(qkv, qkv, qkv, *done)

def terms(value):
    first = value.astype(BF16)
    rest = value - first.astype(F32)
    second = rest.astype(BF16)
    return first, second, (rest - second.astype(F32)).astype(BF16)

def attend_back_kernel(starts, chunk, q_ref, k_ref, v_ref, mixed_ref, grad_ref, total_ref, *refs):
    pair = pl.program_id(0)
    *done, out_ref, left, right, acc = refs
    if done:
        out_ref[:, : starts[0], :] = done[0][...]
    scale = HEAD ** -0.5
    zero = jnp.zeros((), BF16)
    for begin, end in zip(starts, starts[1:]):
        size = end - begin
        for offset, part in chunks(size, chunk):
            rows = slice(begin + offset, begin + offset + part)
            lane = lax.broadcasted_iota(jnp.int32, (part, 128), 1)
            queries, grads = q_ref[rows, :] * scale, grad_ref[rows, :]
            product = grads.astype(F32) * mixed_ref[rows, :].astype(F32)
            total_all = total_ref[rows, :]
            for head in range(2):
                own = (lane < HEAD) if head == 0 else (lane >= HEAD)
                free = HEAD * (1 - head)
                inner = jnp.sum(jnp.where(own, product, 0.0), axis=1, keepdims=True)
                total = jnp.sum(jnp.where(lane == 2 * pair + head, total_all, 0.0), axis=1, keepdims=True)
                for target, value, line in ((left, queries, total), (right, grads, inner)):
                    wide = jnp.where(own, value, zero)
                    for i, term in enumerate(terms(line)):
                        wide = jnp.where(lane == free + i, term, wide)
                    target[head, offset:offset + part, :] = wide
        queries, grads = q_ref[begin:end, :], grad_ref[begin:end, :]
        acc[...] = jnp.zeros_like(acc)
        for offset, part in chunks(size, chunk):
            rows = slice(begin + offset, begin + offset + part)
            lane = lax.broadcasted_iota(jnp.int32, (part, 128), 1)
            keys, values = k_ref[rows, :], v_ref[rows, :]
            grad_key, grad_value = [], []
            for head in range(2):
                own = (lane < HEAD) if head == 0 else (lane >= HEAD)
                free = HEAD * (1 - head)
                minus = jnp.where((lane >= free) & (lane < free + 3), -jnp.ones((), BF16), zero)
                scores = outer_t(jnp.where(own, keys, minus), left[head, :size, :])
                probs = jnp.exp(scores)
                grad_scores = outer_t(jnp.where(own, values, minus), right[head, :size, :])
                grad_scores = (probs * grad_scores).astype(BF16)
                grad_value.append(jnp.dot(probs.astype(BF16), grads, preferred_element_type=F32))
                grad_key.append(jnp.dot(grad_scores, queries, preferred_element_type=F32))
                acc[head, :size, :] += lax.dot_general(grad_scores, keys, (((0,), (0,)), ((), ())), preferred_element_type=F32)
            out_ref[1, rows, :] = (jnp.where(lane < HEAD, *grad_key) * scale).astype(BF16)
            out_ref[2, rows, :] = jnp.where(lane < HEAD, *grad_value).astype(BF16)
        lane = lax.broadcasted_iota(jnp.int32, (size, 128), 1)
        out_ref[0, begin:end, :] = (jnp.where(lane < HEAD, acc[0, :size, :], acc[1, :size, :]) * scale).astype(BF16)

def attend_backward(qkv, mixed, totals, grad_mixed, starts, done=(), chunk=400):
    rows, width = starts[-1], mixed.shape[1]
    pairs = width // 128
    longest = max(e - s for s, e in zip(starts, starts[1:]))
    block = lambda first: pl.BlockSpec((rows, 128), lambda j: (0, first * pairs + j))
    return pl.pallas_call(
        functools.partial(attend_back_kernel, starts, chunk),
        grid=(pairs,),
        out_shape=jax.ShapeDtypeStruct((3, rows, width), BF16),
        in_specs=[block(0), block(1), block(2), block(0), block(0)]
        + [pl.BlockSpec((rows, 128), lambda j: (0, 0))]
        + [pl.BlockSpec((3, starts[0], 128), lambda j: (0, 0, j))][: len(done)],
        out_specs=pl.BlockSpec((3, rows, 128), lambda j: (0, 0, j)),
        scratch_shapes=[
            pltpu.VMEM((2, longest, 128), BF16),
            pltpu.VMEM((2, longest, 128), BF16),
            pltpu.VMEM((2, longest, 128), F32),
        ],
        compiler_params=pltpu.CompilerParams(vmem_limit_bytes=24 * 2**20),
        cost_estimate=BRIEF,
    )(qkv, qkv, qkv, mixed, grad_mixed, totals, *done)


def slot_table(side, size, c):
    pixel = lax.broadcasted_iota(jnp.int32, (side * side, size), 0)
    column = lax.broadcasted_iota(jnp.int32, (side * side, size), 1)
    row, spot = column // SLOT - c * side, column % SLOT
    table = (row >= 0) & (row < side) & (spot < side) & (pixel == row * side + spot)
    return table.astype(BF16)


def two_terms(value):
    first = value.astype(BF16)
    return first, (value - first.astype(F32)).astype(BF16)


def resize_kernel(starts, inputs, *refs):
    sources, base_ref, pos_ref, vectors = refs[:3], refs[3], refs[4], refs[5 : 5 + inputs]
    low_ref, high_ref, *resizes, sems, out_ref, small = refs[5 + inputs :]
    copies = [
        pltpu.make_async_copy(source, target, sems.at[i])
        for i, (source, target) in enumerate(zip(sources, resizes))
    ]
    for copy in copies:
        copy.start()
    share = base_ref.shape[1]
    base = jnp.concatenate([base_ref[c] for c in range(3)])
    for start, side, resize_ref, copy in zip(starts, SIDES, resizes, copies):
        copy.wait()
        size = up_to(3 * side * SLOT, 128)
        own = sum(outer_t(base, term) for term in two_terms(resize_ref[...])[::-1]).astype(BF16)
        if side == SLOT:
            for c in range(3):
                first = start + c * side * SLOT
                out_ref[:, first : first + side * SLOT] = own[c * share : (c + 1) * share]
        else:
            out_ref[:, start : start + size] = sum(
                dot(own[c * share : (c + 1) * share], slot_table(side, size, c)) for c in range(3)
            ).astype(BF16)
    spots, width = pos_ref.shape[1], out_ref.shape[1] - starts[3]
    rise = vectors[-1].shape[1] // share
    for i, ref in enumerate(vectors):
        rows = [ref[:, k * share : (k + 1) * share] for k in range(ref.shape[1] // share)]
        for k, row in enumerate(rows):
            small[i + k : i + k + 1, :] = row.astype(F32)
    count = len(vectors) - 1 + rise

    def shift(rows, by):
        row = lax.broadcasted_iota(jnp.int32, (rows, width), 0)
        column = lax.broadcasted_iota(jnp.int32, (rows, width), 1)
        return ((row + by == column) & (row < count + 64 * (by == 0))).astype(BF16)

    small[count:, :] = jnp.zeros((16 - count, share), F32)
    out_ref[:, starts[3] :] = (
        dot(pos_ref[...], shift(spots, 0)) + inner_t(small[...].astype(BF16), shift(16, spots))
    ).astype(BF16)
    low_ref[...] = out_ref[:, : low_ref.shape[1]]
    high_ref[...] = out_ref[:, low_ref.shape[1] :]


def resize_all(resizes, base_kernel, posemb, vectors, starts, columns):
    whole = pl.BlockSpec(memory_space=pltpu.VMEM)
    share = base_kernel.shape[1]
    half = jax.ShapeDtypeStruct((share, columns // 2), BF16)
    return pl.pallas_call(
        functools.partial(resize_kernel, starts, len(vectors)),
        out_shape=(half, half),
        in_specs=[pl.BlockSpec(memory_space=pl.ANY)] * 3 + [whole] * (2 + len(vectors)),
        out_specs=(whole, whole),
        scratch_shapes=[pltpu.VMEM(r.shape, F32) for r in resizes]
        + [
            pltpu.SemaphoreType.DMA((3,)),
            pltpu.VMEM((share, columns), BF16),
            pltpu.VMEM((16, share), F32),
        ],
        compiler_params=pltpu.CompilerParams(vmem_limit_bytes=60 * 2**20),
        cost_estimate=BRIEF,
    )(*resizes, base_kernel, posemb, *vectors)


def enter_kernel(embed_pieces, qkv_pieces, starts, bounds, spots, where_ref, *refs):
    patches, map_ref, refs = refs[:3], refs[3], refs[4:]
    embed_parts, refs = refs[: len(embed_pieces)], refs[len(embed_pieces) :]
    qkv_parts, refs = refs[: len(qkv_pieces)], refs[len(qkv_pieces) :]
    embedded, units, qkv, lines_ref, inverse_ref, small_ref = refs[:6]
    normed, table, weight, embed_sems, qkv_sems = refs[6:]
    width = embedded.shape[1]
    embed_copies = place_copies(embed_pieces, embed_parts, table, where_ref, embed_sems)
    qkv_copies = place_copies(qkv_pieces, qkv_parts, weight, where_ref, qkv_sems)
    for copy in embed_copies + qkv_copies:
        copy.start()
    for copy in embed_copies:
        copy.wait()
    smalls = table[:, bounds[3] :]
    small_ref[...] = smalls
    row = lax.broadcasted_iota(jnp.int32, (16, 128), 0)
    lane = lax.broadcasted_iota(jnp.int32, (16, 128), 1)
    lines = outer_t(((lane == row + spots) & (row < 9)).astype(BF16), smalls)
    lines_ref[...] = lines
    for i, patch_ref in enumerate(patches):
        rows = slice(starts[i], starts[i + 1])
        value = outer_t(patch_ref[...], table[:, bounds[i] : bounds[i + 1]])
        for part in reversed(terms(map_ref[rows, :])):
            value = value + outer_t(part, smalls)
        embedded[rows, :] = value
        unit_rows, inverse = unit(value)
        inverse_ref[rows, :] = inverse
        units[rows, :] = unit_rows.astype(BF16)
        normed[rows, :] = (unit_rows * lines[1:2] + lines[2:3]).astype(BF16)
    for copy in qkv_copies:
        copy.wait()
    for i in range(3):
        columns = slice(i * width, (i + 1) * width)
        value = dot(normed[...], weight[:, columns])
        if i != 1:
            value = value + lines[3 + i // 2 : 4 + i // 2]
        qkv[:, columns] = value.astype(BF16)


def enter_all(embed_parts, qkv_parts, patches, maps, starts, bounds, spots):
    whole = pl.BlockSpec(memory_space=pltpu.VMEM)
    anywhere = pl.BlockSpec(memory_space=pl.ANY)
    parts = [*embed_parts.parts, *qkv_parts.parts]
    rows, width = maps.shape[0], 16 * parts[0].shape[1]
    return pl.pallas_call(
        functools.partial(
            enter_kernel, embed_parts.pieces, qkv_parts.pieces, starts, bounds, spots
        ),
        out_shape=(
            jax.ShapeDtypeStruct((rows, width), F32),
            jax.ShapeDtypeStruct((rows, width), BF16),
            jax.ShapeDtypeStruct((rows, 3 * width), BF16),
            jax.ShapeDtypeStruct((16, width), F32),
            jax.ShapeDtypeStruct((rows, 1), F32),
            jax.ShapeDtypeStruct((width, embed_parts.columns - bounds[3]), BF16),
        ),
        in_specs=[pl.BlockSpec(memory_space=pltpu.SMEM)]
        + [whole] * 4
        + [pl.BlockSpec(memory_space=pltpu.HBM)] * len(parts),
        out_specs=[whole] * 6,
        scratch_shapes=[
            pltpu.VMEM((rows, width), BF16),
            pltpu.VMEM((width, embed_parts.columns), BF16),
            pltpu.VMEM((width, 3 * width), BF16),
            pltpu.SemaphoreType.DMA((copies_of(embed_parts.pieces),)),
            pltpu.SemaphoreType.DMA((copies_of(qkv_parts.pieces),)),
        ],
        compiler_params=pltpu.CompilerParams(vmem_limit_bytes=58 * 2**20),
        cost_estimate=BRIEF,
    )(embed_parts.where, *patches, maps, *parts)


def base_gradient_kernel(starts, *refs):
    resizes, sum_ref, out_ref = refs[:3], refs[3], refs[4]
    share = sum_ref.shape[0]
    total = None
    for start, side, resize_ref in zip(starts, SIDES, resizes):
        size = up_to(3 * side * SLOT, 128)
        given = sum_ref[:, start : start + size]
        if side == SLOT:
            own = [given[:, c * side * SLOT : (c + 1) * side * SLOT] for c in range(3)]
        else:
            own = [outer_t(given, slot_table(side, size, c)).astype(BF16) for c in range(3)]
        own = jnp.concatenate(own)
        for term in two_terms(resize_ref[...])[::-1]:
            value = dot(own, term)
            total = value if total is None else total + value
    for c in range(3):
        out_ref[c] = total[c * share : (c + 1) * share]


def base_gradient(resizes, embed_sum, shape, starts):
    whole = pl.BlockSpec(memory_space=pltpu.VMEM)
    return pl.pallas_call(
        functools.partial(base_gradient_kernel, starts),
        out_shape=jax.ShapeDtypeStruct(shape, F32),
        in_specs=[whole] * 4,
        out_specs=whole,
        compiler_params=pltpu.CompilerParams(vmem_limit_bytes=24 * 2**20),
        cost_estimate=BRIEF,
    )(*resizes, embed_sum)


def gelu_pair(value):
    slope = math.sqrt(2 / math.pi)
    square = value * value
    curve = jnp.tanh(value * (slope + (slope * 0.044715) * square))
    half = 0.5 * value
    rise = 0.5 + 0.5 * curve
    bend = (half - half * (curve * curve)) * (slope + (3 * slope * 0.044715) * square)
    return value * rise, rise + bend


ORDER = (0, 8, 4, 12, 2, 10, 6, 14)


def feed_kernel(starts, chunk, where_ref, *refs):
    mixed_ref, embedded_ref, lines_ref, b_up_ref = refs[:4]
    up_parts, down_parts, cotangents, refs = refs[4:12], refs[12:16], refs[16:19], refs[19:]
    finals = refs[:3]
    up_keep, up_give, down_keep, down_give, g_bias_ref = refs[3:8]
    branch_ref, g_mixed_ref, sums_ref = refs[8:11]
    middle, normed, grads, act, grad_up, total, back = refs[11:18]
    w_up, w_down, w_out, g_up, g_down, g_out = refs[18:24]
    up_in, down_in, out_in, up_out, down_out, out_out, one, ends = refs[24:]
    step, steps = pl.program_id(0), pl.num_programs(0)
    rows = middle.shape[0]
    me, other = where_ref[0], where_ref[1]
    slot = lax.rem(step, 2)
    tile = w_up.shape[2]
    up_rows, down_rows = up_keep.shape[2], w_down.shape[1] // 4
    out_columns = up_parts[0].shape[2] - 2 * tile
    count = 16

    def at(index, size):
        return pl.ds(pl.multiple_of(index * size, size), size)

    def load_up(s, half):
        t = lax.bitwise_xor(s, me // 4)
        return [
            pltpu.make_async_copy(
                up_parts[4 * (d % 2) + 2 * half + ORDER.index(d - d % 2) // 4].at[
                    ORDER.index(d - d % 2) % 4, :, at(lax.rem(t, 2), tile)
                ],
                w_up.at[lax.rem(s, 2), at(lax.bitwise_xor(me, d), up_rows), :],
                up_in.at[lax.rem(s, 2), d],
            )
            for d in range(count)
        ]

    def load_down(s):
        copies = []
        for j in range(4):
            place_ = s // 2 + 2 * lax.rem(s, 2)
            copies.append(
                pltpu.make_async_copy(
                    down_parts[2 * (j % 2) + j // 2].at[place_],
                    w_down.at[lax.rem(s, 2), at(lax.bitwise_xor(lax.rem(me, 4), j), down_rows), :],
                    down_in.at[lax.rem(s, 2), j],
                )
            )
        return copies

    def load(s):
        t = lax.bitwise_xor(s, me // 4)
        side = lax.bitwise_xor(t // 2, other)
        for half in range(2):

            @pl.when(side == half)
            def _():
                for copy in load_up(s, half):
                    copy.start()

        for copy in load_down(s):
            copy.start()

    def load_out():
        return [
            pltpu.make_async_copy(
                up_parts[4 * (d % 2) + 2 * half + ORDER.index(d - d % 2) // 4].at[
                    ORDER.index(d - d % 2) % 4, :, pl.ds(2 * tile, out_columns)
                ],
                w_out.at[
                    at(lax.bitwise_xor(me, d), up_rows), at(lax.bitwise_xor(other, half), out_columns)
                ],
                out_in.at[half, d],
            )
            for half in range(2)
            for d in range(count)
        ]

    def store(s):
        t = lax.bitwise_xor(s, me // 4)
        side = lax.bitwise_xor(t // 2, other)
        copies = []
        for d in range(count):
            copies.append(
                pltpu.make_async_copy(
                    g_up.at[lax.rem(s, 2), at(lax.bitwise_xor(me, d), up_rows), :],
                    (up_keep, up_give)[d % 2].at[side, d // 2, :, at(lax.rem(t, 2), tile)],
                    up_out.at[lax.rem(s, 2), d],
                )
            )
        for j in range(4):
            copies.append(
                pltpu.make_async_copy(
                    g_down.at[lax.rem(s, 2), at(lax.bitwise_xor(lax.rem(me, 4), j), down_rows), :],
                    (down_keep, down_give)[j % 2].at[2 * s + j // 2, pl.ds(0, down_rows), :],
                    down_out.at[lax.rem(s, 2), j],
                )
            )
        return copies

    def store_out():
        return [
            pltpu.make_async_copy(
                g_out.at[at(lax.bitwise_xor(me, d), up_rows), :],
                (down_keep, down_give)[d % 2].at[d // 2, pl.ds(down_rows, up_rows), :],
                out_out.at[d],
            )
            for d in range(count)
        ]

    @pl.when(step == 0)
    def _():
        copy = pltpu.make_async_copy(embedded_ref, middle, one.at[0])
        copy.start()
        for first in load_out():
            first.start()
        load(0)
        for i, ref in enumerate(cotangents):
            grads[starts[i] : starts[i + 1], :] = ref[0]
        copy.wait()
        for first in load_out():
            first.wait()
        for first, size in chunks(rows, 416):
            part = slice(first, first + size)
            value = middle[part, :] + dot(mixed_ref[part, :], w_out[...]) + lines_ref[5:6, :]
            middle[part, :] = value
            unit_rows, _ = unit(value)
            normed[part, :] = (unit_rows * lines_ref[6:7, :] + lines_ref[7:8, :]).astype(BF16)
            total[part, :] = value + lines_ref[8:9, :]
            back[part, :] = jnp.zeros((size, back.shape[1]), F32)

    @pl.when(step + 1 < steps)
    def _():
        load(step + 1)

    for copy in load_up(step, 0) + load_down(step):
        copy.wait()

    column = jnp.zeros((1, tile), F32)
    for first, size in chunks(rows, chunk):
        part = slice(first, first + size)
        up = dot(normed[part, :], w_up[slot]) + b_up_ref[...]
        value, slope = gelu_pair(up)
        value = value.astype(BF16)
        act[part, :] = value
        grad = (slope * outer_t(grads[part, :], w_down[slot])).astype(BF16)
        grad_up[part, :] = grad
        column += jnp.sum(grad.astype(F32), axis=0, keepdims=True)
        total[part, :] += dot(value, w_down[slot])
        back[part, :] += outer_t(grad, w_up[slot])
    g_bias_ref[...] = column

    @pl.when(step >= 2)
    def _():
        for copy in store(step - 2):
            copy.wait()

    g_down[slot] = inner_t(act[...], grads[...]).astype(BF16)
    g_up[slot] = inner_t(normed[...], grad_up[...]).astype(BF16)
    for copy in store(step):
        copy.start()

    @pl.when(step == steps - 1)
    def _():
        done = []

        def leave(source, target):
            done.append(pltpu.make_async_copy(source, target, ends.at[len(done)]))
            done[-1].start()

        for i, ref in enumerate(finals):
            part = pl.ds(starts[i], starts[i + 1] - starts[i])
            act[part, :] = total[part, :].astype(BF16)
            leave(act.at[part, :], ref.at[0])
        width = middle.shape[1]
        sums = [jnp.zeros((1, width), F32)] * 4
        for first, size in chunks(rows, 416):
            part = pl.ds(first, size)
            unit_rows, inverse = unit(middle[part, :])
            out = back[part, :]
            down = grads[part, :].astype(F32)
            grad, gain, bias = norm_backward(out, unit_rows, inverse, lines_ref[6:7, :])
            low = (grad + down).astype(BF16)
            normed[part, :] = low
            leave(normed.at[part, :], branch_ref.at[part, :])
            grad_up[part, :] = outer_t(low, w_out[...]).astype(BF16)
            leave(grad_up.at[part, :], g_mixed_ref.at[part, :])
            found = (
                gain[None],
                bias[None],
                jnp.sum(down, axis=0, keepdims=True),
                jnp.sum(low.astype(F32), axis=0, keepdims=True),
            )
            sums = [a + b for a, b in zip(sums, found)]
        g_out[...] = inner_t(mixed_ref[...], normed[...]).astype(BF16)
        for last in store_out():
            last.start()
        sums_ref[...] = jnp.concatenate(sums + [jnp.zeros((4, width), F32)])
        for last in store_out() + store(step - 1) + store(step) + done:
            last.wait()


def feed_all(where, mixed, embedded, lines, b_up, up_parts, down_parts, cotangents, starts, chunk=624):
    rows, width = mixed.shape
    tile = (up_parts[0].shape[2] - width // 2) // 2
    hidden = 4 * tile
    up_rows = up_parts[0].shape[1]
    down_rows = down_parts[0].shape[1]
    fixed = lambda *shape: pl.BlockSpec(
        shape, lambda s, w: (0,) * len(shape), pipeline_mode=pl.Buffered(1)
    )
    whole = lambda *shape: pl.BlockSpec(shape, lambda s, w: (0,) * len(shape))
    mine = pl.BlockSpec((1, tile), lambda s, w: (0, lax.bitwise_xor(s, w[0] // 4)))
    anywhere = pl.BlockSpec(memory_space=pl.ANY)
    like = lambda shape, kind: jax.ShapeDtypeStruct(shape, kind)
    return pl.pallas_call(
        functools.partial(feed_kernel, starts, chunk),
        grid_spec=pltpu.PrefetchScalarGridSpec(
            num_scalar_prefetch=1,
            grid=(4,),
            in_specs=[fixed(rows, width), anywhere, fixed(16, width), mine]
            + [pl.BlockSpec(memory_space=pltpu.HBM)] * 12
            + [fixed(*c.shape) for c in cotangents],
            out_specs=[anywhere] * 7 + [mine, anywhere, anywhere, whole(8, width)],
            scratch_shapes=[
                pltpu.VMEM((rows, width), F32),
                pltpu.VMEM((rows, width), BF16),
                pltpu.VMEM((rows, width), BF16),
                pltpu.VMEM((rows, tile), BF16),
                pltpu.VMEM((rows, tile), BF16),
                pltpu.VMEM((rows, width), F32),
                pltpu.VMEM((rows, width), F32),
                pltpu.VMEM((2, width, tile), BF16),
                pltpu.VMEM((2, tile, width), BF16),
                pltpu.VMEM((width, width), BF16),
                pltpu.VMEM((2, width, tile), BF16),
                pltpu.VMEM((2, tile, width), BF16),
                pltpu.VMEM((width, width), BF16),
                pltpu.SemaphoreType.DMA((2, 16)),
                pltpu.SemaphoreType.DMA((2, 4)),
                pltpu.SemaphoreType.DMA((2, 16)),
                pltpu.SemaphoreType.DMA((2, 16)),
                pltpu.SemaphoreType.DMA((2, 4)),
                pltpu.SemaphoreType.DMA((16,)),
                pltpu.SemaphoreType.DMA((1,)),
                pltpu.SemaphoreType.DMA((3 + 2 * len(chunks(rows, 416)),)),
            ],
        ),
        out_shape=[like(c.shape, BF16) for c in cotangents]
        + [like((2, 8, up_rows, hidden // 2), BF16)] * 2
        + [like((8, down_rows + up_rows, width), BF16)] * 2
        + [
            like((1, hidden), F32),
            like((rows, width), BF16),
            like((rows, width), BF16),
            like((8, width), F32),
        ],
        compiler_params=pltpu.CompilerParams(vmem_limit_bytes=56 * 2**20),
        cost_estimate=BRIEF,
    )(where, mixed, embedded, lines, b_up, *up_parts, *down_parts, *cotangents)


def spread_copies(source, segments, where_ref, sems, first=0):
    me, other = where_ref[0], where_ref[1]
    copies = []
    for start, columns, targets, half, there in segments:
        for d in range(16):
            rows = source.shape[0] // 16
            row = pl.ds(pl.multiple_of(lax.bitwise_xor(me, d) * rows, rows), rows)
            target = targets[d % 2]
            if half is not None:
                target = target.at[lax.bitwise_xor(other, half)]
            copies.append(
                pltpu.make_async_copy(
                    source.at[row, pl.ds(start, columns)],
                    target.at[d // 2, :, pl.ds(there, columns)],
                    sems.at[first + len(copies)],
                )
            )
    return copies


def leave_kernel(pieces, starts, bounds, spots, low_columns, chunk, where_ref, *refs):
    grads, units, branch, lines_ref, given_ref, bias_ref, inverse_ref, map_ref = refs[:8]
    patches, parts, refs = refs[8:11], refs[11 : 11 + len(pieces)], refs[11 + len(pieces) :]
    low_ref, low_outs, high_outs, refs = refs[0], refs[1:3], refs[3:5], refs[5:]
    normed, weight, embed_out, qkv_out, sums, weight_sems, out_sems = refs
    rows, width = low_ref.shape
    weights = place_copies(pieces, parts, weight, where_ref, weight_sems)
    half = embed_out.shape[1] // 2
    quarter = half // 2
    low = low_columns - half
    rest = (3 * width - low) // 2
    segments = [
        (qkv_out, (0, low, low_outs, None, half)),
        (qkv_out, (low, rest, high_outs, 0, quarter)),
        (qkv_out, (low + rest, rest, high_outs, 1, quarter)),
        (embed_out, (0, half, low_outs, None, 0)),
        (embed_out, (half, quarter, high_outs, 0, 0)),
        (embed_out, (half + quarter, quarter, high_outs, 1, 0)),
    ]
    copies = []
    for source, segment in segments:
        copies += spread_copies(source, [segment], where_ref, out_sems, len(copies))
    for copy in weights:
        copy.start()
    normed[...] = (units[...].astype(F32) * lines_ref[1:2, :] + lines_ref[2:3, :]).astype(BF16)
    for i in range(3):
        columns = slice(i * width, (i + 1) * width)
        qkv_out[:, columns] = inner_t(normed[...], grads[i]).astype(BF16)
        for copy in copies[16 * i - 16 : 16 * i] if i < 2 else copies[16:48]:
            copy.start()
    sums[...] = jnp.zeros_like(sums)
    sums[5:6, :] = given_ref[3:4, :]
    sums[6:9, :] = given_ref[:3, :]
    for copy in weights:
        copy.wait()
    totals = [jnp.zeros((1, width), F32)] * 4
    for first, size in chunks(rows, chunk):
        part = slice(first, first + size)
        found = sum(
            outer_t(grads[i, part, :], weight[:, i * width : (i + 1) * width]) for i in range(3)
        )
        grad, gain, bias = norm_backward(
            found, units[part, :].astype(F32), inverse_ref[part, :], lines_ref[1:2, :]
        )
        low_ref[part, :] = (grad + branch[part, :].astype(F32)).astype(BF16)
        found = [gain[None], bias[None]] + [
            jnp.sum(grads[i, part, :].astype(F32), axis=0, keepdims=True) for i in (0, 2)
        ]
        totals = [a + b for a, b in zip(totals, found)]
    for i, value in enumerate(totals):
        sums[i + 1 : i + 2, :] = value
    row = lax.broadcasted_iota(jnp.int32, (16, 128), 0)
    lane = lax.broadcasted_iota(jnp.int32, (16, 128), 1)
    smalls = inner_t(sums[...].astype(BF16), ((lane == row + spots) & (row < 9)).astype(BF16))
    rise = bias_ref.shape[1]
    smalls += dot(bias_ref[...], ((lane == row + spots + 9)[:rise]).astype(BF16))
    started = 48
    for i, patch_ref in enumerate(patches):
        part = slice(starts[i], starts[i + 1])
        size = bounds[i + 1] - bounds[i]
        above, below = two_terms(map_ref[part, :])
        found = inner_t(low_ref[part, :], jnp.concatenate([patch_ref[...], above, below], axis=1))
        embed_out[:, bounds[i] : bounds[i + 1]] = found[:, :size].astype(BF16)
        smalls += found[:, size : size + 128] + found[:, size + 128 :]
        if bounds[i + 1] >= half and started == 48:
            started = 64
            for copy in copies[48:64]:
                copy.start()
    embed_out[:, bounds[3] :] = smalls.astype(BF16)
    for copy in copies[started:]:
        copy.start()
    for copy in copies:
        copy.wait()


def leave_all(
    qkv_parts,
    grad_qkv,
    units,
    branch,
    lines,
    given,
    bias,
    inverse,
    maps,
    patches,
    starts,
    bounds,
    spots,
    low_columns,
    chunk=416,
):
    _, rows, width = grad_qkv.shape
    whole = pl.BlockSpec(memory_space=pltpu.VMEM)
    anywhere = pl.BlockSpec(memory_space=pl.ANY)
    parts = qkv_parts.parts
    columns = bounds[3] + 128
    block = width // 16
    high_columns = (3 * width + columns - low_columns) // 2
    return pl.pallas_call(
        functools.partial(
            leave_kernel, qkv_parts.pieces, starts, bounds, spots, low_columns, chunk
        ),
        out_shape=[jax.ShapeDtypeStruct((rows, width), BF16)]
        + [jax.ShapeDtypeStruct((8, block, low_columns), BF16)] * 2
        + [jax.ShapeDtypeStruct((2, 8, block, high_columns), BF16)] * 2,
        in_specs=[pl.BlockSpec(memory_space=pltpu.SMEM)]
        + [whole] * 11
        + [pl.BlockSpec(memory_space=pltpu.HBM)] * len(parts),
        out_specs=[whole] + [anywhere] * 4,
        scratch_shapes=[
            pltpu.VMEM((rows, width), BF16),
            pltpu.VMEM((width, 3 * width), BF16),
            pltpu.VMEM((width, columns), BF16),
            pltpu.VMEM((width, 3 * width), BF16),
            pltpu.VMEM((16, width), F32),
            pltpu.SemaphoreType.DMA((copies_of(qkv_parts.pieces),)),
            pltpu.SemaphoreType.DMA((96,)),
        ],
        compiler_params=pltpu.CompilerParams(vmem_limit_bytes=44 * 2**20),
        cost_estimate=BRIEF,
    )(
        qkv_parts.where,
        grad_qkv,
        units,
        branch,
        lines,
        given,
        bias,
        inverse,
        maps,
        *patches,
        *parts,
    )


def dot(first, second):
    return jnp.dot(first, second, preferred_element_type=F32)


def inner_t(first, second):
    return lax.dot_general(first, second, (((0,), (0,)), ((), ())), preferred_element_type=F32)


def body(count, pixels, resizes, posmaps, weights, cotangents):
    base_kernel, patch_bias, posemb = weights[:3]
    ln1_gain, ln1_bias, qkv_weight, qv_bias, out_weight, out_bias = weights[3:9]
    ln2_gain, ln2_bias, up_weight, up_bias, down_weight, down_bias = weights[9:]
    channels, base_pixels, share = base_kernel.shape
    width = share * count
    spots = posemb.shape[0]
    where = jnp.stack([lax.axis_index("fsdp"), lax.axis_index("rep")]).astype(jnp.int32)
    tokens = [c.shape[1] for c in cotangents]
    starts = [sum(tokens[:i]) for i in range(4)]
    bits = [2**i for i in range(1, count.bit_length() - 1)]
    inward = [(bit,) for bit in bits]
    outward = inward[::-1]
    turned = inward[:1] + outward[:-1]

    up_per = up_bias.shape[0] // share
    used = spots + 9 + up_per
    bounds = [0]
    for side in SIDES:
        bounds.append(bounds[-1] + up_to(3 * side * SLOT, 128))
    columns = bounds[3] + 128
    vectors = [
        v.reshape(1, -1)
        for v in (
            patch_bias,
            ln1_gain,
            ln1_bias,
            qv_bias[0],
            qv_bias[1],
            out_bias,
            ln2_gain,
            ln2_bias,
            down_bias,
            up_bias,
        )
    ]
    maps = jnp.concatenate(posmaps)
    maps = jnp.concatenate(
        [maps, jnp.ones((maps.shape[0], 1), F32), jnp.zeros((maps.shape[0], 127 - spots), F32)],
        axis=1,
    )

    base_turned = base_kernel.swapaxes(1, 2)
    down_rows = (down_weight.shape[0], out_weight.shape[0])
    up_half, out_half = up_weight.shape[1] // 2, width // 2
    up_block = jnp.concatenate(
        [
            up_weight[:, :up_half],
            out_weight[:, :out_half],
            up_weight[:, up_half:],
            out_weight[:, out_half:],
        ],
        axis=1,
    )
    qkv_shards = Gather(qkv_weight, where, count, outward, split=True).send()
    up_shards = Gather(up_block, where, count, outward, split=True, joined=False).send()
    shards = resize_all(resizes, base_turned, posemb.T, vectors, bounds, columns)
    embed_low = Gather(shards[0], where, count, outward).send()
    embed_high = Gather(shards[1], where, count, outward).send()
    held = go_on((pixels, maps, *shards), qkv_shards)
    held = together(held, embed_low, embed_high)
    held = go_on(held, qkv_shards)
    held = together(held, embed_low, embed_high)
    held, down_weight = after(held, down_weight)
    down_shards = Gather(down_weight, where, count, outward, joined=False).send()
    held = together(held, qkv_shards, up_shards)
    pixels, maps, *_ = held
    patches = patch_all(pixels)
    patches, maps = finish(
        (patches, maps), embed_low, embed_high, qkv_shards, down_shards, up_shards
    )
    for chain in (embed_low, embed_high, qkv_shards, down_shards):
        chain.send()
    patches, maps = complete((patches, maps), embed_low, embed_high, qkv_shards)
    up_shards.send()
    w_qkv = Parts([qkv_shards], where, count)
    w_embed = Parts([embed_low, embed_high], where, count)
    embedded, units, qkv, lines, inverse, columns_small = enter_all(
        w_embed, w_qkv, patches, maps, starts, bounds, spots
    )
    qkv = together(qkv, up_shards, down_shards)
    mixed, totals = attend_forward(qkv, starts)
    mixed = together(mixed, up_shards, down_shards)
    mixed = complete(mixed, up_shards, down_shards)
    w_up = Parts([up_shards], where, count)
    w_down = Parts([down_shards], where, count)
    b_up = columns_small[:, spots + 9 : used].astype(F32)
    b_up = b_up.reshape(count, share, up_per).swapaxes(1, 2).reshape(1, -1)
    (
        *results,
        up_keep,
        up_give,
        down_keep,
        down_give,
        grad_b_up,
        branch,
        grad_mixed,
        sums,
    ) = feed_all(
        w_up.where, mixed, embedded, lines, b_up, w_up.quarters(2), w_down.quarters(1), cotangents, starts
    )
    rows16 = (down_rows[0] * count // 16, down_rows[1] * count // 16)
    down_sums = Scatter(
        *ordered(down_keep, down_give, where, count, rows16), where, count, inward
    ).send()
    up_sums = Scatter(
        *ordered(up_keep, up_give, where, count, split=True), where, count, inward, split=True
    ).send()
    grad_qkv = attend_backward(qkv, mixed, totals, grad_mixed, starts[:2])
    grad_qkv = together(grad_qkv, down_sums, up_sums)
    grad_qkv = attend_backward(qkv, mixed, totals, grad_mixed, starts[1:], (grad_qkv,))
    bias_columns = grad_b_up.reshape(width, up_per).astype(BF16)
    grad_qkv, bias_columns = after(grad_qkv, bias_columns)
    grad_qkv = together(grad_qkv, down_sums, up_sums)
    half = columns // 2
    low_columns = half + 5 * width // 3
    grad_low, *shares = leave_all(
        w_qkv,
        grad_qkv,
        units,
        branch,
        lines,
        sums,
        bias_columns,
        inverse,
        maps,
        patches,
        starts,
        bounds,
        spots,
        low_columns,
    )
    grad_low, *arrived = after((grad_low, *shares), *down_sums.sent, *up_sums.sent)
    grad_low, *shares = grad_low
    low_sums = Scatter(*ordered(*shares[:2], where, count), where, count, inward).send()
    high_sums = Scatter(
        *ordered(*shares[2:], where, count, split=True), where, count, inward, split=True
    ).send()
    for chain in (down_sums, up_sums):
        chain.sent, arrived = arrived[: len(chain.sent)], arrived[len(chain.sent) :]
    grad_low = together(grad_low, down_sums, up_sums)
    grad_low = together(grad_low, low_sums)
    grad_low = together(grad_low, high_sums)
    pixel_grads = unpatch_all(grad_low, w_embed, starts, bounds, [p.shape[2] for p in pixels])
    pixel_grads = together(pixel_grads, down_sums, up_sums)
    pixel_grads = go_on(pixel_grads, high_sums, low_sums, high_sums, low_sums, high_sums)
    pixel_grads = go_on(pixel_grads, up_sums, low_sums)
    pixel_grads = complete(pixel_grads, down_sums, high_sums, up_sums, low_sums)

    low, high = low_sums.result, high_sums.result
    quarter = half // 2
    embed_sum = jnp.concatenate([low[:, :half]] + [h[:, :quarter] for h in high], axis=1)
    qkv_sum = jnp.concatenate([low[:, half:]] + [h[:, quarter:] for h in high], axis=1).astype(F32)
    down_sum = down_sums.result.astype(F32)
    up_sum = jnp.concatenate(up_sums.result, axis=1).astype(F32)
    base_grad = base_gradient(resizes, embed_sum, base_turned.shape, bounds).swapaxes(1, 2)
    small_sum = embed_sum[:, bounds[3] : bounds[3] + used].astype(F32)
    vectors = small_sum[:, spots : spots + 9].T
    return (
        *results,
        *pixel_grads,
        base_grad,
        vectors[0],
        small_sum[:, :spots].T,
        vectors[1],
        vectors[2],
        qkv_sum,
        vectors[3:5],
        down_sum[down_rows[0] :],
        vectors[5],
        vectors[6],
        vectors[7],
        up_sum,
        small_sum[:, spots + 9 :].reshape(-1),
        down_sum[: down_rows[0]],
        vectors[8],
    )


def solution(mesh):
    count = mesh.shape["fsdp"]

    def run(*args):
        return body(count, args[:3], args[3:6], args[6:9], args[9:24], args[24:])

    images = ("rep", "fsdp")
    weight_specs = (
        P(None, None, "fsdp"),
        P("fsdp"),
        P(None, "fsdp"),
        P("fsdp"),
        P("fsdp"),
        P("fsdp", None),
        P(None, "fsdp"),
        P("fsdp", None),
        P("fsdp"),
        P("fsdp"),
        P("fsdp"),
        P("fsdp", None),
        P("fsdp"),
        P("fsdp", None),
        P("fsdp"),
    )
    return jax.shard_map(
        run,
        mesh=mesh,
        in_specs=(P(images, None, None, None),) * 3
        + (P(),) * 6
        + weight_specs
        + (P(images, None, None),) * 3,
        out_specs=(P(images, None, None),) * 3
        + (P(images, None, None, None),) * 3
        + weight_specs,
        check_vma=False,
    )
```
